32 devices in a mesh: slab: 4 (over y, x), tile: 8 (over z, core).
Axes of the slice: x: 2, y: 2, z: 4, core: 2. Of those that a mesh axis runs over, the one named last changes fastest.
Arguments:
- volume: float32 [16, 256, 1024], P('slab', 'tile'), may hold values from -6 to 6
Outputs:
- histogram: float32 [1, 16, 32, 64], P(None, 'tile', None, 'slab')
The draws below stay inside these ranges and needn't reach their ends.
All inputs are finite; a program needn't handle non-finite values.
Results may differ from the reference program's by a relative error of at most 0.00005.
Values sent between devices are 32-bit elements; how exact they have to be, the bound alone decides.
A program may use at most 64 MiB of HBM per device.

```python
import jax
import jax.numpy as jnp
from jax import lax

RADIUS = 4
POOL = 16
DIRS = 32
NZ = 16
NX = 256
NY = 1024
VZ = 1
VX = 16
VY = 64


def shard_levels(stream_key, shape, pieces, low, top_value):
    gain = 1.0
    for position, shards_of in pieces:
        draws = jax.random.uniform(jax.random.fold_in(jax.random.fold_in(stream_key, 6), position), (shards_of,), jnp.float32, low / len(pieces), top_value / len(pieces))
        gain = gain * jnp.repeat(jnp.exp(draws), shape[position] // shards_of).reshape((-1,) + (1,) * (len(shape) - 1 - position))
    return gain


def gaussian(own_key, extent, scale, limit, cuts=(), held_as=jnp.bfloat16):
    level = shard_levels(own_key, extent, cuts, -0.22, 0.18) if cuts else 1.0
    drawn = jax.random.normal(own_key, extent, jnp.float32) * scale * level
    return jnp.minimum(jnp.maximum(drawn, -limit), limit).astype(held_as)


def setup_inputs(seed: int = 0) -> dict:
    streams_of = jax.random.split(jax.random.key(seed), 2)
    return {
        "volume": gaussian(streams_of[0], (NZ, NX, NY), 1.0, 6.0, ((0, 4), (1, 8)), jnp.float32),
    }


def kernel_taps():
    offsets = jnp.arange(-RADIUS, RADIUS + 1).astype(jnp.float32)
    base = jnp.exp(-offsets * offsets / 8.0)
    smooth = base / jnp.sqrt(jnp.sum(base * base))
    slope = -offsets * base
    deriv = slope / jnp.sqrt(jnp.sum(slope * slope))
    return (smooth, deriv)

def direction_table():
    index = jnp.arange(DIRS).astype(jnp.float32)
    height = 1.0 - (index + 0.5) / DIRS
    radial = jnp.sqrt(1.0 - height * height)
    phase = 2.399963229728653 * index
    d_z = height
    d_x = radial * jnp.cos(phase)
    d_y = radial * jnp.sin(phase)
    return jnp.stack([d_z * d_z, 2.0 * d_z * d_x, 2.0 * d_z * d_y, d_x * d_x, 2.0 * d_x * d_y, d_y * d_y], axis=1)

def filtered(padded, weights, axis, count):
    total = weights[0] * lax.slice_in_dim(padded, 0, count, axis=axis)
    for shift_index in range(1, 2 * RADIUS + 1):
        total = total + weights[shift_index] * lax.slice_in_dim(padded, shift_index, shift_index + count, axis=axis)
    return total

def padded_along(field, axis):
    widths = [(0, 0), (0, 0), (0, 0)]
    widths[axis] = (RADIUS, RADIUS)
    return jnp.pad(field, widths)

def pooled(field):
    return field.reshape(VZ, POOL, VX, POOL, VY, POOL).sum(axis=(1, 3, 5))

def reference(volume):
    smooth, deriv = kernel_taps()
    zpad = padded_along(volume, 0)
    z_smooth = filtered(zpad, smooth, 0, NZ)
    z_deriv = filtered(zpad, deriv, 0, NZ)
    xpad_smooth = padded_along(z_smooth, 1)
    xpad_deriv = padded_along(z_deriv, 1)
    both_smooth = filtered(xpad_smooth, smooth, 1, NX)
    smooth_deriv = filtered(xpad_smooth, deriv, 1, NX)
    deriv_smooth = filtered(xpad_deriv, smooth, 1, NX)
    grad_y = filtered(padded_along(both_smooth, 2), deriv, 2, NY)
    grad_x = filtered(padded_along(smooth_deriv, 2), smooth, 2, NY)
    grad_z = filtered(padded_along(deriv_smooth, 2), smooth, 2, NY)
    tensor = jnp.stack([pooled(grad_z * grad_z), pooled(grad_z * grad_x), pooled(grad_z * grad_y), pooled(grad_x * grad_x), pooled(grad_x * grad_y), pooled(grad_y * grad_y)])
    coeffs = direction_table()
    hist = jnp.einsum('kc,cabv->abkv', coeffs, tensor, precision=lax.Precision.HIGHEST)
    return hist / float(POOL ** 3)
```

```python
import functools

import jax
import jax.numpy as jnp
import ml_dtypes
import numpy as np
from jax import lax
from jax.experimental import pallas as pl
from jax.experimental.pallas import tpu as pltpu
from jax.sharding import PartitionSpec as P

RADIUS = 4
POOL = 16
DIRS = 32
MESH = pl.DeviceIdType.MESH
LANES = 128
EDGE = 2 * RADIUS


def extended(cells, sides, width):
    for axis, dim in sides:
        count = lax.axis_size(axis)
        ends = count - 1
        head = lax.slice_in_dim(cells, 0, width, axis=dim)
        tail = lax.slice_in_dim(cells, cells.shape[dim] - width, cells.shape[dim], axis=dim)
        cells = jnp.concatenate(
            [
                lax.ppermute(tail, axis, [(i, (i + 1) % count) for i in range(ends)]),
                cells,
                lax.ppermute(head, axis, [((i + 1) % count, i) for i in range(ends)]),
            ],
            axis=dim,
        )
    return cells


def kernel_taps():
    offsets = jnp.arange(-RADIUS, RADIUS + 1).astype(jnp.float32)
    base = jnp.exp(-offsets * offsets / 8.0)
    smooth = base / jnp.sqrt(jnp.sum(base * base))
    slope = -offsets * base
    deriv = slope / jnp.sqrt(jnp.sum(slope * slope))
    return (smooth, deriv)


def direction_table():
    index = jnp.arange(DIRS).astype(jnp.float32)
    height = 1.0 - (index + 0.5) / DIRS
    radial = jnp.sqrt(1.0 - height * height)
    phase = 2.399963229728653 * index
    d_x = radial * jnp.cos(phase)
    d_y = radial * jnp.sin(phase)
    return jnp.stack(
        [
            height * height,
            2.0 * height * d_x,
            2.0 * height * d_y,
            d_x * d_x,
            2.0 * d_x * d_y,
            d_y * d_y,
        ],
        axis=1,
    )


def filtered(padded, weights, axis, count):
    total = weights[0] * lax.slice_in_dim(padded, 0, count, axis=axis)
    for shift_index in range(1, 2 * RADIUS + 1):
        total = total + weights[shift_index] * lax.slice_in_dim(
            padded, shift_index, shift_index + count, axis=axis
        )
    return total


def pooled_full(field):
    planes, rows, cells = field.shape
    return field.reshape(planes // POOL, POOL, rows // POOL, POOL, cells // POOL, POOL).sum(
        axis=(1, 3, 5)
    )


def body(volume):
    smooth, deriv = kernel_taps()
    planes, rows, cells = volume.shape
    coeffs = direction_table()
    regrouped = lax.all_to_all(volume, "slab", split_axis=2, concat_axis=0, tiled=True)
    depth = regrouped.shape[0]
    owned = regrouped.shape[2]
    padded = extended(regrouped, (("slab", 2), ("tile", 1)), RADIUS)
    zpad = jnp.pad(padded, ((RADIUS, RADIUS), (0, 0), (0, 0)))
    z_smooth = filtered(zpad, smooth, 0, depth)
    z_deriv = filtered(zpad, deriv, 0, depth)
    both_smooth = filtered(z_smooth, smooth, 1, rows)
    smooth_deriv = filtered(z_smooth, deriv, 1, rows)
    deriv_smooth = filtered(z_deriv, smooth, 1, rows)
    grad_y = filtered(both_smooth, deriv, 2, owned)
    grad_x = filtered(smooth_deriv, smooth, 2, owned)
    grad_z = filtered(deriv_smooth, smooth, 2, owned)
    tensor = jnp.stack(
        [
            pooled_full(grad_z * grad_z),
            pooled_full(grad_z * grad_x),
            pooled_full(grad_z * grad_y),
            pooled_full(grad_x * grad_x),
            pooled_full(grad_x * grad_y),
            pooled_full(grad_y * grad_y),
        ]
    )
    hist = jnp.einsum("kc,cabv->abkv", coeffs, tensor, precision=lax.Precision.HIGHEST)
    return hist / float(POOL**3)


def host_taps():
    offsets = np.arange(-RADIUS, RADIUS + 1).astype(np.float64)
    base = np.exp(-offsets * offsets / 8.0)
    slope = -offsets * base
    return base / np.sqrt(np.sum(base * base)), slope / np.sqrt(np.sum(slope * slope))


def host_directions():
    index = np.arange(DIRS).astype(np.float32)
    height = np.float32(1.0) - (index + np.float32(0.5)) / np.float32(DIRS)
    radial = np.sqrt(np.float32(1.0) - height * height)
    phase = np.float32(2.399963229728653) * index
    d_x = radial * np.cos(phase)
    d_y = radial * np.sin(phase)
    two = np.float32(2.0)
    return np.stack(
        [height * height, two * height * d_x, two * height * d_y, d_x * d_x, two * d_x * d_y, d_y * d_y],
        axis=1,
    ).astype(np.float32)


def tap_at(weights, distance):
    index = distance + RADIUS
    inside = (index >= 0) & (index <= 2 * RADIUS)
    return np.where(inside, weights[np.clip(index, 0, 2 * RADIUS)], 0.0)


def halves(matrix):
    high = matrix.astype(np.float32).astype(ml_dtypes.bfloat16)
    low = (matrix - high.astype(np.float64)).astype(np.float32).astype(ml_dtypes.bfloat16)
    return np.stack([high, low])


def row_places(planes, rows):
    z, x = np.meshgrid(np.arange(planes), np.arange(rows), indexing="ij")
    parts = [(RADIUS, rows - RADIUS), (0, RADIUS), (rows - RADIUS, rows)]
    places = [(z[:, a:b].ravel(), x[:, a:b].ravel()) for a, b in parts]
    near, step = np.meshgrid(np.arange(planes), np.arange(RADIUS), indexing="ij")
    places.append((near.ravel(), step.ravel() - RADIUS))
    places.append((near.ravel(), step.ravel() + rows))
    return np.concatenate([p[0] for p in places]), np.concatenate([p[1] for p in places])


def y_weights(owned):
    smooth, deriv = host_taps()
    edge = np.concatenate([np.arange(-RADIUS, 0), owned + np.arange(RADIUS)])
    out = np.arange(owned)
    table = np.zeros((owned + LANES, 2 * owned))
    for column, weights in enumerate((smooth, deriv)):
        span = slice(column * owned, (column + 1) * owned)
        table[:owned, span] = tap_at(weights, out[:, None] - out[None, :])
        for copy in range(3):
            start = owned + copy * EDGE
            table[start : start + EDGE, span] = tap_at(weights, edge[:, None] - out[None, :])
    return halves(table)


def zx_weights(planes, rows):
    smooth, deriv = host_taps()
    z_in, x_in = row_places(planes, rows)
    z_out, x_out = (g.ravel() for g in np.meshgrid(np.arange(planes), np.arange(rows), indexing="ij"))
    fields = []
    for z_taps, x_taps in ((deriv, smooth), (smooth, deriv), (smooth, smooth)):
        blocks = []
        for group in (-1, 0, 1):
            along_z = tap_at(z_taps, group * planes + z_in[None, :] - z_out[:, None])
            blocks.append(along_z * tap_at(x_taps, x_in[None, :] - x_out[:, None]))
        fields.append(np.concatenate(blocks, axis=1))
    return halves(np.concatenate(fields, axis=0))


def histogram_weights(rows):
    voxels = rows // POOL
    inside = (np.arange(rows)[None, :] // POOL == np.arange(voxels)[:, None]).astype(np.float32)
    table = host_directions()[None, :, :, None] * inside[:, None, None, :]
    return (table.reshape(voxels * DIRS, -1) / np.float32(POOL**3)).astype(np.float32)


def split(values):
    high = values.astype(jnp.bfloat16)
    low = (values - high.astype(jnp.float32)).astype(jnp.bfloat16)
    return high, low


def dot(a, b):
    return jnp.dot(a, b, preferred_element_type=jnp.float32)


def exact_dot(a, b):
    return jnp.dot(a, b, preferred_element_type=jnp.float32, precision=lax.Precision.HIGHEST)


def kernel(
    slabs, tiles, x_hbm, wy_hbm, wzx_hbm, whist_ref, out_ref,
    x_ref, wy_ref, wzx_ref, stage, recv, halo_l, halo_r, y_high, y_low,
    load_sem, send_sem, recv_sem, fl_send, fl_recv, fr_send, fr_recv,
):
    planes, rows, cells = x_ref.shape
    owned = cells // slabs
    band = planes * RADIUS
    body_rows = planes * rows
    mid = body_rows - 2 * band
    e_at = mid + band
    total = body_rows + 2 * band
    s = lax.axis_index("slab")
    t = lax.axis_index("tile")
    has_left = t > 0
    has_right = t < tiles - 1

    loads = [
        pltpu.make_async_copy(src, dst, load_sem.at[i])
        for i, (src, dst) in enumerate(((x_hbm, x_ref), (wy_hbm, wy_ref), (wzx_hbm, wzx_ref)))
    ]
    for load in loads:
        load.start()

    barrier = pltpu.get_barrier_semaphore()
    for k in range(1, slabs):
        pl.semaphore_signal(barrier, inc=1, device_id=(lax.rem(s + k, slabs), t), device_id_type=MESH)

    @pl.when(has_left)
    def _():
        pl.semaphore_signal(barrier, inc=1, device_id=(s, t - 1), device_id_type=MESH)

    @pl.when(has_right)
    def _():
        pl.semaphore_signal(barrier, inc=1, device_id=(s, t + 1), device_id_type=MESH)

    loads[0].wait()
    for d in range(slabs):
        span = slice(d * owned, (d + 1) * owned)
        for z in range(planes):
            inner = rows - 2 * RADIUS
            stage[d, z * inner : (z + 1) * inner, :] = x_ref[z, RADIUS : rows - RADIUS, span]
        top = [x_ref[z, 0:RADIUS, span] for z in range(planes)]
        bottom = [x_ref[z, rows - RADIUS : rows, span] for z in range(planes)]
        stage[d, mid : mid + band, :] = jnp.concatenate(top, axis=0)
        stage[d, e_at + EDGE : e_at + EDGE + band, :] = jnp.concatenate(bottom, axis=0)

    lane = lax.broadcasted_iota(jnp.int32, (body_rows, LANES), 1)
    nothing = jnp.zeros((body_rows, LANES), jnp.float32)

    def side(d, lanes):
        if d < 0 or d >= slabs:
            return nothing
        return jnp.concatenate(
            [stage[d, 0:e_at, lanes], stage[d, e_at + EDGE : e_at + EDGE + band, lanes]], axis=0
        )

    edges = nothing
    for d in range(slabs):
        before = side(d - 1, slice(owned - LANES, owned))
        after = side(d + 1, slice(0, LANES))
        both = jnp.where(lane >= LANES // 2, before, after)
        turned = pltpu.roll(both, d * EDGE + RADIUS, 1)
        edges = jnp.where(lane // EDGE == d, turned, edges)
    edges = edges.T
    for d in range(slabs):
        stage[d, e_at : e_at + EDGE, 0:LANES] = edges[d * EDGE : (d + 1) * EDGE]
        stage[d, e_at : e_at + EDGE, LANES:] = jnp.zeros((EDGE, owned - LANES), jnp.float32)

    beside = jnp.where(has_left, 1, 0) + jnp.where(has_right, 1, 0)
    pl.semaphore_wait(barrier, slabs - 1 + beside)

    def to_peer(k):
        peer = lax.rem(s + k, slabs)
        return pltpu.make_async_remote_copy(
            src_ref=stage.at[peer], dst_ref=recv.at[s],
            send_sem=send_sem.at[k], recv_sem=recv_sem.at[s],
            device_id=(peer, t), device_id_type=MESH,
        )

    def from_peer(p):
        return pltpu.make_async_remote_copy(
            src_ref=stage.at[p], dst_ref=recv.at[p],
            send_sem=send_sem.at[0], recv_sem=recv_sem.at[p],
            device_id=(p, t), device_id_type=MESH,
        )

    def to_left(p):
        return pltpu.make_async_remote_copy(
            src_ref=recv.at[p, pl.ds(mid, band + EDGE)], dst_ref=halo_r.at[p],
            send_sem=fl_send.at[p], recv_sem=fl_recv.at[p],
            device_id=(s, t - 1), device_id_type=MESH,
        )

    def to_right(p):
        return pltpu.make_async_remote_copy(
            src_ref=recv.at[p, pl.ds(e_at, band + EDGE)], dst_ref=halo_l.at[p],
            send_sem=fr_send.at[p], recv_sem=fr_recv.at[p],
            device_id=(s, t + 1), device_id_type=MESH,
        )

    sends = [to_peer(k) for k in range(1, slabs)]
    for send in sends:
        send.start()

    def forward(p):
        @pl.when(has_left)
        def _():
            to_left(p).start()

        @pl.when(has_right)
        def _():
            to_right(p).start()

    recv[s] = stage[s]
    forward(s)

    @pl.when(jnp.logical_not(has_left))
    def _():
        halo_l[...] = jnp.zeros_like(halo_l)

    @pl.when(jnp.logical_not(has_right))
    def _():
        halo_r[...] = jnp.zeros_like(halo_r)

    for ref in (y_high, y_low):
        ref[0:total, :] = jnp.zeros((total, 2 * owned), jnp.bfloat16)
        ref[(slabs + 1) * total : (slabs + 2) * total, :] = jnp.zeros((total, 2 * owned), jnp.bfloat16)

    lane = lax.broadcasted_iota(jnp.int32, (total, LANES), 1)
    row = lax.broadcasted_iota(jnp.int32, (total, LANES), 0)
    owner = jnp.where(row < body_rows, 0, jnp.where(row < body_rows + band, 1, 2))
    own_edge = lane // EDGE == owner

    def along_y(p):
        @pl.when(has_left)
        def _():
            to_right(p).wait_recv()

        @pl.when(has_right)
        def _():
            to_left(p).wait_recv()

        block = jnp.concatenate(
            [
                recv[p, 0:e_at, :],
                recv[p, e_at + EDGE : e_at + EDGE + band, :],
                halo_l[p, EDGE : EDGE + band, :],
                halo_r[p, 0:band, :],
            ],
            axis=0,
        )
        ends = jnp.concatenate(
            [
                recv[p, e_at : e_at + EDGE, 0:LANES],
                halo_l[p, 0:EDGE, 0:LANES],
                halo_r[p, band : band + EDGE, 0:LANES],
                jnp.zeros((LANES - 3 * EDGE, LANES), jnp.float32),
            ],
            axis=0,
        ).T
        ends = jnp.concatenate([ends, ends[e_at : e_at + band], ends[mid : mid + band]], axis=0)
        ends = jnp.where(own_edge, ends, 0.0)
        high, low = split(jnp.concatenate([block, ends], axis=1))
        result = dot(high, wy_ref[0]) + dot(low, wy_ref[0]) + dot(high, wy_ref[1])
        high, low = split(result)
        at = pl.ds(pl.multiple_of((p + 1) * total, 16), total)
        y_high[at, :] = high
        y_low[at, :] = low

    loads[1].wait()
    loads[2].wait()
    for k in range(1, slabs):
        p = lax.rem(s + slabs - k, slabs)
        from_peer(p).wait_recv()
        forward(p)
        along_y(lax.rem(p + 1, slabs))
    along_y(lax.rem(s + 1, slabs))

    sums = [jnp.zeros((rows, owned), jnp.float32) for _ in range(6)]

    def group(g, sums):
        at = pl.ds(pl.multiple_of(g * total, 16), 3 * total)
        smooth_y = slice(0, owned)
        deriv_y = slice(owned, 2 * owned)
        two = slice(0, 2 * body_rows)
        one = slice(2 * body_rows, 3 * body_rows)

        def gradient(out, field):
            high = y_high[at, field]
            low = y_low[at, field]
            return dot(wzx_ref[0, out, :], high) + dot(wzx_ref[0, out, :], low) + dot(wzx_ref[1, out, :], high)

        pair = gradient(two, smooth_y)
        grad_z = pair[:body_rows]
        grad_x = pair[body_rows:]
        grad_y = gradient(one, deriv_y)
        products = (
            grad_z * grad_z, grad_z * grad_x, grad_z * grad_y,
            grad_x * grad_x, grad_x * grad_y, grad_y * grad_y,
        )
        return tuple(
            held + product.reshape(planes, rows, owned).sum(axis=0)
            for held, product in zip(sums, products)
        )

    sums = lax.fori_loop(0, slabs, group, tuple(sums))
    mixed = exact_dot(whist_ref[...], jnp.concatenate(sums, axis=0))
    cell = lax.broadcasted_iota(jnp.int32, (owned, owned // POOL), 0)
    voxel = lax.broadcasted_iota(jnp.int32, (owned, owned // POOL), 1)
    pooled = exact_dot(mixed, (cell // POOL == voxel).astype(jnp.float32))
    for b in range(rows // POOL):
        out_ref[0, b] = pooled[b * DIRS : (b + 1) * DIRS]

    for send in sends:
        send.wait_send()
    for p in range(slabs):
        @pl.when(has_left)
        def _():
            to_left(p).wait_send()

        @pl.when(has_right)
        def _():
            to_right(p).wait_send()


def fused(slabs, tiles, volume):
    planes, rows, cells = volume.shape
    owned = cells // slabs
    band = planes * RADIUS
    body_rows = planes * rows
    total = body_rows + 2 * band
    wy = y_weights(owned)
    wzx = zx_weights(planes, rows)
    whist = histogram_weights(rows)
    f32, bf16 = jnp.float32, jnp.bfloat16
    dma = pltpu.SemaphoreType.DMA((slabs,))
    halo = pltpu.VMEM((slabs, band + EDGE, owned), f32)
    whole = pltpu.VMEM((slabs, body_rows + EDGE, owned), f32)
    held = pltpu.VMEM(((slabs + 2) * total, 2 * owned), bf16)
    return pl.pallas_call(
        functools.partial(kernel, slabs, tiles),
        out_shape=jax.ShapeDtypeStruct((1, rows // POOL, DIRS, owned // POOL), f32),
        in_specs=[pl.BlockSpec(memory_space=pl.ANY)] * 3 + [pl.BlockSpec(memory_space=pltpu.VMEM)],
        out_specs=pl.BlockSpec(memory_space=pltpu.VMEM),
        scratch_shapes=[
            pltpu.VMEM(volume.shape, f32),
            pltpu.VMEM(wy.shape, bf16),
            pltpu.VMEM(wzx.shape, bf16),
            whole, whole, halo, halo, held, held,
            pltpu.SemaphoreType.DMA((3,)),
            dma, dma, dma, dma, dma, dma,
        ],
        compiler_params=pltpu.CompilerParams(
            collective_id=0, has_side_effects=True, vmem_limit_bytes=40 * 1024 * 1024
        ),
    )(volume, jnp.asarray(wy), jnp.asarray(wzx), jnp.asarray(whist))


def fits(slabs, tiles, planes, rows, cells):
    owned = cells // slabs
    return (
        slabs * planes == POOL and planes >= RADIUS and planes * rows == LANES
        and rows % POOL == 0 and rows >= 4 * RADIUS and (planes * RADIUS) % 16 == 0
        and owned % LANES == 0 and slabs * EDGE <= LANES
    )


def solution(mesh):
    slabs, tiles = mesh.shape["slab"], mesh.shape["tile"]

    def whole(volume):
        if slabs > 1 and tiles > 1 and fits(slabs, tiles, *volume.shape):
            return fused(slabs, tiles, volume)
        return body(volume)

    return jax.shard_map(
        whole,
        mesh=mesh,
        in_specs=(P("slab", "tile", None),),
        out_specs=P(None, "tile", None, "slab"),
        check_vma=False,
    )
```

```python
import functools

import jax
import jax.numpy as jnp
import ml_dtypes
import numpy as np
from jax import lax
from jax.experimental import pallas as pl
from jax.experimental.pallas import tpu as pltpu
from jax.sharding import PartitionSpec as P

RADIUS = 4
POOL = 16
DIRS = 32
MESH = pl.DeviceIdType.MESH
LANES = 128
EDGE = 2 * RADIUS
END_PART = 4 * EDGE


def extended(cells, sides, width):
    for axis, dim in sides:
        count = lax.axis_size(axis)
        ends = count - 1
        head = lax.slice_in_dim(cells, 0, width, axis=dim)
        tail = lax.slice_in_dim(cells, cells.shape[dim] - width, cells.shape[dim], axis=dim)
        cells = jnp.concatenate(
            [
                lax.ppermute(tail, axis, [(i, (i + 1) % count) for i in range(ends)]),
                cells,
                lax.ppermute(head, axis, [((i + 1) % count, i) for i in range(ends)]),
            ],
            axis=dim,
        )
    return cells


def kernel_taps():
    offsets = jnp.arange(-RADIUS, RADIUS + 1).astype(jnp.float32)
    base = jnp.exp(-offsets * offsets / 8.0)
    smooth = base / jnp.sqrt(jnp.sum(base * base))
    slope = -offsets * base
    deriv = slope / jnp.sqrt(jnp.sum(slope * slope))
    return (smooth, deriv)


def direction_table():
    index = jnp.arange(DIRS).astype(jnp.float32)
    height = 1.0 - (index + 0.5) / DIRS
    radial = jnp.sqrt(1.0 - height * height)
    phase = 2.399963229728653 * index
    d_x = radial * jnp.cos(phase)
    d_y = radial * jnp.sin(phase)
    return jnp.stack(
        [
            height * height,
            2.0 * height * d_x,
            2.0 * height * d_y,
            d_x * d_x,
            2.0 * d_x * d_y,
            d_y * d_y,
        ],
        axis=1,
    )


def filtered(padded, weights, axis, count):
    total = weights[0] * lax.slice_in_dim(padded, 0, count, axis=axis)
    for shift_index in range(1, 2 * RADIUS + 1):
        total = total + weights[shift_index] * lax.slice_in_dim(
            padded, shift_index, shift_index + count, axis=axis
        )
    return total


def pooled_full(field):
    planes, rows, cells = field.shape
    return field.reshape(planes // POOL, POOL, rows // POOL, POOL, cells // POOL, POOL).sum(
        axis=(1, 3, 5)
    )


def body(volume):
    smooth, deriv = kernel_taps()
    planes, rows, cells = volume.shape
    coeffs = direction_table()
    regrouped = lax.all_to_all(volume, "slab", split_axis=2, concat_axis=0, tiled=True)
    depth = regrouped.shape[0]
    owned = regrouped.shape[2]
    padded = extended(regrouped, (("slab", 2), ("tile", 1)), RADIUS)
    zpad = jnp.pad(padded, ((RADIUS, RADIUS), (0, 0), (0, 0)))
    z_smooth = filtered(zpad, smooth, 0, depth)
    z_deriv = filtered(zpad, deriv, 0, depth)
    both_smooth = filtered(z_smooth, smooth, 1, rows)
    smooth_deriv = filtered(z_smooth, deriv, 1, rows)
    deriv_smooth = filtered(z_deriv, smooth, 1, rows)
    grad_y = filtered(both_smooth, deriv, 2, owned)
    grad_x = filtered(smooth_deriv, smooth, 2, owned)
    grad_z = filtered(deriv_smooth, smooth, 2, owned)
    tensor = jnp.stack(
        [
            pooled_full(grad_z * grad_z),
            pooled_full(grad_z * grad_x),
            pooled_full(grad_z * grad_y),
            pooled_full(grad_x * grad_x),
            pooled_full(grad_x * grad_y),
            pooled_full(grad_y * grad_y),
        ]
    )
    hist = jnp.einsum("kc,cabv->abkv", coeffs, tensor, precision=lax.Precision.HIGHEST)
    return hist / float(POOL**3)


def host_taps():
    offsets = np.arange(-RADIUS, RADIUS + 1).astype(np.float64)
    base = np.exp(-offsets * offsets / 8.0)
    slope = -offsets * base
    return base / np.sqrt(np.sum(base * base)), slope / np.sqrt(np.sum(slope * slope))


def host_directions():
    index = np.arange(DIRS).astype(np.float32)
    height = np.float32(1.0) - (index + np.float32(0.5)) / np.float32(DIRS)
    radial = np.sqrt(np.float32(1.0) - height * height)
    phase = np.float32(2.399963229728653) * index
    d_x = radial * np.cos(phase)
    d_y = radial * np.sin(phase)
    two = np.float32(2.0)
    return np.stack(
        [height * height, two * height * d_x, two * height * d_y, d_x * d_x, two * d_x * d_y, d_y * d_y],
        axis=1,
    ).astype(np.float32)


def tap_at(weights, distance):
    index = distance + RADIUS
    inside = (index >= 0) & (index <= 2 * RADIUS)
    return np.where(inside, weights[np.clip(index, 0, 2 * RADIUS)], 0.0)


def halves(matrix):
    high = matrix.astype(np.float32).astype(ml_dtypes.bfloat16)
    low = (matrix - high.astype(np.float64)).astype(np.float32).astype(ml_dtypes.bfloat16)
    return np.stack([high, low])


def row_places(planes, rows):
    z, x = np.meshgrid(np.arange(planes), np.arange(rows), indexing="ij")
    parts = [(RADIUS, rows - RADIUS), (0, RADIUS), (rows - RADIUS, rows)]
    places = [(z[:, a:b].ravel(), x[:, a:b].ravel()) for a, b in parts]
    near, step = np.meshgrid(np.arange(planes), np.arange(RADIUS), indexing="ij")
    places.append((near.ravel(), step.ravel() - RADIUS))
    places.append((near.ravel(), step.ravel() + rows))
    return np.concatenate([p[0] for p in places]), np.concatenate([p[1] for p in places])


def y_weights(owned):
    smooth, deriv = host_taps()
    edge = np.concatenate([np.arange(-RADIUS, 0), owned + np.arange(RADIUS)])
    out = np.arange(owned)
    inner = halves(np.concatenate([tap_at(w, out[:, None] - out[None, :]) for w in (smooth, deriv)], axis=1))
    outer = halves(np.concatenate([tap_at(w, edge[:, None] - out[None, :]) for w in (smooth, deriv)], axis=1))
    ends = np.zeros((LANES, 2 * owned), ml_dtypes.bfloat16)
    for part, which in enumerate((0, 0, 1)):
        for copy in range(3):
            start = part * END_PART + copy * EDGE
            ends[start : start + EDGE] = outer[which]
    return np.concatenate([inner[0], inner[1], ends], axis=0)


def zx_weights(planes, rows):
    smooth, deriv = host_taps()
    z_in, x_in = row_places(planes, rows)
    z_out, x_out = (g.ravel() for g in np.meshgrid(np.arange(planes), np.arange(rows), indexing="ij"))
    fields = []
    for z_taps, x_taps in ((deriv, smooth), (smooth, deriv), (smooth, smooth)):
        blocks = []
        for group in (-1, 0, 1):
            along_z = tap_at(z_taps, group * planes + z_in[None, :] - z_out[:, None])
            blocks.append(along_z * tap_at(x_taps, x_in[None, :] - x_out[:, None]))
        fields.append(np.concatenate(blocks, axis=1))
    return halves(np.concatenate(fields, axis=0))


def histogram_weights(rows):
    voxels = rows // POOL
    inside = (np.arange(rows)[None, :] // POOL == np.arange(voxels)[:, None]).astype(np.float32)
    table = host_directions()[None, :, :, None] * inside[:, None, None, :]
    return (table.reshape(voxels * DIRS, -1) / np.float32(POOL**3)).astype(np.float32)


def split(values):
    high = values.astype(jnp.bfloat16)
    low = (values - high.astype(jnp.float32)).astype(jnp.bfloat16)
    return high, low


def dot(a, b):
    return jnp.dot(a, b, preferred_element_type=jnp.float32)


def exact_dot(a, b):
    return jnp.dot(a, b, preferred_element_type=jnp.float32, precision=lax.Precision.HIGHEST)


def kernel(
    slabs, tiles, x_hbm, wy_hbm, wzx_hbm, whist_hbm, out_ref,
    x_ref, wy_ref, wzx_ref, whist_ref, stage, recv, halo_l, halo_r, y_high, y_low,
    load_sem, send_sem, recv_sem, fl_send, fl_recv, fr_send, fr_recv,
):
    planes, rows, cells = x_ref.shape
    owned = cells // slabs
    band = planes * RADIUS
    body_rows = planes * rows
    mid = body_rows - 2 * band
    e_at = mid + band
    total = body_rows + 2 * band
    s = lax.axis_index("slab")
    t = lax.axis_index("tile")
    has_left = t > 0
    has_right = t < tiles - 1

    loads = [
        pltpu.make_async_copy(src, dst, load_sem.at[i])
        for i, (src, dst) in enumerate(((x_hbm, x_ref), (wy_hbm, wy_ref), (wzx_hbm, wzx_ref), (whist_hbm, whist_ref)))
    ]
    for load in loads:
        load.start()

    barrier = pltpu.get_barrier_semaphore()
    for k in range(1, slabs):
        pl.semaphore_signal(barrier, inc=1, device_id=(lax.rem(s + k, slabs), t), device_id_type=MESH)

    @pl.when(has_left)
    def _():
        pl.semaphore_signal(barrier, inc=1, device_id=(s, t - 1), device_id_type=MESH)

    @pl.when(has_right)
    def _():
        pl.semaphore_signal(barrier, inc=1, device_id=(s, t + 1), device_id_type=MESH)

    loads[0].wait()
    for d in range(slabs):
        span = slice(d * owned, (d + 1) * owned)
        for z in range(planes):
            inner = rows - 2 * RADIUS
            stage[d, z * inner : (z + 1) * inner, :] = x_ref[z, RADIUS : rows - RADIUS, span]
        top = [x_ref[z, 0:RADIUS, span] for z in range(planes)]
        bottom = [x_ref[z, rows - RADIUS : rows, span] for z in range(planes)]
        stage[d, mid : mid + band, :] = jnp.concatenate(top, axis=0)
        stage[d, e_at + EDGE : e_at + EDGE + band, :] = jnp.concatenate(bottom, axis=0)

    lane = lax.broadcasted_iota(jnp.int32, (body_rows, LANES), 1)
    nothing = jnp.zeros((body_rows, LANES), jnp.float32)

    def side(d, lanes):
        if d < 0 or d >= slabs:
            return nothing
        return jnp.concatenate(
            [stage[d, 0:e_at, lanes], stage[d, e_at + EDGE : e_at + EDGE + band, lanes]], axis=0
        )

    edges = nothing
    for d in range(slabs):
        before = side(d - 1, slice(owned - LANES, owned))
        after = side(d + 1, slice(0, LANES))
        both = jnp.where(lane >= LANES // 2, before, after)
        turned = pltpu.roll(both, d * EDGE + RADIUS, 1)
        edges = jnp.where(lane // EDGE == d, turned, edges)
    edges = edges.T
    for d in range(slabs):
        stage[d, e_at : e_at + EDGE, 0:LANES] = edges[d * EDGE : (d + 1) * EDGE]
        stage[d, e_at : e_at + EDGE, LANES:] = jnp.zeros((EDGE, owned - LANES), jnp.float32)

    beside = jnp.where(has_left, 1, 0) + jnp.where(has_right, 1, 0)
    pl.semaphore_wait(barrier, slabs - 1 + beside)

    def to_peer(k):
        peer = lax.rem(s + k, slabs)
        return pltpu.make_async_remote_copy(
            src_ref=stage.at[peer], dst_ref=recv.at[s],
            send_sem=send_sem.at[k], recv_sem=recv_sem.at[s],
            device_id=(peer, t), device_id_type=MESH,
        )

    def from_peer(p):
        return pltpu.make_async_remote_copy(
            src_ref=stage.at[p], dst_ref=recv.at[p],
            send_sem=send_sem.at[0], recv_sem=recv_sem.at[p],
            device_id=(p, t), device_id_type=MESH,
        )

    def to_left(p):
        return pltpu.make_async_remote_copy(
            src_ref=recv.at[p, pl.ds(mid, band + EDGE)], dst_ref=halo_r.at[p],
            send_sem=fl_send.at[p], recv_sem=fl_recv.at[p],
            device_id=(s, t - 1), device_id_type=MESH,
        )

    def to_right(p):
        return pltpu.make_async_remote_copy(
            src_ref=recv.at[p, pl.ds(e_at, band + EDGE)], dst_ref=halo_l.at[p],
            send_sem=fr_send.at[p], recv_sem=fr_recv.at[p],
            device_id=(s, t + 1), device_id_type=MESH,
        )

    sends = [to_peer(k) for k in range(1, slabs)]
    for send in sends:
        send.start()

    def forward(p):
        @pl.when(has_left)
        def _():
            to_left(p).start()

        @pl.when(has_right)
        def _():
            to_right(p).start()

    recv[s] = stage[s]
    forward(s)

    @pl.when(jnp.logical_not(has_left))
    def _():
        halo_l[...] = jnp.zeros_like(halo_l)

    @pl.when(jnp.logical_not(has_right))
    def _():
        halo_r[...] = jnp.zeros_like(halo_r)

    for ref in (y_high, y_low):
        ref[0:total, :] = jnp.zeros((total, 2 * owned), jnp.bfloat16)
        ref[(slabs + 1) * total : (slabs + 2) * total, :] = jnp.zeros((total, 2 * owned), jnp.bfloat16)

    lane = lax.broadcasted_iota(jnp.int32, (total, LANES), 1)
    row = lax.broadcasted_iota(jnp.int32, (total, LANES), 0)
    owner = jnp.where(row < body_rows, 0, jnp.where(row < body_rows + band, 1, 2))
    own_edge = lane // EDGE == owner

    def along_y(p):
        @pl.when(has_left)
        def _():
            to_right(p).wait_recv()

        @pl.when(has_right)
        def _():
            to_left(p).wait_recv()

        block = jnp.concatenate(
            [
                recv[p, 0:e_at, :],
                recv[p, e_at + EDGE : e_at + EDGE + band, :],
                halo_l[p, EDGE : EDGE + band, :],
                halo_r[p, 0:band, :],
            ],
            axis=0,
        )
        ends = jnp.concatenate(
            [
                recv[p, e_at : e_at + EDGE, 0:LANES],
                halo_l[p, 0:EDGE, 0:LANES],
                halo_r[p, band : band + EDGE, 0:LANES],
                jnp.zeros((LANES - 3 * EDGE, LANES), jnp.float32),
            ],
            axis=0,
        ).T
        ends = jnp.concatenate([ends, ends[e_at : e_at + band], ends[mid : mid + band]], axis=0)
        ends = jnp.where(own_edge, ends, 0.0)
        high, low = split(ends)
        high = high.astype(jnp.float32)
        low = low.astype(jnp.float32)
        ends = high + pltpu.roll(low, END_PART, 1) + pltpu.roll(high, 2 * END_PART, 1)
        high, low = split(block)
        inner, finer = wy_ref[0:owned], wy_ref[owned : 2 * owned]
        result = dot(high, inner) + dot(low, inner) + dot(high, finer)
        result = result + dot(ends.astype(jnp.bfloat16), wy_ref[2 * owned : 2 * owned + LANES])
        high, low = split(result)
        at = pl.ds(pl.multiple_of((p + 1) * total, 16), total)
        y_high[at, :] = high
        y_low[at, :] = low

    loads[1].wait()
    loads[2].wait()
    for k in range(1, slabs):
        p = lax.rem(s + slabs - k, slabs)
        from_peer(p).wait_recv()
        forward(p)
        along_y(lax.rem(p + 1, slabs))
    along_y(lax.rem(s + 1, slabs))

    sums = [jnp.zeros((rows, owned), jnp.float32) for _ in range(6)]

    def group(g, sums):
        at = pl.ds(pl.multiple_of(g * total, 16), 3 * total)
        smooth_y = slice(0, owned)
        deriv_y = slice(owned, 2 * owned)
        two = slice(0, 2 * body_rows)
        one = slice(2 * body_rows, 3 * body_rows)

        def gradient(out, field):
            high = y_high[at, field]
            low = y_low[at, field]
            return dot(wzx_ref[0, out, :], high) + dot(wzx_ref[0, out, :], low) + dot(wzx_ref[1, out, :], high)

        pair = gradient(two, smooth_y)
        grad_z = pair[:body_rows]
        grad_x = pair[body_rows:]
        grad_y = gradient(one, deriv_y)
        products = (
            grad_z * grad_z, grad_z * grad_x, grad_z * grad_y,
            grad_x * grad_x, grad_x * grad_y, grad_y * grad_y,
        )
        return tuple(
            held + product.reshape(planes, rows, owned).sum(axis=0)
            for held, product in zip(sums, products)
        )

    sums = lax.fori_loop(0, slabs, group, tuple(sums))
    loads[3].wait()
    mixed = exact_dot(whist_ref[...], jnp.concatenate(sums, axis=0))
    cell = lax.broadcasted_iota(jnp.int32, (owned, owned // POOL), 0)
    voxel = lax.broadcasted_iota(jnp.int32, (owned, owned // POOL), 1)
    pooled = exact_dot(mixed, (cell // POOL == voxel).astype(jnp.float32))
    for b in range(rows // POOL):
        out_ref[0, b] = pooled[b * DIRS : (b + 1) * DIRS]

    for send in sends:
        send.wait_send()
    for p in range(slabs):
        @pl.when(has_left)
        def _():
            to_left(p).wait_send()

        @pl.when(has_right)
        def _():
            to_right(p).wait_send()


def fused(slabs, tiles, volume):
    planes, rows, cells = volume.shape
    owned = cells // slabs
    band = planes * RADIUS
    body_rows = planes * rows
    total = body_rows + 2 * band
    wy = y_weights(owned)
    wzx = zx_weights(planes, rows)
    whist = histogram_weights(rows)
    f32, bf16 = jnp.float32, jnp.bfloat16
    dma = pltpu.SemaphoreType.DMA((slabs,))
    halo = pltpu.VMEM((slabs, band + EDGE, owned), f32)
    whole = pltpu.VMEM((slabs, body_rows + EDGE, owned), f32)
    held = pltpu.VMEM(((slabs + 2) * total, 2 * owned), bf16)
    return pl.pallas_call(
        functools.partial(kernel, slabs, tiles),
        out_shape=jax.ShapeDtypeStruct((1, rows // POOL, DIRS, owned // POOL), f32),
        in_specs=[pl.BlockSpec(memory_space=pltpu.HBM)] * 4,
        out_specs=pl.BlockSpec(memory_space=pltpu.VMEM),
        scratch_shapes=[
            pltpu.VMEM(volume.shape, f32),
            pltpu.VMEM(wy.shape, bf16),
            pltpu.VMEM(wzx.shape, bf16),
            pltpu.VMEM(whist.shape, f32),
            whole, whole, halo, halo, held, held,
            pltpu.SemaphoreType.DMA((4,)),
            dma, dma, dma, dma, dma, dma,
        ],
        compiler_params=pltpu.CompilerParams(
            collective_id=0, has_side_effects=True, vmem_limit_bytes=40 * 1024 * 1024
        ),
    )(volume, jnp.asarray(wy), jnp.asarray(wzx), jnp.asarray(whist))


def fits(slabs, tiles, planes, rows, cells):
    owned = cells // slabs
    return (
        slabs * planes == POOL and planes >= RADIUS and planes * rows == LANES
        and rows % POOL == 0 and rows >= 4 * RADIUS and (planes * RADIUS) % 16 == 0
        and owned % LANES == 0 and slabs * EDGE <= LANES
    )


def solution(mesh):
    slabs, tiles = mesh.shape["slab"], mesh.shape["tile"]

    def whole(volume):
        if slabs > 1 and tiles > 1 and fits(slabs, tiles, *volume.shape):
            return fused(slabs, tiles, volume)
        return body(volume)

    return jax.shard_map(
        whole,
        mesh=mesh,
        in_specs=(P("slab", "tile", None),),
        out_specs=P(None, "tile", None, "slab"),
        check_vma=False,
    )
```

```python
import functools

import jax
import jax.numpy as jnp
import ml_dtypes
import numpy as np
from jax import lax
from jax.experimental import pallas as pl
from jax.experimental.pallas import tpu as pltpu
from jax.sharding import PartitionSpec as P

RADIUS = 4
POOL = 16
DIRS = 32
MESH = pl.DeviceIdType.MESH
LANES = 128
CHUNKS = 2
EDGE = 2 * RADIUS
END_PART = 4 * EDGE


def extended(cells, sides, width):
    for axis, dim in sides:
        count = lax.axis_size(axis)
        ends = count - 1
        head = lax.slice_in_dim(cells, 0, width, axis=dim)
        tail = lax.slice_in_dim(cells, cells.shape[dim] - width, cells.shape[dim], axis=dim)
        cells = jnp.concatenate(
            [
                lax.ppermute(tail, axis, [(i, (i + 1) % count) for i in range(ends)]),
                cells,
                lax.ppermute(head, axis, [((i + 1) % count, i) for i in range(ends)]),
            ],
            axis=dim,
        )
    return cells


def kernel_taps():
    offsets = jnp.arange(-RADIUS, RADIUS + 1).astype(jnp.float32)
    base = jnp.exp(-offsets * offsets / 8.0)
    smooth = base / jnp.sqrt(jnp.sum(base * base))
    slope = -offsets * base
    deriv = slope / jnp.sqrt(jnp.sum(slope * slope))
    return (smooth, deriv)


def direction_table():
    index = jnp.arange(DIRS).astype(jnp.float32)
    height = 1.0 - (index + 0.5) / DIRS
    radial = jnp.sqrt(1.0 - height * height)
    phase = 2.399963229728653 * index
    d_x = radial * jnp.cos(phase)
    d_y = radial * jnp.sin(phase)
    return jnp.stack(
        [
            height * height,
            2.0 * height * d_x,
            2.0 * height * d_y,
            d_x * d_x,
            2.0 * d_x * d_y,
            d_y * d_y,
        ],
        axis=1,
    )


def filtered(padded, weights, axis, count):
    total = weights[0] * lax.slice_in_dim(padded, 0, count, axis=axis)
    for shift_index in range(1, 2 * RADIUS + 1):
        total = total + weights[shift_index] * lax.slice_in_dim(
            padded, shift_index, shift_index + count, axis=axis
        )
    return total


def pooled_full(field):
    planes, rows, cells = field.shape
    return field.reshape(planes // POOL, POOL, rows // POOL, POOL, cells // POOL, POOL).sum(
        axis=(1, 3, 5)
    )


def body(volume):
    smooth, deriv = kernel_taps()
    planes, rows, cells = volume.shape
    coeffs = direction_table()
    regrouped = lax.all_to_all(volume, "slab", split_axis=2, concat_axis=0, tiled=True)
    depth = regrouped.shape[0]
    owned = regrouped.shape[2]
    padded = extended(regrouped, (("slab", 2), ("tile", 1)), RADIUS)
    zpad = jnp.pad(padded, ((RADIUS, RADIUS), (0, 0), (0, 0)))
    z_smooth = filtered(zpad, smooth, 0, depth)
    z_deriv = filtered(zpad, deriv, 0, depth)
    both_smooth = filtered(z_smooth, smooth, 1, rows)
    smooth_deriv = filtered(z_smooth, deriv, 1, rows)
    deriv_smooth = filtered(z_deriv, smooth, 1, rows)
    grad_y = filtered(both_smooth, deriv, 2, owned)
    grad_x = filtered(smooth_deriv, smooth, 2, owned)
    grad_z = filtered(deriv_smooth, smooth, 2, owned)
    tensor = jnp.stack(
        [
            pooled_full(grad_z * grad_z),
            pooled_full(grad_z * grad_x),
            pooled_full(grad_z * grad_y),
            pooled_full(grad_x * grad_x),
            pooled_full(grad_x * grad_y),
            pooled_full(grad_y * grad_y),
        ]
    )
    hist = jnp.einsum("kc,cabv->abkv", coeffs, tensor, precision=lax.Precision.HIGHEST)
    return hist / float(POOL**3)


def host_taps():
    offsets = np.arange(-RADIUS, RADIUS + 1).astype(np.float64)
    base = np.exp(-offsets * offsets / 8.0)
    slope = -offsets * base
    return base / np.sqrt(np.sum(base * base)), slope / np.sqrt(np.sum(slope * slope))


def host_directions():
    index = np.arange(DIRS).astype(np.float32)
    height = np.float32(1.0) - (index + np.float32(0.5)) / np.float32(DIRS)
    radial = np.sqrt(np.float32(1.0) - height * height)
    phase = np.float32(2.399963229728653) * index
    d_x = radial * np.cos(phase)
    d_y = radial * np.sin(phase)
    two = np.float32(2.0)
    return np.stack(
        [height * height, two * height * d_x, two * height * d_y, d_x * d_x, two * d_x * d_y, d_y * d_y],
        axis=1,
    ).astype(np.float32)


def tap_at(weights, distance):
    index = distance + RADIUS
    inside = (index >= 0) & (index <= 2 * RADIUS)
    return np.where(inside, weights[np.clip(index, 0, 2 * RADIUS)], 0.0)


def halves(matrix):
    high = matrix.astype(np.float32).astype(ml_dtypes.bfloat16)
    low = (matrix - high.astype(np.float64)).astype(np.float32).astype(ml_dtypes.bfloat16)
    return np.stack([high, low])


def y_weights(owned):
    smooth, deriv = host_taps()
    edge = np.concatenate([np.arange(-RADIUS, 0), owned + np.arange(RADIUS)])
    out = np.arange(owned)
    inner = halves(np.concatenate([tap_at(w, out[:, None] - out[None, :]) for w in (smooth, deriv)], axis=1))
    outer = halves(np.concatenate([tap_at(w, edge[:, None] - out[None, :]) for w in (smooth, deriv)], axis=1))
    ends = np.zeros((LANES, 2 * owned), ml_dtypes.bfloat16)
    for part, which in enumerate((0, 0, 1)):
        for copy in range(3):
            start = part * END_PART + copy * EDGE
            ends[start : start + EDGE] = outer[which]
    return np.concatenate([inner[0], inner[1], ends], axis=0)


def zx_weights(planes, rows):
    smooth, deriv = host_taps()
    z_out, x_out = (g.ravel()[:, None] for g in np.meshgrid(np.arange(planes), np.arange(rows), indexing="ij"))
    step = np.arange(EDGE)
    around = np.where(step < RADIUS, rows + step, step - EDGE)
    tables = []
    for places in (np.arange(rows), around):
        z_in, x_in = (g.ravel()[None, :] for g in np.meshgrid(np.arange(planes), places, indexing="ij"))
        fields = []
        for z_taps, x_taps in ((deriv, smooth), (smooth, deriv), (smooth, smooth)):
            blocks = [
                tap_at(z_taps, group * planes + z_in - z_out) * tap_at(x_taps, x_in - x_out)
                for group in (-1, 0, 1)
            ]
            fields.append(np.concatenate(blocks, axis=1))
        tables.append(halves(np.concatenate(fields, axis=0)))
    inner, outer = tables
    return inner, np.concatenate([outer[0], outer[0], outer[1]], axis=1)


def histogram_weights(rows):
    voxels = rows // POOL
    inside = (np.arange(rows)[None, :] // POOL == np.arange(voxels)[:, None]).astype(np.float32)
    table = host_directions()[None, :, :, None] * inside[:, None, None, :]
    return (table.reshape(voxels * DIRS, -1) / np.float32(POOL**3)).astype(np.float32)


def split(values):
    high = values.astype(jnp.bfloat16)
    low = (values - high.astype(jnp.float32)).astype(jnp.bfloat16)
    return high, low


def dot(a, b):
    return jnp.dot(a, b, preferred_element_type=jnp.float32)


def exact_dot(a, b):
    return jnp.dot(a, b, preferred_element_type=jnp.float32, precision=lax.Precision.HIGHEST)


def kernel(
    slabs, tiles, x_hbm, wy_hbm, wzx_hbm, wring_hbm, whist_hbm, out_ref,
    x_ref, wy_ref, wzx_ref, wring_ref, whist_ref,
    recv, halo_l, halo_r, ends_out, ends_in, ends_l, ends_r, ends_main, ends_ring,
    y_high, y_low, ring_high, ring_low, partial,
    load_sem, send_sem, recv_sem, end_send, end_recv, side_sem, fl_send, fl_recv, fr_send, fr_recv,
):
    planes, rows, cells = x_ref.shape
    owned = cells // slabs
    inner_rows = planes * rows
    ring_rows = planes * EDGE
    part = planes // CHUNKS
    s = lax.axis_index("slab")
    t = lax.axis_index("tile")
    has_left = t > 0
    has_right = t < tiles - 1

    pairs = (
        (x_hbm, x_ref), (wy_hbm, wy_ref), (wzx_hbm, wzx_ref), (wring_hbm, wring_ref), (whist_hbm, whist_ref)
    )
    loads = [pltpu.make_async_copy(src, dst, load_sem.at[i]) for i, (src, dst) in enumerate(pairs)]
    for load in loads:
        load.start()

    barrier = pltpu.get_barrier_semaphore()
    for k in range(1, slabs):
        pl.semaphore_signal(barrier, inc=1, device_id=(lax.rem(s + k, slabs), t), device_id_type=MESH)

    @pl.when(has_left)
    def _():
        pl.semaphore_signal(barrier, inc=1, device_id=(s, t - 1), device_id_type=MESH)

    @pl.when(has_right)
    def _():
        pl.semaphore_signal(barrier, inc=1, device_id=(s, t + 1), device_id_type=MESH)

    loads[0].wait()
    lane = lax.broadcasted_iota(jnp.int32, (inner_rows, LANES), 1)
    edges = jnp.zeros((inner_rows, LANES), jnp.float32)

    def side(d, first):
        if d < 0 or d >= slabs:
            return jnp.zeros((inner_rows, LANES), jnp.float32)
        return x_ref[:, :, first : first + LANES].reshape(inner_rows, LANES)

    for d in range(slabs):
        before = side(d - 1, d * owned - LANES)
        after = side(d + 1, (d + 1) * owned)
        both = jnp.where(lane >= LANES // 2, before, after)
        turned = pltpu.roll(both, d * EDGE + RADIUS, 1)
        edges = jnp.where(lane // EDGE == d, turned, edges)
    edges = edges.T
    for d in range(slabs):
        ends_out[d] = edges[d * EDGE : (d + 1) * EDGE]

    beside = jnp.where(has_left, 1, 0) + jnp.where(has_right, 1, 0)
    pl.semaphore_wait(barrier, slabs - 1 + beside)

    def ends_copy(src, dst, k):
        return pltpu.make_async_remote_copy(
            src_ref=ends_out.at[dst], dst_ref=ends_in.at[src],
            send_sem=end_send.at[k], recv_sem=end_recv.at[src],
            device_id=(dst, t), device_id_type=MESH,
        )

    def block_copy(src, dst, k, c):
        first = pl.multiple_of(dst * owned, LANES)
        return pltpu.make_async_remote_copy(
            src_ref=x_ref.at[pl.ds(c * part, part), :, pl.ds(first, owned)],
            dst_ref=recv.at[src, pl.ds(c * part, part)],
            send_sem=send_sem.at[k * CHUNKS + c], recv_sem=recv_sem.at[src * CHUNKS + c],
            device_id=(dst, t), device_id_type=MESH,
        )

    def ends_left():
        return pltpu.make_async_remote_copy(
            src_ref=ends_in, dst_ref=ends_r, send_sem=side_sem.at[0], recv_sem=side_sem.at[1],
            device_id=(s, t - 1), device_id_type=MESH,
        )

    def ends_right():
        return pltpu.make_async_remote_copy(
            src_ref=ends_in, dst_ref=ends_l, send_sem=side_sem.at[2], recv_sem=side_sem.at[3],
            device_id=(s, t + 1), device_id_type=MESH,
        )

    def to_left(p, c):
        here = pl.ds(c * part, part)
        return pltpu.make_async_remote_copy(
            src_ref=recv.at[p, here, pl.ds(0, EDGE)], dst_ref=halo_r.at[p, here],
            send_sem=fl_send.at[p * CHUNKS + c], recv_sem=fl_recv.at[p * CHUNKS + c],
            device_id=(s, t - 1), device_id_type=MESH,
        )

    def to_right(p, c):
        here = pl.ds(c * part, part)
        return pltpu.make_async_remote_copy(
            src_ref=recv.at[p, here, pl.ds(rows - EDGE, EDGE)], dst_ref=halo_l.at[p, here],
            send_sem=fr_send.at[p * CHUNKS + c], recv_sem=fr_recv.at[p * CHUNKS + c],
            device_id=(s, t + 1), device_id_type=MESH,
        )

    def forward(p, c):
        @pl.when(has_left)
        def _():
            to_left(p, c).start()

        @pl.when(has_right)
        def _():
            to_right(p, c).start()

    sends = [ends_copy(s, lax.rem(s + k, slabs), k) for k in range(1, slabs)]
    sends += [block_copy(s, lax.rem(s + k, slabs), k, c) for c in range(CHUNKS) for k in range(1, slabs)]
    for send in sends:
        send.start()

    recv[s] = x_ref[:, :, pl.ds(pl.multiple_of(s * owned, LANES), owned)]
    ends_in[s] = ends_out[s]
    for c in range(CHUNKS):
        forward(s, c)

    @pl.when(jnp.logical_not(has_left))
    def _():
        halo_l[...] = jnp.zeros_like(halo_l)
        ends_l[...] = jnp.zeros_like(ends_l)

    @pl.when(jnp.logical_not(has_right))
    def _():
        halo_r[...] = jnp.zeros_like(halo_r)
        ends_r[...] = jnp.zeros_like(ends_r)

    for ref, count in ((y_high, inner_rows), (y_low, inner_rows), (ring_high, ring_rows), (ring_low, ring_rows)):
        blank = jnp.zeros((count, 2 * owned), jnp.bfloat16)
        ref[0:count, :] = blank
        ref[(slabs + 1) * count : (slabs + 2) * count, :] = blank

    for k in range(1, slabs):
        p = lax.rem(s + slabs - k, slabs)
        ends_copy(p, p, 0).wait_recv()

    @pl.when(has_left)
    def _():
        ends_left().start()

    @pl.when(has_right)
    def _():
        ends_right().start()

    @pl.when(has_left)
    def _():
        ends_right().wait_recv()

    @pl.when(has_right)
    def _():
        ends_left().wait_recv()

    def packed(ends):
        high, low = split(ends)
        high = high.astype(jnp.float32)
        low = low.astype(jnp.float32)
        all_parts = high + pltpu.roll(low, END_PART, 1) + pltpu.roll(high, 2 * END_PART, 1)
        return all_parts.astype(jnp.bfloat16)

    ring_lane = lax.broadcasted_iota(jnp.int32, (planes, EDGE, LANES), 2) // EDGE
    ring_step = lax.broadcasted_iota(jnp.int32, (planes, EDGE, LANES), 1)
    rest = jnp.zeros((LANES - 3 * EDGE, LANES), jnp.float32)
    for p in range(slabs):
        turned = jnp.concatenate([ends_in[p], ends_l[p], ends_r[p], rest], axis=0).T
        ends_main[p] = packed(jnp.where(lane < EDGE, turned, 0.0))
        turned = turned.reshape(planes, rows, LANES)
        right = jnp.where(ring_lane == 2, turned[:, 0:EDGE], 0.0)
        left = jnp.where(ring_lane == 1, turned[:, rows - EDGE : rows], 0.0)
        ring = jnp.where(ring_step < RADIUS, right, left).reshape(ring_rows, LANES)
        ends_ring[p * ring_rows : (p + 1) * ring_rows, :] = packed(ring)

    loads[1].wait()

    def along_y(block, ends):
        high, low = split(block)
        inner, finer = wy_ref[0:owned], wy_ref[owned : 2 * owned]
        result = dot(high, inner) + dot(low, inner) + dot(high, finer)
        return split(result + dot(ends, wy_ref[2 * owned : 2 * owned + LANES]))

    def inner_along_y(p):
        high, low = along_y(recv[p].reshape(inner_rows, owned), ends_main[p])
        at = pl.ds(pl.multiple_of((p + 1) * inner_rows, 16), inner_rows)
        y_high[at, :] = high
        y_low[at, :] = low

    inner_along_y(s)
    for c in range(CHUNKS):
        for k in range(1, slabs):
            p = lax.rem(s + slabs - k, slabs)
            block_copy(p, p, 0, c).wait_recv()
            forward(p, c)
    for k in range(1, slabs):
        inner_along_y(lax.rem(s + slabs - k, slabs))

    smooth_y = slice(0, owned)
    deriv_y = slice(owned, 2 * owned)
    pair = slice(0, 2 * inner_rows)
    last = slice(2 * inner_rows, 3 * inner_rows)
    loads[2].wait()

    def inner_group(g, carry):
        at = pl.ds(pl.multiple_of(g * inner_rows, 16), 3 * inner_rows)
        for out, field in ((pair, smooth_y), (last, deriv_y)):
            high = y_high[at, field]
            low = y_low[at, field]
            coarse = wzx_ref[0, out, :]
            partial[g, out, :] = dot(coarse, high) + dot(coarse, low) + dot(wzx_ref[1, out, :], high)
        return carry

    lax.fori_loop(0, slabs, inner_group, 0)

    for p in range(slabs):
        for c in range(CHUNKS):
            @pl.when(has_left)
            def _():
                to_right(p, c).wait_recv()

            @pl.when(has_right)
            def _():
                to_left(p, c).wait_recv()

    step = lax.broadcasted_iota(jnp.int32, (slabs, planes, EDGE, owned), 2)
    ring = jnp.where(step < RADIUS, halo_r[...], halo_l[...]).reshape(slabs * ring_rows, owned)
    high, low = along_y(ring, ends_ring[...])
    ring_high[ring_rows : (slabs + 1) * ring_rows, :] = high
    ring_low[ring_rows : (slabs + 1) * ring_rows, :] = low
    loads[3].wait()

    def group(g, sums):
        at = pl.ds(pl.multiple_of(g * ring_rows, 16), 3 * ring_rows)

        def gradient(out, field):
            high = ring_high[at, field]
            low = ring_low[at, field]
            return partial[g, out, :] + dot(wring_ref[out, :], jnp.concatenate([high, low, high], axis=0))

        both = gradient(pair, smooth_y)
        grad_z = both[:inner_rows]
        grad_x = both[inner_rows:]
        grad_y = gradient(last, deriv_y)
        products = (
            grad_z * grad_z, grad_z * grad_x, grad_z * grad_y,
            grad_x * grad_x, grad_x * grad_y, grad_y * grad_y,
        )
        return tuple(
            held + product.reshape(planes, rows, owned).sum(axis=0)
            for held, product in zip(sums, products)
        )

    blank = jnp.zeros((rows, owned), jnp.float32)
    sums = lax.fori_loop(0, slabs, group, (blank,) * 6)
    loads[4].wait()
    mixed = exact_dot(whist_ref[...], jnp.concatenate(sums, axis=0))
    cell = lax.broadcasted_iota(jnp.int32, (owned, owned // POOL), 0)
    voxel = lax.broadcasted_iota(jnp.int32, (owned, owned // POOL), 1)
    pooled = exact_dot(mixed, (cell // POOL == voxel).astype(jnp.float32))
    for b in range(rows // POOL):
        out_ref[0, b] = pooled[b * DIRS : (b + 1) * DIRS]

    for send in sends:
        send.wait_send()

    @pl.when(has_left)
    def _():
        ends_left().wait_send()
        for p in range(slabs):
            for c in range(CHUNKS):
                to_left(p, c).wait_send()

    @pl.when(has_right)
    def _():
        ends_right().wait_send()
        for p in range(slabs):
            for c in range(CHUNKS):
                to_right(p, c).wait_send()


def fused(slabs, tiles, volume):
    planes, rows, cells = volume.shape
    owned = cells // slabs
    inner_rows = planes * rows
    ring_rows = planes * EDGE
    wy = y_weights(owned)
    wzx, wring = zx_weights(planes, rows)
    whist = histogram_weights(rows)
    f32, bf16 = jnp.float32, jnp.bfloat16
    one = pltpu.SemaphoreType.DMA((slabs,))
    many = pltpu.SemaphoreType.DMA((slabs * CHUNKS,))
    halo = pltpu.VMEM((slabs, planes, EDGE, owned), f32)
    ends = pltpu.VMEM((slabs, EDGE, LANES), f32)
    held = pltpu.VMEM(((slabs + 2) * inner_rows, 2 * owned), bf16)
    ring = pltpu.VMEM(((slabs + 2) * ring_rows, 2 * owned), bf16)
    return pl.pallas_call(
        functools.partial(kernel, slabs, tiles),
        out_shape=jax.ShapeDtypeStruct((1, rows // POOL, DIRS, owned // POOL), f32),
        in_specs=[pl.BlockSpec(memory_space=pl.ANY)] * 5,
        out_specs=pl.BlockSpec(memory_space=pltpu.VMEM),
        scratch_shapes=[
            pltpu.VMEM(volume.shape, f32),
            pltpu.VMEM(wy.shape, bf16),
            pltpu.VMEM(wzx.shape, bf16),
            pltpu.VMEM(wring.shape, bf16),
            pltpu.VMEM(whist.shape, f32),
            pltpu.VMEM((slabs, planes, rows, owned), f32),
            halo, halo, ends, ends, ends, ends,
            pltpu.VMEM((slabs, inner_rows, LANES), bf16),
            pltpu.VMEM((slabs * ring_rows, LANES), bf16),
            held, held, ring, ring,
            pltpu.VMEM((slabs, 3 * inner_rows, owned), f32),
            pltpu.SemaphoreType.DMA((5,)),
            many, many, one, one, pltpu.SemaphoreType.DMA((4,)), many, many, many, many,
        ],
        compiler_params=pltpu.CompilerParams(collective_id=0, has_side_effects=True),
    )(volume, jnp.asarray(wy), jnp.asarray(wzx), jnp.asarray(wring), jnp.asarray(whist))


def fits(slabs, tiles, planes, rows, cells):
    owned = cells // slabs
    return (
        slabs * planes == POOL and planes >= RADIUS and planes * rows == LANES
        and rows % POOL == 0 and planes % CHUNKS == 0 and (planes * EDGE) % 16 == 0
        and owned % LANES == 0 and slabs * EDGE <= LANES
    )


def solution(mesh):
    slabs, tiles = mesh.shape["slab"], mesh.shape["tile"]

    def whole(volume):
        if slabs > 1 and tiles > 1 and fits(slabs, tiles, *volume.shape):
            return fused(slabs, tiles, volume)
        return body(volume)

    return jax.shard_map(
        whole,
        mesh=mesh,
        in_specs=(P("slab", "tile", None),),
        out_specs=P(None, "tile", None, "slab"),
        check_vma=False,
    )
```

```python
import functools

import jax
import jax.numpy as jnp
import ml_dtypes
import numpy as np
from jax import lax
from jax.experimental import pallas as pl
from jax.experimental.pallas import tpu as pltpu
from jax.sharding import PartitionSpec as P

RADIUS = 4
POOL = 16
DIRS = 32
MESH = pl.DeviceIdType.MESH
LANES = 128
CHUNKS = 2
EDGE = 2 * RADIUS
END_PART = 4 * EDGE


def extended(cells, sides, width):
    for axis, dim in sides:
        count = lax.axis_size(axis)
        ends = count - 1
        head = lax.slice_in_dim(cells, 0, width, axis=dim)
        tail = lax.slice_in_dim(cells, cells.shape[dim] - width, cells.shape[dim], axis=dim)
        cells = jnp.concatenate(
            [
                lax.ppermute(tail, axis, [(i, (i + 1) % count) for i in range(ends)]),
                cells,
                lax.ppermute(head, axis, [((i + 1) % count, i) for i in range(ends)]),
            ],
            axis=dim,
        )
    return cells


def kernel_taps():
    offsets = jnp.arange(-RADIUS, RADIUS + 1).astype(jnp.float32)
    base = jnp.exp(-offsets * offsets / 8.0)
    smooth = base / jnp.sqrt(jnp.sum(base * base))
    slope = -offsets * base
    deriv = slope / jnp.sqrt(jnp.sum(slope * slope))
    return (smooth, deriv)


def direction_table():
    index = jnp.arange(DIRS).astype(jnp.float32)
    height = 1.0 - (index + 0.5) / DIRS
    radial = jnp.sqrt(1.0 - height * height)
    phase = 2.399963229728653 * index
    d_x = radial * jnp.cos(phase)
    d_y = radial * jnp.sin(phase)
    return jnp.stack(
        [
            height * height,
            2.0 * height * d_x,
            2.0 * height * d_y,
            d_x * d_x,
            2.0 * d_x * d_y,
            d_y * d_y,
        ],
        axis=1,
    )


def filtered(padded, weights, axis, count):
    total = weights[0] * lax.slice_in_dim(padded, 0, count, axis=axis)
    for shift_index in range(1, 2 * RADIUS + 1):
        total = total + weights[shift_index] * lax.slice_in_dim(
            padded, shift_index, shift_index + count, axis=axis
        )
    return total


def pooled_full(field):
    planes, rows, cells = field.shape
    return field.reshape(planes // POOL, POOL, rows // POOL, POOL, cells // POOL, POOL).sum(
        axis=(1, 3, 5)
    )


def body(volume):
    smooth, deriv = kernel_taps()
    planes, rows, cells = volume.shape
    coeffs = direction_table()
    regrouped = lax.all_to_all(volume, "slab", split_axis=2, concat_axis=0, tiled=True)
    depth = regrouped.shape[0]
    owned = regrouped.shape[2]
    padded = extended(regrouped, (("slab", 2), ("tile", 1)), RADIUS)
    zpad = jnp.pad(padded, ((RADIUS, RADIUS), (0, 0), (0, 0)))
    z_smooth = filtered(zpad, smooth, 0, depth)
    z_deriv = filtered(zpad, deriv, 0, depth)
    both_smooth = filtered(z_smooth, smooth, 1, rows)
    smooth_deriv = filtered(z_smooth, deriv, 1, rows)
    deriv_smooth = filtered(z_deriv, smooth, 1, rows)
    grad_y = filtered(both_smooth, deriv, 2, owned)
    grad_x = filtered(smooth_deriv, smooth, 2, owned)
    grad_z = filtered(deriv_smooth, smooth, 2, owned)
    tensor = jnp.stack(
        [
            pooled_full(grad_z * grad_z),
            pooled_full(grad_z * grad_x),
            pooled_full(grad_z * grad_y),
            pooled_full(grad_x * grad_x),
            pooled_full(grad_x * grad_y),
            pooled_full(grad_y * grad_y),
        ]
    )
    hist = jnp.einsum("kc,cabv->abkv", coeffs, tensor, precision=lax.Precision.HIGHEST)
    return hist / float(POOL**3)


def host_taps():
    offsets = np.arange(-RADIUS, RADIUS + 1).astype(np.float64)
    base = np.exp(-offsets * offsets / 8.0)
    slope = -offsets * base
    return base / np.sqrt(np.sum(base * base)), slope / np.sqrt(np.sum(slope * slope))


def host_directions():
    index = np.arange(DIRS).astype(np.float32)
    height = np.float32(1.0) - (index + np.float32(0.5)) / np.float32(DIRS)
    radial = np.sqrt(np.float32(1.0) - height * height)
    phase = np.float32(2.399963229728653) * index
    d_x = radial * np.cos(phase)
    d_y = radial * np.sin(phase)
    two = np.float32(2.0)
    return np.stack(
        [height * height, two * height * d_x, two * height * d_y, d_x * d_x, two * d_x * d_y, d_y * d_y],
        axis=1,
    ).astype(np.float32)


def tap_at(weights, distance):
    index = distance + RADIUS
    inside = (index >= 0) & (index <= 2 * RADIUS)
    return np.where(inside, weights[np.clip(index, 0, 2 * RADIUS)], 0.0)


def halves(matrix):
    high = matrix.astype(np.float32).astype(ml_dtypes.bfloat16)
    low = (matrix - high.astype(np.float64)).astype(np.float32).astype(ml_dtypes.bfloat16)
    return np.stack([high, low])


def y_weights(owned):
    smooth, deriv = host_taps()
    edge = np.concatenate([np.arange(-RADIUS, 0), owned + np.arange(RADIUS)])
    out = np.arange(owned)
    inner = halves(np.concatenate([tap_at(w, out[:, None] - out[None, :]) for w in (smooth, deriv)], axis=1))
    outer = halves(np.concatenate([tap_at(w, edge[:, None] - out[None, :]) for w in (smooth, deriv)], axis=1))
    ends = np.zeros((LANES, 2 * owned), ml_dtypes.bfloat16)
    for part, which in enumerate((0, 0, 1)):
        for copy in range(3):
            start = part * END_PART + copy * EDGE
            ends[start : start + EDGE] = outer[which]
    return np.concatenate([inner[0], inner[1], ends], axis=0)


def zx_weights(planes, rows):
    smooth, deriv = host_taps()
    z_out, x_out = (g.ravel()[:, None] for g in np.meshgrid(np.arange(planes), np.arange(rows), indexing="ij"))
    step = np.arange(EDGE)
    around = np.where(step < RADIUS, rows + step, step - EDGE)
    grids = [np.meshgrid(np.arange(planes), places, indexing="ij") for places in (np.arange(rows), around)]
    z_in = np.concatenate([z.ravel() for z, _ in grids])[None, :]
    x_in = np.concatenate([x.ravel() for _, x in grids])[None, :]
    blocks = []
    for fields in (((deriv, smooth), (smooth, deriv)), ((smooth, smooth),)):
        for group in (-1, 0, 1):
            for z_taps, x_taps in fields:
                blocks.append(tap_at(z_taps, group * planes + z_in - z_out) * tap_at(x_taps, x_in - x_out))
    high, low = halves(np.concatenate(blocks, axis=0))
    return np.concatenate([high, high, low], axis=1)


def histogram_weights(rows):
    voxels = rows // POOL
    inside = (np.arange(rows)[None, :] // POOL == np.arange(voxels)[:, None]).astype(np.float32)
    table = host_directions()[None, :, :, None] * inside[:, None, None, :]
    return (table.reshape(voxels * DIRS, -1) / np.float32(POOL**3)).astype(np.float32)


def split(values):
    high = values.astype(jnp.bfloat16)
    low = (values - high.astype(jnp.float32)).astype(jnp.bfloat16)
    return high, low


def dot(a, b):
    return jnp.dot(a, b, preferred_element_type=jnp.float32)


def exact_dot(a, b):
    return jnp.dot(a, b, preferred_element_type=jnp.float32, precision=lax.Precision.HIGHEST)


def kernel(
    slabs, tiles, x_hbm, wy_hbm, wzx_hbm, whist_hbm, out_ref,
    x_ref, wy_ref, wzx_ref, whist_ref,
    recv, halo_l, halo_r, ends_out, ends_in, ends_l, ends_r, ends_all, partial,
    load_sem, send_sem, recv_sem, end_send, end_recv, side_sem, fl_send, fl_recv, fr_send, fr_recv,
):
    planes, rows, cells = x_ref.shape
    owned = cells // slabs
    inner_rows = planes * rows
    ring_rows = planes * EDGE
    part = planes // CHUNKS
    s = lax.axis_index("slab")
    t = lax.axis_index("tile")
    has_left = t > 0
    has_right = t < tiles - 1

    pairs = (
        (x_hbm, x_ref), (wy_hbm, wy_ref), (wzx_hbm, wzx_ref), (whist_hbm, whist_ref)
    )
    loads = [pltpu.make_async_copy(src, dst, load_sem.at[i]) for i, (src, dst) in enumerate(pairs)]
    for load in loads:
        load.start()

    barrier = pltpu.get_barrier_semaphore()
    for k in range(1, slabs):
        pl.semaphore_signal(barrier, inc=1, device_id=(lax.rem(s + k, slabs), t), device_id_type=MESH)

    @pl.when(has_left)
    def _():
        pl.semaphore_signal(barrier, inc=1, device_id=(s, t - 1), device_id_type=MESH)

    @pl.when(has_right)
    def _():
        pl.semaphore_signal(barrier, inc=1, device_id=(s, t + 1), device_id_type=MESH)

    loads[0].wait()
    lane = lax.broadcasted_iota(jnp.int32, (inner_rows, LANES), 1)
    edges = jnp.zeros((inner_rows, LANES), jnp.float32)

    def side(d, first):
        if d < 0 or d >= slabs:
            return jnp.zeros((inner_rows, LANES), jnp.float32)
        return x_ref[:, :, first : first + LANES].reshape(inner_rows, LANES)

    for d in range(slabs):
        before = side(d - 1, d * owned - LANES)
        after = side(d + 1, (d + 1) * owned)
        both = jnp.where(lane >= LANES // 2, before, after)
        turned = pltpu.roll(both, d * EDGE + RADIUS, 1)
        edges = jnp.where(lane // EDGE == d, turned, edges)
    edges = edges.T
    for d in range(slabs):
        ends_out[d] = edges[d * EDGE : (d + 1) * EDGE]

    beside = jnp.where(has_left, 1, 0) + jnp.where(has_right, 1, 0)
    pl.semaphore_wait(barrier, slabs - 1 + beside)

    def ends_copy(src, dst, k):
        return pltpu.make_async_remote_copy(
            src_ref=ends_out.at[dst], dst_ref=ends_in.at[src],
            send_sem=end_send.at[k], recv_sem=end_recv.at[src],
            device_id=(dst, t), device_id_type=MESH,
        )

    def block_copy(src, dst, k, c):
        first = pl.multiple_of(dst * owned, LANES)
        return pltpu.make_async_remote_copy(
            src_ref=x_ref.at[pl.ds(c * part, part), :, pl.ds(first, owned)],
            dst_ref=recv.at[src, pl.ds(c * part, part)],
            send_sem=send_sem.at[k * CHUNKS + c], recv_sem=recv_sem.at[src * CHUNKS + c],
            device_id=(dst, t), device_id_type=MESH,
        )

    def ends_left():
        return pltpu.make_async_remote_copy(
            src_ref=ends_in, dst_ref=ends_r, send_sem=side_sem.at[0], recv_sem=side_sem.at[1],
            device_id=(s, t - 1), device_id_type=MESH,
        )

    def ends_right():
        return pltpu.make_async_remote_copy(
            src_ref=ends_in, dst_ref=ends_l, send_sem=side_sem.at[2], recv_sem=side_sem.at[3],
            device_id=(s, t + 1), device_id_type=MESH,
        )

    def to_left(p, c):
        here = pl.ds(c * part, part)
        return pltpu.make_async_remote_copy(
            src_ref=recv.at[p, here, pl.ds(0, EDGE)], dst_ref=halo_r.at[p, here],
            send_sem=fl_send.at[p * CHUNKS + c], recv_sem=fl_recv.at[p * CHUNKS + c],
            device_id=(s, t - 1), device_id_type=MESH,
        )

    def to_right(p, c):
        here = pl.ds(c * part, part)
        return pltpu.make_async_remote_copy(
            src_ref=recv.at[p, here, pl.ds(rows - EDGE, EDGE)], dst_ref=halo_l.at[p, here],
            send_sem=fr_send.at[p * CHUNKS + c], recv_sem=fr_recv.at[p * CHUNKS + c],
            device_id=(s, t + 1), device_id_type=MESH,
        )

    def forward(p, c):
        @pl.when(has_left)
        def _():
            to_left(p, c).start()

        @pl.when(has_right)
        def _():
            to_right(p, c).start()

    paired = slabs & (slabs - 1) == 0

    def peer_to(k):
        return s ^ k if paired else lax.rem(s + k, slabs)

    def peer_from(k):
        return s ^ k if paired else lax.rem(s + slabs - k, slabs)

    sends = [ends_copy(s, peer_to(k), k) for k in range(1, slabs)]
    sends += [block_copy(s, peer_to(k), k, c) for k in range(1, slabs) for c in range(CHUNKS)]
    for send in sends:
        send.start()

    recv[s] = x_ref[:, :, pl.ds(pl.multiple_of(s * owned, LANES), owned)]
    ends_in[s] = ends_out[s]
    for c in range(CHUNKS):
        forward(s, c)

    @pl.when(jnp.logical_not(has_left))
    def _():
        halo_l[...] = jnp.zeros_like(halo_l)
        ends_l[...] = jnp.zeros_like(ends_l)

    @pl.when(jnp.logical_not(has_right))
    def _():
        halo_r[...] = jnp.zeros_like(halo_r)
        ends_r[...] = jnp.zeros_like(ends_r)

    partial[...] = jnp.zeros_like(partial)
    for k in range(1, slabs):
        p = peer_from(k)
        ends_copy(p, p, 0).wait_recv()

    @pl.when(has_left)
    def _():
        ends_left().start()

    @pl.when(has_right)
    def _():
        ends_right().start()

    @pl.when(has_left)
    def _():
        ends_right().wait_recv()

    @pl.when(has_right)
    def _():
        ends_left().wait_recv()

    def packed(ends):
        high, low = split(ends)
        high = high.astype(jnp.float32)
        low = low.astype(jnp.float32)
        all_parts = high + pltpu.roll(low, END_PART, 1) + pltpu.roll(high, 2 * END_PART, 1)
        return all_parts.astype(jnp.bfloat16)

    ring_lane = lax.broadcasted_iota(jnp.int32, (planes, EDGE, LANES), 2) // EDGE
    ring_step = lax.broadcasted_iota(jnp.int32, (planes, EDGE, LANES), 1)
    rest = jnp.zeros((LANES - 3 * EDGE, LANES), jnp.float32)
    for p in range(slabs):
        turned = jnp.concatenate([ends_in[p], ends_l[p], ends_r[p], rest], axis=0).T
        ends_all[p, 0:inner_rows] = packed(jnp.where(lane < EDGE, turned, 0.0))
        turned = turned.reshape(planes, rows, LANES)
        right = jnp.where(ring_lane == 2, turned[:, 0:EDGE], 0.0)
        left = jnp.where(ring_lane == 1, turned[:, rows - EDGE : rows], 0.0)
        ring = jnp.where(ring_step < RADIUS, right, left).reshape(ring_rows, LANES)
        ends_all[p, inner_rows : inner_rows + ring_rows] = packed(ring)

    loads[1].wait()
    loads[2].wait()
    step = lax.broadcasted_iota(jnp.int32, (planes, EDGE, owned), 1)
    pair = 2 * inner_rows

    def add_source(p):
        for c in range(CHUNKS):
            @pl.when(has_left)
            def _():
                to_right(p, c).wait_recv()

            @pl.when(has_right)
            def _():
                to_left(p, c).wait_recv()

        ring = jnp.where(step < RADIUS, halo_r[p], halo_l[p]).reshape(ring_rows, owned)
        high, low = split(jnp.concatenate([recv[p].reshape(inner_rows, owned), ring], axis=0))
        inner, finer = wy_ref[0:owned], wy_ref[owned : 2 * owned]
        result = dot(high, inner) + dot(low, inner) + dot(high, finer)
        result = result + dot(ends_all[p], wy_ref[2 * owned : 2 * owned + LANES])
        high, low = split(result)
        parts = jnp.concatenate([high, low, high], axis=0)
        for out, count, first, field in ((0, pair, 0, 0), (pair, inner_rows, 3 * pair, owned)):
            share = dot(wzx_ref[first : first + 3 * count, :], parts[:, field : field + owned])
            for i in range(3):
                partial[p + 2 - i, out : out + count, :] += share[i * count : (i + 1) * count]

    def arrive(k):
        p = peer_from(k)
        for c in range(CHUNKS):
            block_copy(p, p, 0, c).wait_recv()
            forward(p, c)

    add_source(s)
    for k in range(1, slabs - 1):
        arrive(k)
    for k in range(1, slabs - 1):
        add_source(peer_from(k))
    arrive(slabs - 1)
    add_source(peer_from(slabs - 1))

    def group(g, sums):
        grad_z = partial[g + 1, 0:inner_rows, :]
        grad_x = partial[g + 1, inner_rows:pair, :]
        grad_y = partial[g + 1, pair : pair + inner_rows, :]
        products = (
            grad_z * grad_z, grad_z * grad_x, grad_z * grad_y,
            grad_x * grad_x, grad_x * grad_y, grad_y * grad_y,
        )
        return tuple(
            held + product.reshape(planes, rows, owned).sum(axis=0)
            for held, product in zip(sums, products)
        )

    blank = jnp.zeros((rows, owned), jnp.float32)
    sums = lax.fori_loop(0, slabs, group, (blank,) * 6)
    loads[3].wait()
    mixed = exact_dot(whist_ref[...], jnp.concatenate(sums, axis=0))
    voxel = lax.broadcasted_iota(jnp.int32, (owned // POOL, owned), 0)
    cell = lax.broadcasted_iota(jnp.int32, (owned // POOL, owned), 1)
    pooled = lax.dot_general(
        (cell // POOL == voxel).astype(jnp.float32), mixed, (((1,), (1,)), ((), ())),
        precision=lax.Precision.HIGHEST, preferred_element_type=jnp.float32,
    )
    for b in range(rows // POOL):
        out_ref[0, b] = pooled[:, b * DIRS : (b + 1) * DIRS]

    for send in sends:
        send.wait_send()

    @pl.when(has_left)
    def _():
        ends_left().wait_send()
        for p in range(slabs):
            for c in range(CHUNKS):
                to_left(p, c).wait_send()

    @pl.when(has_right)
    def _():
        ends_right().wait_send()
        for p in range(slabs):
            for c in range(CHUNKS):
                to_right(p, c).wait_send()


def fused(slabs, tiles, volume):
    planes, rows, cells = volume.shape
    owned = cells // slabs
    inner_rows = planes * rows
    ring_rows = planes * EDGE
    wy = y_weights(owned)
    wzx = zx_weights(planes, rows)
    whist = histogram_weights(rows)
    f32, bf16 = jnp.float32, jnp.bfloat16
    one = pltpu.SemaphoreType.DMA((slabs,))
    many = pltpu.SemaphoreType.DMA((slabs * CHUNKS,))
    halo = pltpu.VMEM((slabs, planes, EDGE, owned), f32)
    ends = pltpu.VMEM((slabs, EDGE, LANES), f32)
    turned = pl.pallas_call(
        functools.partial(kernel, slabs, tiles),
        out_shape=jax.ShapeDtypeStruct((1, rows // POOL, owned // POOL, DIRS), f32),
        in_specs=[pl.BlockSpec(memory_space=pl.ANY)] * 4,
        out_specs=pl.BlockSpec(memory_space=pltpu.VMEM),
        scratch_shapes=[
            pltpu.VMEM(volume.shape, f32),
            pltpu.VMEM(wy.shape, bf16),
            pltpu.VMEM(wzx.shape, bf16),
            pltpu.VMEM(whist.shape, f32),
            pltpu.VMEM((slabs, planes, rows, owned), f32),
            halo, halo, ends, ends, ends, ends,
            pltpu.VMEM((slabs, inner_rows + ring_rows, LANES), bf16),
            pltpu.VMEM((slabs + 2, 3 * inner_rows, owned), f32),
            pltpu.SemaphoreType.DMA((4,)),
            many, many, one, one, pltpu.SemaphoreType.DMA((4,)), many, many, many, many,
        ],
        compiler_params=pltpu.CompilerParams(collective_id=0, has_side_effects=True),
    )(volume, jnp.asarray(wy), jnp.asarray(wzx), jnp.asarray(whist))
    return jnp.swapaxes(turned, 2, 3)


def fits(slabs, tiles, planes, rows, cells):
    owned = cells // slabs
    return (
        slabs * planes == POOL and planes >= RADIUS and planes * rows == LANES
        and rows % POOL == 0 and planes % CHUNKS == 0 and (planes * EDGE) % 16 == 0
        and owned % LANES == 0 and slabs * EDGE <= LANES
    )


def solution(mesh):
    slabs, tiles = mesh.shape["slab"], mesh.shape["tile"]

    def whole(volume):
        if slabs > 1 and tiles > 1 and fits(slabs, tiles, *volume.shape):
            return fused(slabs, tiles, volume)
        return body(volume)

    return jax.shard_map(
        whole,
        mesh=mesh,
        in_specs=(P("slab", "tile", None),),
        out_specs=P(None, "tile", None, "slab"),
        check_vma=False,
    )
```

```python
import functools

import jax
import jax.numpy as jnp
import ml_dtypes
import numpy as np
from jax import lax
from jax.experimental import pallas as pl
from jax.experimental.pallas import tpu as pltpu
from jax.sharding import PartitionSpec as P

RADIUS = 4
POOL = 16
DIRS = 32
MESH = pl.DeviceIdType.MESH
LANES = 128
CHUNKS = 1
VMEM_LIMIT = 64 * 2**20 - 128 * 2**10
EDGE = 2 * RADIUS
END_PART = 4 * EDGE


def extended(cells, sides, width):
    for axis, dim in sides:
        count = lax.axis_size(axis)
        ends = count - 1
        head = lax.slice_in_dim(cells, 0, width, axis=dim)
        tail = lax.slice_in_dim(cells, cells.shape[dim] - width, cells.shape[dim], axis=dim)
        cells = jnp.concatenate(
            [
                lax.ppermute(tail, axis, [(i, (i + 1) % count) for i in range(ends)]),
                cells,
                lax.ppermute(head, axis, [((i + 1) % count, i) for i in range(ends)]),
            ],
            axis=dim,
        )
    return cells


def kernel_taps():
    offsets = jnp.arange(-RADIUS, RADIUS + 1).astype(jnp.float32)
    base = jnp.exp(-offsets * offsets / 8.0)
    smooth = base / jnp.sqrt(jnp.sum(base * base))
    slope = -offsets * base
    deriv = slope / jnp.sqrt(jnp.sum(slope * slope))
    return (smooth, deriv)


def direction_table():
    index = jnp.arange(DIRS).astype(jnp.float32)
    height = 1.0 - (index + 0.5) / DIRS
    radial = jnp.sqrt(1.0 - height * height)
    phase = 2.399963229728653 * index
    d_x = radial * jnp.cos(phase)
    d_y = radial * jnp.sin(phase)
    return jnp.stack(
        [
            height * height,
            2.0 * height * d_x,
            2.0 * height * d_y,
            d_x * d_x,
            2.0 * d_x * d_y,
            d_y * d_y,
        ],
        axis=1,
    )


def filtered(padded, weights, axis, count):
    total = weights[0] * lax.slice_in_dim(padded, 0, count, axis=axis)
    for shift_index in range(1, 2 * RADIUS + 1):
        total = total + weights[shift_index] * lax.slice_in_dim(
            padded, shift_index, shift_index + count, axis=axis
        )
    return total


def pooled_full(field):
    planes, rows, cells = field.shape
    return field.reshape(planes // POOL, POOL, rows // POOL, POOL, cells // POOL, POOL).sum(
        axis=(1, 3, 5)
    )


def body(volume):
    smooth, deriv = kernel_taps()
    planes, rows, cells = volume.shape
    coeffs = direction_table()
    regrouped = lax.all_to_all(volume, "slab", split_axis=2, concat_axis=0, tiled=True)
    depth = regrouped.shape[0]
    owned = regrouped.shape[2]
    padded = extended(regrouped, (("slab", 2), ("tile", 1)), RADIUS)
    zpad = jnp.pad(padded, ((RADIUS, RADIUS), (0, 0), (0, 0)))
    z_smooth = filtered(zpad, smooth, 0, depth)
    z_deriv = filtered(zpad, deriv, 0, depth)
    both_smooth = filtered(z_smooth, smooth, 1, rows)
    smooth_deriv = filtered(z_smooth, deriv, 1, rows)
    deriv_smooth = filtered(z_deriv, smooth, 1, rows)
    grad_y = filtered(both_smooth, deriv, 2, owned)
    grad_x = filtered(smooth_deriv, smooth, 2, owned)
    grad_z = filtered(deriv_smooth, smooth, 2, owned)
    tensor = jnp.stack(
        [
            pooled_full(grad_z * grad_z),
            pooled_full(grad_z * grad_x),
            pooled_full(grad_z * grad_y),
            pooled_full(grad_x * grad_x),
            pooled_full(grad_x * grad_y),
            pooled_full(grad_y * grad_y),
        ]
    )
    hist = jnp.einsum("kc,cabv->abkv", coeffs, tensor, precision=lax.Precision.HIGHEST)
    return hist / float(POOL**3)


def host_taps():
    offsets = np.arange(-RADIUS, RADIUS + 1).astype(np.float64)
    base = np.exp(-offsets * offsets / 8.0)
    slope = -offsets * base
    return base / np.sqrt(np.sum(base * base)), slope / np.sqrt(np.sum(slope * slope))


def host_directions():
    index = np.arange(DIRS).astype(np.float32)
    height = np.float32(1.0) - (index + np.float32(0.5)) / np.float32(DIRS)
    radial = np.sqrt(np.float32(1.0) - height * height)
    phase = np.float32(2.399963229728653) * index
    d_x = radial * np.cos(phase)
    d_y = radial * np.sin(phase)
    two = np.float32(2.0)
    return np.stack(
        [height * height, two * height * d_x, two * height * d_y, d_x * d_x, two * d_x * d_y, d_y * d_y],
        axis=1,
    ).astype(np.float32)


def tap_at(weights, distance):
    index = distance + RADIUS
    inside = (index >= 0) & (index <= 2 * RADIUS)
    return np.where(inside, weights[np.clip(index, 0, 2 * RADIUS)], 0.0)


def halves(matrix):
    high = matrix.astype(np.float32).astype(ml_dtypes.bfloat16)
    low = (matrix - high.astype(np.float64)).astype(np.float32).astype(ml_dtypes.bfloat16)
    return np.stack([high, low])


def y_weights(owned):
    smooth, deriv = host_taps()
    edge = np.concatenate([np.arange(-RADIUS, 0), owned + np.arange(RADIUS)])
    out = np.arange(owned)
    inner = halves(np.concatenate([tap_at(w, out[:, None] - out[None, :]) for w in (smooth, deriv)], axis=1))
    outer = halves(np.concatenate([tap_at(w, edge[:, None] - out[None, :]) for w in (smooth, deriv)], axis=1))
    ends = np.zeros((LANES, 2 * owned), ml_dtypes.bfloat16)
    for part, which in enumerate((0, 0, 1)):
        for copy in range(3):
            start = part * END_PART + copy * EDGE
            ends[start : start + EDGE] = outer[which]
    return np.concatenate([inner[0], inner[1], ends], axis=0)


def zx_weights(planes, rows):
    smooth, deriv = host_taps()
    z_out, x_out = (g.ravel()[:, None] for g in np.meshgrid(np.arange(planes), np.arange(rows), indexing="ij"))
    step = np.arange(EDGE)
    around = np.where(step < RADIUS, rows + step, step - EDGE)
    tables = []
    for places in (np.arange(rows), around):
        z_in, x_in = (g.ravel()[None, :] for g in np.meshgrid(np.arange(planes), places, indexing="ij"))
        fields = []
        for z_taps, x_taps in ((deriv, smooth), (smooth, deriv), (smooth, smooth)):
            blocks = [
                tap_at(z_taps, group * planes + z_in - z_out) * tap_at(x_taps, x_in - x_out)
                for group in (-1, 0, 1)
            ]
            fields.append(np.concatenate(blocks, axis=1))
        tables.append(halves(np.concatenate(fields, axis=0)))
    inner, outer = tables
    return inner, np.concatenate([outer[0], outer[0], outer[1]], axis=1)


def histogram_weights(rows):
    voxels = rows // POOL
    inside = (np.arange(rows)[None, :] // POOL == np.arange(voxels)[:, None]).astype(np.float32)
    table = host_directions()[None, :, :, None] * inside[:, None, None, :]
    return (table.reshape(voxels * DIRS, -1) / np.float32(POOL**3)).astype(np.float32)


def split(values):
    high = values.astype(jnp.bfloat16)
    low = (values - high.astype(jnp.float32)).astype(jnp.bfloat16)
    return high, low


def dot(a, b):
    return jnp.dot(a, b, preferred_element_type=jnp.float32)


def exact_dot(a, b):
    return jnp.dot(a, b, preferred_element_type=jnp.float32, precision=lax.Precision.HIGHEST)


def kernel(
    slabs, tiles, x_hbm, wy_hbm, wzx_hbm, wring_hbm, whist_hbm, out_ref,
    x_ref, wy_ref, wzx_ref, wring_ref, whist_ref,
    recv, halo_l, halo_r, ends_out, ends_in, ends_l, ends_r, ends_main, ends_ring,
    y_high, y_low, ring_high, ring_low, partial,
    load_sem, send_sem, recv_sem, end_send, end_recv, side_sem, fl_send, fl_recv, fr_send, fr_recv,
):
    planes, rows, cells = x_ref.shape
    owned = cells // slabs
    inner_rows = planes * rows
    ring_rows = planes * EDGE
    part = planes // CHUNKS
    s = lax.axis_index("slab")
    t = lax.axis_index("tile")
    has_left = t > 0
    has_right = t < tiles - 1

    pairs = (
        (x_hbm, x_ref), (wy_hbm, wy_ref), (wzx_hbm, wzx_ref), (wring_hbm, wring_ref),
        (whist_hbm.at[pl.ds(0, whist_ref.shape[0])], whist_ref),
    )
    loads = [pltpu.make_async_copy(src, dst, load_sem.at[i]) for i, (src, dst) in enumerate(pairs)]
    for load in loads:
        load.start()

    barrier = pltpu.get_barrier_semaphore()
    for k in range(1, slabs):
        pl.semaphore_signal(barrier, inc=1, device_id=(lax.rem(s + k, slabs), t), device_id_type=MESH)

    @pl.when(has_left)
    def _():
        pl.semaphore_signal(barrier, inc=1, device_id=(s, t - 1), device_id_type=MESH)

    @pl.when(has_right)
    def _():
        pl.semaphore_signal(barrier, inc=1, device_id=(s, t + 1), device_id_type=MESH)

    loads[0].wait()
    lane = lax.broadcasted_iota(jnp.int32, (inner_rows, LANES), 1)
    edges = jnp.zeros((inner_rows, LANES), jnp.float32)

    def side(d, first):
        if d < 0 or d >= slabs:
            return jnp.zeros((inner_rows, LANES), jnp.float32)
        return x_ref[:, :, first : first + LANES].reshape(inner_rows, LANES)

    for d in range(slabs):
        before = side(d - 1, d * owned - LANES)
        after = side(d + 1, (d + 1) * owned)
        both = jnp.where(lane >= LANES // 2, before, after)
        turned = pltpu.roll(both, d * EDGE + RADIUS, 1)
        edges = jnp.where(lane // EDGE == d, turned, edges)
    edges = edges.T
    for d in range(slabs):
        ends_out[d] = edges[d * EDGE : (d + 1) * EDGE]

    beside = jnp.where(has_left, 1, 0) + jnp.where(has_right, 1, 0)
    pl.semaphore_wait(barrier, slabs - 1 + beside)

    def ends_copy(src, dst, k):
        return pltpu.make_async_remote_copy(
            src_ref=ends_out.at[dst], dst_ref=ends_in.at[src],
            send_sem=end_send.at[k], recv_sem=end_recv.at[src],
            device_id=(dst, t), device_id_type=MESH,
        )

    def block_copy(src, dst, k, c):
        first = pl.multiple_of(dst * owned, LANES)
        return pltpu.make_async_remote_copy(
            src_ref=x_ref.at[pl.ds(c * part, part), :, pl.ds(first, owned)],
            dst_ref=recv.at[src, pl.ds(c * part, part)],
            send_sem=send_sem.at[k * CHUNKS + c], recv_sem=recv_sem.at[src * CHUNKS + c],
            device_id=(dst, t), device_id_type=MESH,
        )

    def ends_left():
        return pltpu.make_async_remote_copy(
            src_ref=ends_in, dst_ref=ends_r, send_sem=side_sem.at[0], recv_sem=side_sem.at[1],
            device_id=(s, t - 1), device_id_type=MESH,
        )

    def ends_right():
        return pltpu.make_async_remote_copy(
            src_ref=ends_in, dst_ref=ends_l, send_sem=side_sem.at[2], recv_sem=side_sem.at[3],
            device_id=(s, t + 1), device_id_type=MESH,
        )

    def to_left(p, c):
        here = pl.ds(c * part, part)
        return pltpu.make_async_remote_copy(
            src_ref=recv.at[p, here, pl.ds(0, EDGE)], dst_ref=halo_r.at[p, here],
            send_sem=fl_send.at[p * CHUNKS + c], recv_sem=fl_recv.at[p * CHUNKS + c],
            device_id=(s, t - 1), device_id_type=MESH,
        )

    def to_right(p, c):
        here = pl.ds(c * part, part)
        return pltpu.make_async_remote_copy(
            src_ref=recv.at[p, here, pl.ds(rows - EDGE, EDGE)], dst_ref=halo_l.at[p, here],
            send_sem=fr_send.at[p * CHUNKS + c], recv_sem=fr_recv.at[p * CHUNKS + c],
            device_id=(s, t + 1), device_id_type=MESH,
        )

    def forward(p, c):
        @pl.when(has_left)
        def _():
            to_left(p, c).start()

        @pl.when(has_right)
        def _():
            to_right(p, c).start()

    paired = slabs & (slabs - 1) == 0

    def peer_to(k):
        return s ^ k if paired else lax.rem(s + k, slabs)

    def peer_from(k):
        return s ^ k if paired else lax.rem(s + slabs - k, slabs)

    sends = [ends_copy(s, peer_to(k), k) for k in range(1, slabs)]
    sends += [block_copy(s, peer_to(k), k, c) for k in range(1, slabs) for c in range(CHUNKS)]
    for send in sends:
        send.start()

    recv[s] = x_ref[:, :, pl.ds(pl.multiple_of(s * owned, LANES), owned)]
    ends_in[s] = ends_out[s]
    for c in range(CHUNKS):
        forward(s, c)

    @pl.when(jnp.logical_not(has_left))
    def _():
        halo_l[...] = jnp.zeros_like(halo_l)
        ends_l[...] = jnp.zeros_like(ends_l)

    @pl.when(jnp.logical_not(has_right))
    def _():
        halo_r[...] = jnp.zeros_like(halo_r)
        ends_r[...] = jnp.zeros_like(ends_r)

    for ref, count in ((y_high, inner_rows), (y_low, inner_rows), (ring_high, ring_rows), (ring_low, ring_rows)):
        blank = jnp.zeros((count, 2 * owned), jnp.bfloat16)
        ref[0:count, :] = blank
        ref[(slabs + 1) * count : (slabs + 2) * count, :] = blank

    for k in range(1, slabs):
        p = peer_from(k)
        ends_copy(p, p, 0).wait_recv()

    @pl.when(has_left)
    def _():
        ends_left().start()

    @pl.when(has_right)
    def _():
        ends_right().start()

    @pl.when(has_left)
    def _():
        ends_right().wait_recv()

    @pl.when(has_right)
    def _():
        ends_left().wait_recv()

    def packed(ends):
        high, low = split(ends)
        high = high.astype(jnp.float32)
        low = low.astype(jnp.float32)
        all_parts = high + pltpu.roll(low, END_PART, 1) + pltpu.roll(high, 2 * END_PART, 1)
        return all_parts.astype(jnp.bfloat16)

    ring_lane = lax.broadcasted_iota(jnp.int32, (planes, EDGE, LANES), 2) // EDGE
    ring_step = lax.broadcasted_iota(jnp.int32, (planes, EDGE, LANES), 1)
    rest = jnp.zeros((LANES - 3 * EDGE, LANES), jnp.float32)
    for p in range(slabs):
        turned = jnp.concatenate([ends_in[p], ends_l[p], ends_r[p], rest], axis=0).T
        ends_main[p] = packed(jnp.where(lane < EDGE, turned, 0.0))
        turned = turned.reshape(planes, rows, LANES)
        right = jnp.where(ring_lane == 2, turned[:, 0:EDGE], 0.0)
        left = jnp.where(ring_lane == 1, turned[:, rows - EDGE : rows], 0.0)
        ring = jnp.where(ring_step < RADIUS, right, left).reshape(ring_rows, LANES)
        ends_ring[p * ring_rows : (p + 1) * ring_rows, :] = packed(ring)

    loads[1].wait()

    def along_y(block, ends):
        high, low = split(block)
        inner, finer = wy_ref[0:owned], wy_ref[owned : 2 * owned]
        result = dot(high, inner) + dot(low, inner) + dot(high, finer)
        return split(result + dot(ends, wy_ref[2 * owned : 2 * owned + LANES]))

    def inner_along_y(p):
        high, low = along_y(recv[p].reshape(inner_rows, owned), ends_main[p])
        at = pl.ds(pl.multiple_of((p + 1) * inner_rows, 16), inner_rows)
        y_high[at, :] = high
        y_low[at, :] = low

    inner_along_y(s)
    for k in range(1, slabs):
        p = peer_from(k)
        for c in range(CHUNKS):
            block_copy(p, p, 0, c).wait_recv()
            forward(p, c)
        if k == slabs - 2:
            for earlier in range(1, slabs - 1):
                inner_along_y(peer_from(earlier))
    inner_along_y(peer_from(slabs - 1))

    smooth_y = slice(0, owned)
    deriv_y = slice(owned, 2 * owned)
    pair = slice(0, 2 * inner_rows)
    last = slice(2 * inner_rows, 3 * inner_rows)
    loads[2].wait()

    def inner_group(g, carry):
        at = pl.ds(pl.multiple_of(g * inner_rows, 16), 3 * inner_rows)
        for out, field in ((pair, smooth_y), (last, deriv_y)):
            high = y_high[at, field]
            low = y_low[at, field]
            coarse = wzx_ref[0, out, :]
            partial[g, out, :] = dot(coarse, high) + dot(coarse, low) + dot(wzx_ref[1, out, :], high)
        return carry

    lax.fori_loop(0, slabs, inner_group, 0)

    for p in range(slabs):
        for c in range(CHUNKS):
            @pl.when(has_left)
            def _():
                to_right(p, c).wait_recv()

            @pl.when(has_right)
            def _():
                to_left(p, c).wait_recv()

    step = lax.broadcasted_iota(jnp.int32, (slabs, planes, EDGE, owned), 2)
    ring = jnp.where(step < RADIUS, halo_r[...], halo_l[...]).reshape(slabs * ring_rows, owned)
    high, low = along_y(ring, ends_ring[...])
    ring_high[ring_rows : (slabs + 1) * ring_rows, :] = high
    ring_low[ring_rows : (slabs + 1) * ring_rows, :] = low
    loads[3].wait()

    def group(g, sums):
        at = pl.ds(pl.multiple_of(g * ring_rows, 16), 3 * ring_rows)

        def gradient(out, field):
            high = ring_high[at, field]
            low = ring_low[at, field]
            return partial[g, out, :] + dot(wring_ref[out, :], jnp.concatenate([high, low, high], axis=0))

        both = gradient(pair, smooth_y)
        grad_z = both[:inner_rows]
        grad_x = both[inner_rows:]
        grad_y = gradient(last, deriv_y)
        products = (
            grad_z * grad_z, grad_z * grad_x, grad_z * grad_y,
            grad_x * grad_x, grad_x * grad_y, grad_y * grad_y,
        )
        return tuple(
            held + product.reshape(planes, rows, owned).sum(axis=0)
            for held, product in zip(sums, products)
        )

    blank = jnp.zeros((rows, owned), jnp.float32)
    sums = lax.fori_loop(0, slabs, group, (blank,) * 6)
    loads[4].wait()
    mixed = exact_dot(whist_ref[...], jnp.concatenate(sums, axis=0))
    cell = lax.broadcasted_iota(jnp.int32, (owned, owned // POOL), 0)
    voxel = lax.broadcasted_iota(jnp.int32, (owned, owned // POOL), 1)
    pooled = exact_dot(mixed, (cell // POOL == voxel).astype(jnp.float32))
    for b in range(rows // POOL):
        out_ref[0, b] = pooled[b * DIRS : (b + 1) * DIRS]

    for send in sends:
        send.wait_send()

    @pl.when(has_left)
    def _():
        ends_left().wait_send()
        for p in range(slabs):
            for c in range(CHUNKS):
                to_left(p, c).wait_send()

    @pl.when(has_right)
    def _():
        ends_right().wait_send()
        for p in range(slabs):
            for c in range(CHUNKS):
                to_right(p, c).wait_send()


def fused(slabs, tiles, volume):
    planes, rows, cells = volume.shape
    owned = cells // slabs
    inner_rows = planes * rows
    ring_rows = planes * EDGE
    wy = y_weights(owned)
    wzx, wring = zx_weights(planes, rows)
    whist = histogram_weights(rows)
    padded = np.zeros((1024, whist.shape[1]), np.float32)
    padded[: whist.shape[0]] = whist
    f32, bf16 = jnp.float32, jnp.bfloat16
    one = pltpu.SemaphoreType.DMA((slabs,))
    many = pltpu.SemaphoreType.DMA((slabs * CHUNKS,))
    halo = pltpu.VMEM((slabs, planes, EDGE, owned), f32)
    ends = pltpu.VMEM((slabs, EDGE, LANES), f32)
    held = pltpu.VMEM(((slabs + 2) * inner_rows, 2 * owned), bf16)
    ring = pltpu.VMEM(((slabs + 2) * ring_rows, 2 * owned), bf16)
    return pl.pallas_call(
        functools.partial(kernel, slabs, tiles),
        out_shape=jax.ShapeDtypeStruct((1, rows // POOL, DIRS, owned // POOL), f32),
        in_specs=[pl.BlockSpec(memory_space=pl.ANY)] * 5,
        out_specs=pl.BlockSpec(memory_space=pltpu.VMEM),
        scratch_shapes=[
            pltpu.VMEM(volume.shape, f32),
            pltpu.VMEM(wy.shape, bf16),
            pltpu.VMEM(wzx.shape, bf16),
            pltpu.VMEM(wring.shape, bf16),
            pltpu.VMEM(whist.shape, f32),
            pltpu.VMEM((slabs, planes, rows, owned), f32),
            halo, halo, ends, ends, ends, ends,
            pltpu.VMEM((slabs, inner_rows, LANES), bf16),
            pltpu.VMEM((slabs * ring_rows, LANES), bf16),
            held, held, ring, ring,
            pltpu.VMEM((slabs, 3 * inner_rows, owned), f32),
            pltpu.SemaphoreType.DMA((5,)),
            many, many, one, one, pltpu.SemaphoreType.DMA((4,)), many, many, many, many,
        ],
        compiler_params=pltpu.CompilerParams(collective_id=0, has_side_effects=True, vmem_limit_bytes=VMEM_LIMIT),
    )(volume, jnp.asarray(wy), jnp.asarray(wzx), jnp.asarray(wring), jnp.asarray(padded))


def fits(slabs, tiles, planes, rows, cells):
    owned = cells // slabs
    return (
        slabs * planes == POOL and planes >= RADIUS and planes * rows == LANES
        and rows % POOL == 0 and planes % CHUNKS == 0 and (planes * EDGE) % 16 == 0
        and owned % LANES == 0 and slabs * EDGE <= LANES
    )


def solution(mesh):
    slabs, tiles = mesh.shape["slab"], mesh.shape["tile"]

    def whole(volume):
        if slabs > 1 and tiles > 1 and fits(slabs, tiles, *volume.shape):
            return fused(slabs, tiles, volume)
        return body(volume)

    return jax.shard_map(
        whole,
        mesh=mesh,
        in_specs=(P("slab", "tile", None),),
        out_specs=P(None, "tile", None, "slab"),
        check_vma=False,
    )
```

```python
import functools

import jax
import jax.numpy as jnp
import ml_dtypes
import numpy as np
from jax import lax
from jax.experimental import pallas as pl
from jax.experimental.pallas import tpu as pltpu
from jax.sharding import PartitionSpec as P

RADIUS = 4
POOL = 16
DIRS = 32
MESH = pl.DeviceIdType.MESH
LANES = 128
CHUNKS = 1
EDGE = 2 * RADIUS
END_PART = 4 * EDGE


def extended(cells, sides, width):
    for axis, dim in sides:
        count = lax.axis_size(axis)
        ends = count - 1
        head = lax.slice_in_dim(cells, 0, width, axis=dim)
        tail = lax.slice_in_dim(cells, cells.shape[dim] - width, cells.shape[dim], axis=dim)
        cells = jnp.concatenate(
            [
                lax.ppermute(tail, axis, [(i, (i + 1) % count) for i in range(ends)]),
                cells,
                lax.ppermute(head, axis, [((i + 1) % count, i) for i in range(ends)]),
            ],
            axis=dim,
        )
    return cells


def kernel_taps():
    offsets = jnp.arange(-RADIUS, RADIUS + 1).astype(jnp.float32)
    base = jnp.exp(-offsets * offsets / 8.0)
    smooth = base / jnp.sqrt(jnp.sum(base * base))
    slope = -offsets * base
    deriv = slope / jnp.sqrt(jnp.sum(slope * slope))
    return (smooth, deriv)


def direction_table():
    index = jnp.arange(DIRS).astype(jnp.float32)
    height = 1.0 - (index + 0.5) / DIRS
    radial = jnp.sqrt(1.0 - height * height)
    phase = 2.399963229728653 * index
    d_x = radial * jnp.cos(phase)
    d_y = radial * jnp.sin(phase)
    return jnp.stack(
        [
            height * height,
            2.0 * height * d_x,
            2.0 * height * d_y,
            d_x * d_x,
            2.0 * d_x * d_y,
            d_y * d_y,
        ],
        axis=1,
    )


def filtered(padded, weights, axis, count):
    total = weights[0] * lax.slice_in_dim(padded, 0, count, axis=axis)
    for shift_index in range(1, 2 * RADIUS + 1):
        total = total + weights[shift_index] * lax.slice_in_dim(
            padded, shift_index, shift_index + count, axis=axis
        )
    return total


def pooled_full(field):
    planes, rows, cells = field.shape
    return field.reshape(planes // POOL, POOL, rows // POOL, POOL, cells // POOL, POOL).sum(
        axis=(1, 3, 5)
    )


def body(volume):
    smooth, deriv = kernel_taps()
    planes, rows, cells = volume.shape
    coeffs = direction_table()
    regrouped = lax.all_to_all(volume, "slab", split_axis=2, concat_axis=0, tiled=True)
    depth = regrouped.shape[0]
    owned = regrouped.shape[2]
    padded = extended(regrouped, (("slab", 2), ("tile", 1)), RADIUS)
    zpad = jnp.pad(padded, ((RADIUS, RADIUS), (0, 0), (0, 0)))
    z_smooth = filtered(zpad, smooth, 0, depth)
    z_deriv = filtered(zpad, deriv, 0, depth)
    both_smooth = filtered(z_smooth, smooth, 1, rows)
    smooth_deriv = filtered(z_smooth, deriv, 1, rows)
    deriv_smooth = filtered(z_deriv, smooth, 1, rows)
    grad_y = filtered(both_smooth, deriv, 2, owned)
    grad_x = filtered(smooth_deriv, smooth, 2, owned)
    grad_z = filtered(deriv_smooth, smooth, 2, owned)
    tensor = jnp.stack(
        [
            pooled_full(grad_z * grad_z),
            pooled_full(grad_z * grad_x),
            pooled_full(grad_z * grad_y),
            pooled_full(grad_x * grad_x),
            pooled_full(grad_x * grad_y),
            pooled_full(grad_y * grad_y),
        ]
    )
    hist = jnp.einsum("kc,cabv->abkv", coeffs, tensor, precision=lax.Precision.HIGHEST)
    return hist / float(POOL**3)


def host_taps():
    offsets = np.arange(-RADIUS, RADIUS + 1).astype(np.float64)
    base = np.exp(-offsets * offsets / 8.0)
    slope = -offsets * base
    return base / np.sqrt(np.sum(base * base)), slope / np.sqrt(np.sum(slope * slope))


def host_directions():
    index = np.arange(DIRS).astype(np.float32)
    height = np.float32(1.0) - (index + np.float32(0.5)) / np.float32(DIRS)
    radial = np.sqrt(np.float32(1.0) - height * height)
    phase = np.float32(2.399963229728653) * index
    d_x = radial * np.cos(phase)
    d_y = radial * np.sin(phase)
    two = np.float32(2.0)
    return np.stack(
        [height * height, two * height * d_x, two * height * d_y, d_x * d_x, two * d_x * d_y, d_y * d_y],
        axis=1,
    ).astype(np.float32)


def tap_at(weights, distance):
    index = distance + RADIUS
    inside = (index >= 0) & (index <= 2 * RADIUS)
    return np.where(inside, weights[np.clip(index, 0, 2 * RADIUS)], 0.0)


def halves(matrix):
    high = matrix.astype(np.float32).astype(ml_dtypes.bfloat16)
    low = (matrix - high.astype(np.float64)).astype(np.float32).astype(ml_dtypes.bfloat16)
    return np.stack([high, low])


def y_weights(owned):
    smooth, deriv = host_taps()
    edge = np.concatenate([np.arange(-RADIUS, 0), owned + np.arange(RADIUS)])
    out = np.arange(owned)
    inner = halves(np.concatenate([tap_at(w, out[:, None] - out[None, :]) for w in (smooth, deriv)], axis=1))
    outer = halves(np.concatenate([tap_at(w, edge[:, None] - out[None, :]) for w in (smooth, deriv)], axis=1))
    ends = np.zeros((LANES, 2 * owned), ml_dtypes.bfloat16)
    for part, which in enumerate((0, 0, 1)):
        for copy in range(3):
            start = part * END_PART + copy * EDGE
            ends[start : start + EDGE] = outer[which]
    return np.concatenate([inner[0], inner[1], ends], axis=0)


def zx_weights(planes, rows):
    smooth, deriv = host_taps()
    z_out, x_out = (g.ravel()[:, None] for g in np.meshgrid(np.arange(planes), np.arange(rows), indexing="ij"))
    step = np.arange(EDGE)
    around = np.where(step < RADIUS, rows + step, step - EDGE)
    tables = []
    for places in (np.arange(rows), around):
        z_in, x_in = (g.ravel()[None, :] for g in np.meshgrid(np.arange(planes), places, indexing="ij"))
        fields = []
        for z_taps, x_taps in ((deriv, smooth), (smooth, deriv), (smooth, smooth)):
            blocks = [
                tap_at(z_taps, group * planes + z_in - z_out) * tap_at(x_taps, x_in - x_out)
                for group in (-1, 0, 1)
            ]
            fields.append(np.concatenate(blocks, axis=1))
        tables.append(halves(np.concatenate(fields, axis=0)))
    inner, outer = tables
    count = planes * rows
    shares = [
        inner[:, first:stop, i * count : (i + 1) * count]
        for first, stop in ((0, 2 * count), (2 * count, 3 * count))
        for i in range(3)
    ]
    shares = np.concatenate(shares, axis=1)
    inner = np.concatenate([shares[0], shares[0], shares[1]], axis=1)
    return inner, np.concatenate([outer[0], outer[0], outer[1]], axis=1)


def histogram_weights(rows):
    voxels = rows // POOL
    inside = (np.arange(rows)[None, :] // POOL == np.arange(voxels)[:, None]).astype(np.float32)
    table = host_directions()[None, :, :, None] * inside[:, None, None, :]
    return (table.reshape(voxels * DIRS, -1) / np.float32(POOL**3)).astype(np.float32)


def split(values):
    high = values.astype(jnp.bfloat16)
    low = (values - high.astype(jnp.float32)).astype(jnp.bfloat16)
    return high, low


def dot(a, b):
    return jnp.dot(a, b, preferred_element_type=jnp.float32)


def exact_dot(a, b):
    return jnp.dot(a, b, preferred_element_type=jnp.float32, precision=lax.Precision.HIGHEST)


def kernel(
    slabs, tiles, x_hbm, wy_hbm, wzx_hbm, wring_hbm, whist_hbm, out_ref,
    x_ref, wy_ref, wzx_ref, wring_ref, whist_ref,
    recv, halo_l, halo_r, ends_out, ends_in, ends_l, ends_r, ends_main, ends_ring,
    ring_high, ring_low, partial,
    load_sem, send_sem, recv_sem, end_send, end_recv, side_sem, fl_send, fl_recv, fr_send, fr_recv,
):
    planes, rows, cells = x_ref.shape
    owned = cells // slabs
    inner_rows = planes * rows
    ring_rows = planes * EDGE
    part = planes // CHUNKS
    s = lax.axis_index("slab")
    t = lax.axis_index("tile")
    has_left = t > 0
    has_right = t < tiles - 1

    pairs = (
        (x_hbm, x_ref), (wy_hbm, wy_ref), (wzx_hbm, wzx_ref), (wring_hbm, wring_ref),
        (whist_hbm, whist_ref),
    )
    loads = [pltpu.make_async_copy(src, dst, load_sem.at[i]) for i, (src, dst) in enumerate(pairs)]
    for load in loads:
        load.start()

    barrier = pltpu.get_barrier_semaphore()
    for k in range(1, slabs):
        pl.semaphore_signal(barrier, inc=1, device_id=(lax.rem(s + k, slabs), t), device_id_type=MESH)

    @pl.when(has_left)
    def _():
        pl.semaphore_signal(barrier, inc=1, device_id=(s, t - 1), device_id_type=MESH)

    @pl.when(has_right)
    def _():
        pl.semaphore_signal(barrier, inc=1, device_id=(s, t + 1), device_id_type=MESH)

    loads[0].wait()
    lane = lax.broadcasted_iota(jnp.int32, (inner_rows, LANES), 1)
    edges = jnp.zeros((inner_rows, LANES), jnp.float32)

    def side(d, first):
        if d < 0 or d >= slabs:
            return jnp.zeros((inner_rows, LANES), jnp.float32)
        return x_ref[:, :, first : first + LANES].reshape(inner_rows, LANES)

    for d in range(slabs):
        before = side(d - 1, d * owned - LANES)
        after = side(d + 1, (d + 1) * owned)
        both = jnp.where(lane >= LANES // 2, before, after)
        turned = pltpu.roll(both, d * EDGE + RADIUS, 1)
        edges = jnp.where(lane // EDGE == d, turned, edges)
    edges = edges.T
    for d in range(slabs):
        ends_out[d] = edges[d * EDGE : (d + 1) * EDGE]

    beside = jnp.where(has_left, 1, 0) + jnp.where(has_right, 1, 0)
    pl.semaphore_wait(barrier, slabs - 1 + beside)

    def ends_copy(src, dst, k):
        return pltpu.make_async_remote_copy(
            src_ref=ends_out.at[dst], dst_ref=ends_in.at[src],
            send_sem=end_send.at[k], recv_sem=end_recv.at[src],
            device_id=(dst, t), device_id_type=MESH,
        )

    def block_copy(src, dst, k, c):
        first = pl.multiple_of(dst * owned, LANES)
        return pltpu.make_async_remote_copy(
            src_ref=x_ref.at[pl.ds(c * part, part), :, pl.ds(first, owned)],
            dst_ref=recv.at[src, pl.ds(c * part, part)],
            send_sem=send_sem.at[k * CHUNKS + c], recv_sem=recv_sem.at[src * CHUNKS + c],
            device_id=(dst, t), device_id_type=MESH,
        )

    def ends_left():
        return pltpu.make_async_remote_copy(
            src_ref=ends_in, dst_ref=ends_r, send_sem=side_sem.at[0], recv_sem=side_sem.at[1],
            device_id=(s, t - 1), device_id_type=MESH,
        )

    def ends_right():
        return pltpu.make_async_remote_copy(
            src_ref=ends_in, dst_ref=ends_l, send_sem=side_sem.at[2], recv_sem=side_sem.at[3],
            device_id=(s, t + 1), device_id_type=MESH,
        )

    def to_left(p, c):
        here = pl.ds(c * part, part)
        return pltpu.make_async_remote_copy(
            src_ref=recv.at[p, here, pl.ds(0, EDGE)], dst_ref=halo_r.at[p, here],
            send_sem=fl_send.at[p * CHUNKS + c], recv_sem=fl_recv.at[p * CHUNKS + c],
            device_id=(s, t - 1), device_id_type=MESH,
        )

    def to_right(p, c):
        here = pl.ds(c * part, part)
        return pltpu.make_async_remote_copy(
            src_ref=recv.at[p, here, pl.ds(rows - EDGE, EDGE)], dst_ref=halo_l.at[p, here],
            send_sem=fr_send.at[p * CHUNKS + c], recv_sem=fr_recv.at[p * CHUNKS + c],
            device_id=(s, t + 1), device_id_type=MESH,
        )

    def forward(p, c):
        @pl.when(has_left)
        def _():
            to_left(p, c).start()

        @pl.when(has_right)
        def _():
            to_right(p, c).start()

    paired = slabs & (slabs - 1) == 0

    def peer_to(k):
        return s ^ k if paired else lax.rem(s + k, slabs)

    def peer_from(k):
        return s ^ k if paired else lax.rem(s + slabs - k, slabs)

    sends = [ends_copy(s, peer_to(k), k) for k in range(1, slabs)]
    sends += [block_copy(s, peer_to(k), k, c) for k in range(1, slabs) for c in range(CHUNKS)]
    for send in sends[: -CHUNKS]:
        send.start()

    recv[s] = x_ref[:, :, pl.ds(pl.multiple_of(s * owned, LANES), owned)]
    ends_in[s] = ends_out[s]
    for c in range(CHUNKS):
        forward(s, c)

    @pl.when(jnp.logical_not(has_left))
    def _():
        halo_l[...] = jnp.zeros_like(halo_l)
        ends_l[...] = jnp.zeros_like(ends_l)

    @pl.when(jnp.logical_not(has_right))
    def _():
        halo_r[...] = jnp.zeros_like(halo_r)
        ends_r[...] = jnp.zeros_like(ends_r)

    partial[...] = jnp.zeros_like(partial)
    for ref, count in ((ring_high, ring_rows), (ring_low, ring_rows)):
        blank = jnp.zeros((count, 2 * owned), jnp.bfloat16)
        ref[0:count, :] = blank
        ref[(slabs + 1) * count : (slabs + 2) * count, :] = blank

    for k in range(1, slabs):
        p = peer_from(k)
        ends_copy(p, p, 0).wait_recv()

    @pl.when(has_left)
    def _():
        ends_left().start()

    @pl.when(has_right)
    def _():
        ends_right().start()

    @pl.when(has_left)
    def _():
        ends_right().wait_recv()

    @pl.when(has_right)
    def _():
        ends_left().wait_recv()

    def packed(ends):
        high, low = split(ends)
        high = high.astype(jnp.float32)
        low = low.astype(jnp.float32)
        all_parts = high + pltpu.roll(low, END_PART, 1) + pltpu.roll(high, 2 * END_PART, 1)
        return all_parts.astype(jnp.bfloat16)

    ring_lane = lax.broadcasted_iota(jnp.int32, (planes, EDGE, LANES), 2) // EDGE
    ring_step = lax.broadcasted_iota(jnp.int32, (planes, EDGE, LANES), 1)
    rest = jnp.zeros((LANES - 3 * EDGE, LANES), jnp.float32)
    for p in range(slabs):
        turned = jnp.concatenate([ends_in[p], ends_l[p], ends_r[p], rest], axis=0).T
        ends_main[p] = packed(jnp.where(lane < EDGE, turned, 0.0))
        turned = turned.reshape(planes, rows, LANES)
        right = jnp.where(ring_lane == 2, turned[:, 0:EDGE], 0.0)
        left = jnp.where(ring_lane == 1, turned[:, rows - EDGE : rows], 0.0)
        ring = jnp.where(ring_step < RADIUS, right, left).reshape(ring_rows, LANES)
        ends_ring[p * ring_rows : (p + 1) * ring_rows, :] = packed(ring)

    for send in sends[: -CHUNKS]:
        send.wait_send()
    for send in sends[-CHUNKS:]:
        send.start()
    loads[1].wait()
    loads[2].wait()
    smooth_y = slice(0, owned)
    deriv_y = slice(owned, 2 * owned)
    pair = slice(0, 2 * inner_rows)
    last = slice(2 * inner_rows, 3 * inner_rows)

    def along_y(block, ends):
        high, low = split(block)
        inner, finer = wy_ref[0:owned], wy_ref[owned : 2 * owned]
        result = dot(high, inner) + dot(low, inner) + dot(high, finer)
        return split(result + dot(ends, wy_ref[2 * owned : 2 * owned + LANES]))

    def inner_along_y(p):
        high, low = along_y(recv[p].reshape(inner_rows, owned), ends_main[p])
        parts = jnp.concatenate([high, low, high], axis=0)
        for out, first, field in ((pair, 0, smooth_y), (last, 6 * inner_rows, deriv_y)):
            count = out.stop - out.start
            share = dot(wzx_ref[first : first + 3 * count, :], parts[:, field])
            for i in range(3):
                partial[p + 2 - i, out, :] += share[i * count : (i + 1) * count]

    inner_along_y(s)
    for k in range(1, slabs):
        p = peer_from(k)
        for c in range(CHUNKS):
            block_copy(p, p, 0, c).wait_recv()
            forward(p, c)
        if k == slabs - 2:
            for earlier in range(1, slabs - 1):
                inner_along_y(peer_from(earlier))
    inner_along_y(peer_from(slabs - 1))

    for p in range(slabs):
        for c in range(CHUNKS):
            @pl.when(has_left)
            def _():
                to_right(p, c).wait_recv()

            @pl.when(has_right)
            def _():
                to_left(p, c).wait_recv()

    step = lax.broadcasted_iota(jnp.int32, (slabs, planes, EDGE, owned), 2)
    ring = jnp.where(step < RADIUS, halo_r[...], halo_l[...]).reshape(slabs * ring_rows, owned)
    high, low = along_y(ring, ends_ring[...])
    ring_high[ring_rows : (slabs + 1) * ring_rows, :] = high
    ring_low[ring_rows : (slabs + 1) * ring_rows, :] = low
    loads[3].wait()

    def group(g, sums):
        at = pl.ds(pl.multiple_of(g * ring_rows, 16), 3 * ring_rows)

        def gradient(out, field):
            high = ring_high[at, field]
            low = ring_low[at, field]
            return partial[g + 1, out, :] + dot(wring_ref[out, :], jnp.concatenate([high, low, high], axis=0))

        both = gradient(pair, smooth_y)
        grad_z = both[:inner_rows]
        grad_x = both[inner_rows:]
        grad_y = gradient(last, deriv_y)
        products = (
            grad_z * grad_z, grad_z * grad_x, grad_z * grad_y,
            grad_x * grad_x, grad_x * grad_y, grad_y * grad_y,
        )
        return tuple(
            held + product.reshape(planes, rows, owned).sum(axis=0)
            for held, product in zip(sums, products)
        )

    blank = jnp.zeros((rows, owned), jnp.float32)
    sums = lax.fori_loop(0, slabs, group, (blank,) * 6)
    loads[4].wait()
    mixed = exact_dot(whist_ref[...], jnp.concatenate(sums, axis=0))
    cell = lax.broadcasted_iota(jnp.int32, (owned, owned // POOL), 0)
    voxel = lax.broadcasted_iota(jnp.int32, (owned, owned // POOL), 1)
    pooled = exact_dot(mixed, (cell // POOL == voxel).astype(jnp.float32))
    for b in range(rows // POOL):
        out_ref[0, b] = pooled[b * DIRS : (b + 1) * DIRS]

    for send in sends[-CHUNKS:]:
        send.wait_send()

    @pl.when(has_left)
    def _():
        ends_left().wait_send()
        for p in range(slabs):
            for c in range(CHUNKS):
                to_left(p, c).wait_send()

    @pl.when(has_right)
    def _():
        ends_right().wait_send()
        for p in range(slabs):
            for c in range(CHUNKS):
                to_right(p, c).wait_send()


def fused(slabs, tiles, volume):
    planes, rows, cells = volume.shape
    owned = cells // slabs
    inner_rows = planes * rows
    ring_rows = planes * EDGE
    wy = y_weights(owned)
    wzx, wring = zx_weights(planes, rows)
    whist = histogram_weights(rows)
    f32, bf16 = jnp.float32, jnp.bfloat16
    one = pltpu.SemaphoreType.DMA((slabs,))
    many = pltpu.SemaphoreType.DMA((slabs * CHUNKS,))
    halo = pltpu.VMEM((slabs, planes, EDGE, owned), f32)
    ends = pltpu.VMEM((slabs, EDGE, LANES), f32)
    ring = pltpu.VMEM(((slabs + 2) * ring_rows, 2 * owned), bf16)
    return pl.pallas_call(
        functools.partial(kernel, slabs, tiles),
        out_shape=jax.ShapeDtypeStruct((1, rows // POOL, DIRS, owned // POOL), f32),
        in_specs=[pl.BlockSpec(memory_space=pl.ANY)] * 5,
        out_specs=pl.BlockSpec(memory_space=pltpu.VMEM),
        scratch_shapes=[
            pltpu.VMEM(volume.shape, f32),
            pltpu.VMEM(wy.shape, bf16),
            pltpu.VMEM(wzx.shape, bf16),
            pltpu.VMEM(wring.shape, bf16),
            pltpu.VMEM(whist.shape, f32),
            pltpu.VMEM((slabs, planes, rows, owned), f32),
            halo, halo, ends, ends, ends, ends,
            pltpu.VMEM((slabs, inner_rows, LANES), bf16),
            pltpu.VMEM((slabs * ring_rows, LANES), bf16),
            ring, ring,
            pltpu.VMEM((slabs + 2, 3 * inner_rows, owned), f32),
            pltpu.SemaphoreType.DMA((5,)),
            many, many, one, one, pltpu.SemaphoreType.DMA((4,)), many, many, many, many,
        ],
        compiler_params=pltpu.CompilerParams(collective_id=0, has_side_effects=True),
    )(volume, jnp.asarray(wy), jnp.asarray(wzx), jnp.asarray(wring), jnp.asarray(whist))


def fits(slabs, tiles, planes, rows, cells):
    owned = cells // slabs
    return (
        slabs * planes == POOL and planes >= RADIUS and planes * rows == LANES
        and rows % POOL == 0 and planes % CHUNKS == 0 and (planes * EDGE) % 16 == 0
        and owned % LANES == 0 and slabs * EDGE <= LANES
    )


def solution(mesh):
    slabs, tiles = mesh.shape["slab"], mesh.shape["tile"]

    def whole(volume):
        if slabs > 1 and tiles > 1 and fits(slabs, tiles, *volume.shape):
            return fused(slabs, tiles, volume)
        return body(volume)

    return jax.shard_map(
        whole,
        mesh=mesh,
        in_specs=(P("slab", "tile", None),),
        out_specs=P(None, "tile", None, "slab"),
        check_vma=False,
    )
```

```python
import functools

import jax
import jax.numpy as jnp
import ml_dtypes
import numpy as np
from jax import lax
from jax.experimental import pallas as pl
from jax.experimental.pallas import tpu as pltpu
from jax.sharding import PartitionSpec as P

RADIUS = 4
POOL = 16
DIRS = 32
MESH = pl.DeviceIdType.MESH
LANES = 128
CHUNKS = 2
VMEM_LIMIT = 64 * 2**20 - 480 * 2**10
TALL = 1024
EDGE = 2 * RADIUS
END_PART = 4 * EDGE


def extended(cells, sides, width):
    for axis, dim in sides:
        count = lax.axis_size(axis)
        ends = count - 1
        head = lax.slice_in_dim(cells, 0, width, axis=dim)
        tail = lax.slice_in_dim(cells, cells.shape[dim] - width, cells.shape[dim], axis=dim)
        cells = jnp.concatenate(
            [
                lax.ppermute(tail, axis, [(i, (i + 1) % count) for i in range(ends)]),
                cells,
                lax.ppermute(head, axis, [((i + 1) % count, i) for i in range(ends)]),
            ],
            axis=dim,
        )
    return cells


def kernel_taps():
    offsets = jnp.arange(-RADIUS, RADIUS + 1).astype(jnp.float32)
    base = jnp.exp(-offsets * offsets / 8.0)
    smooth = base / jnp.sqrt(jnp.sum(base * base))
    slope = -offsets * base
    deriv = slope / jnp.sqrt(jnp.sum(slope * slope))
    return (smooth, deriv)


def direction_table():
    index = jnp.arange(DIRS).astype(jnp.float32)
    height = 1.0 - (index + 0.5) / DIRS
    radial = jnp.sqrt(1.0 - height * height)
    phase = 2.399963229728653 * index
    d_x = radial * jnp.cos(phase)
    d_y = radial * jnp.sin(phase)
    return jnp.stack(
        [
            height * height,
            2.0 * height * d_x,
            2.0 * height * d_y,
            d_x * d_x,
            2.0 * d_x * d_y,
            d_y * d_y,
        ],
        axis=1,
    )


def filtered(padded, weights, axis, count):
    total = weights[0] * lax.slice_in_dim(padded, 0, count, axis=axis)
    for shift_index in range(1, 2 * RADIUS + 1):
        total = total + weights[shift_index] * lax.slice_in_dim(
            padded, shift_index, shift_index + count, axis=axis
        )
    return total


def pooled_full(field):
    planes, rows, cells = field.shape
    return field.reshape(planes // POOL, POOL, rows // POOL, POOL, cells // POOL, POOL).sum(
        axis=(1, 3, 5)
    )


def body(volume):
    smooth, deriv = kernel_taps()
    planes, rows, cells = volume.shape
    coeffs = direction_table()
    regrouped = lax.all_to_all(volume, "slab", split_axis=2, concat_axis=0, tiled=True)
    depth = regrouped.shape[0]
    owned = regrouped.shape[2]
    padded = extended(regrouped, (("slab", 2), ("tile", 1)), RADIUS)
    zpad = jnp.pad(padded, ((RADIUS, RADIUS), (0, 0), (0, 0)))
    z_smooth = filtered(zpad, smooth, 0, depth)
    z_deriv = filtered(zpad, deriv, 0, depth)
    both_smooth = filtered(z_smooth, smooth, 1, rows)
    smooth_deriv = filtered(z_smooth, deriv, 1, rows)
    deriv_smooth = filtered(z_deriv, smooth, 1, rows)
    grad_y = filtered(both_smooth, deriv, 2, owned)
    grad_x = filtered(smooth_deriv, smooth, 2, owned)
    grad_z = filtered(deriv_smooth, smooth, 2, owned)
    tensor = jnp.stack(
        [
            pooled_full(grad_z * grad_z),
            pooled_full(grad_z * grad_x),
            pooled_full(grad_z * grad_y),
            pooled_full(grad_x * grad_x),
            pooled_full(grad_x * grad_y),
            pooled_full(grad_y * grad_y),
        ]
    )
    hist = jnp.einsum("kc,cabv->abkv", coeffs, tensor, precision=lax.Precision.HIGHEST)
    return hist / float(POOL**3)


def host_taps():
    offsets = np.arange(-RADIUS, RADIUS + 1).astype(np.float64)
    base = np.exp(-offsets * offsets / 8.0)
    slope = -offsets * base
    return base / np.sqrt(np.sum(base * base)), slope / np.sqrt(np.sum(slope * slope))


def host_directions():
    index = np.arange(DIRS).astype(np.float32)
    height = np.float32(1.0) - (index + np.float32(0.5)) / np.float32(DIRS)
    radial = np.sqrt(np.float32(1.0) - height * height)
    phase = np.float32(2.399963229728653) * index
    d_x = radial * np.cos(phase)
    d_y = radial * np.sin(phase)
    two = np.float32(2.0)
    return np.stack(
        [height * height, two * height * d_x, two * height * d_y, d_x * d_x, two * d_x * d_y, d_y * d_y],
        axis=1,
    ).astype(np.float32)


def tap_at(weights, distance):
    index = distance + RADIUS
    inside = (index >= 0) & (index <= 2 * RADIUS)
    return np.where(inside, weights[np.clip(index, 0, 2 * RADIUS)], 0.0)


def halves(matrix):
    high = matrix.astype(np.float32).astype(ml_dtypes.bfloat16)
    low = (matrix - high.astype(np.float64)).astype(np.float32).astype(ml_dtypes.bfloat16)
    return np.stack([high, low])


def y_weights(owned):
    smooth, deriv = host_taps()
    edge = np.concatenate([np.arange(-RADIUS, 0), owned + np.arange(RADIUS)])
    out = np.arange(owned)
    inner = halves(np.concatenate([tap_at(w, out[:, None] - out[None, :]) for w in (smooth, deriv)], axis=1))
    outer = halves(np.concatenate([tap_at(w, edge[:, None] - out[None, :]) for w in (smooth, deriv)], axis=1))
    ends = np.zeros((LANES, 2 * owned), ml_dtypes.bfloat16)
    for part, which in enumerate((0, 0, 1)):
        for copy in range(3):
            start = part * END_PART + copy * EDGE
            ends[start : start + EDGE] = outer[which]
    return np.concatenate([inner[0], inner[1], ends], axis=0)


def zx_weights(planes, rows):
    smooth, deriv = host_taps()
    z_out, x_out = (g.ravel()[:, None] for g in np.meshgrid(np.arange(planes), np.arange(rows), indexing="ij"))
    step = np.arange(EDGE)
    around = np.where(step < RADIUS, rows + step, step - EDGE)
    tables = []
    for places in (np.arange(rows), around):
        z_in, x_in = (g.ravel()[None, :] for g in np.meshgrid(np.arange(planes), places, indexing="ij"))
        fields = []
        for z_taps, x_taps in ((deriv, smooth), (smooth, deriv), (smooth, smooth)):
            blocks = [
                tap_at(z_taps, group * planes + z_in - z_out) * tap_at(x_taps, x_in - x_out)
                for group in (-1, 0, 1)
            ]
            fields.append(np.concatenate(blocks, axis=1))
        tables.append(halves(np.concatenate(fields, axis=0)))
    inner, outer = tables
    return inner, np.concatenate([outer[0], outer[0], outer[1]], axis=1)


def histogram_weights(rows):
    voxels = rows // POOL
    inside = (np.arange(rows)[None, :] // POOL == np.arange(voxels)[:, None]).astype(np.float32)
    table = host_directions()[None, :, :, None] * inside[:, None, None, :]
    return (table.reshape(voxels * DIRS, -1) / np.float32(POOL**3)).astype(np.float32)


def tall(table):
    rows = np.zeros((max(TALL, table.shape[0]), table.shape[1]), table.dtype)
    rows[: table.shape[0]] = table
    return rows


def split(values):
    high = values.astype(jnp.bfloat16)
    low = (values - high.astype(jnp.float32)).astype(jnp.bfloat16)
    return high, low


def dot(a, b):
    return jnp.dot(a, b, preferred_element_type=jnp.float32)


def exact_dot(a, b):
    return jnp.dot(a, b, preferred_element_type=jnp.float32, precision=lax.Precision.HIGHEST)


def kernel(
    slabs, tiles, x_hbm, wy_hbm, wzx_hbm, wring_hbm, whist_hbm, out_ref,
    x_ref, wy_ref, wzx_ref, wring_ref, whist_ref,
    recv, halo_l, halo_r, ends_out, ends_in, ends_l, ends_r, ends_main, ends_ring,
    y_high, y_low, ring_high, ring_low, partial,
    load_sem, send_sem, recv_sem, end_send, end_recv, side_sem, fl_send, fl_recv, fr_send, fr_recv,
):
    planes, rows, cells = x_ref.shape
    owned = cells // slabs
    inner_rows = planes * rows
    ring_rows = planes * EDGE
    part = planes // CHUNKS
    s = lax.axis_index("slab")
    t = lax.axis_index("tile")
    has_left = t > 0
    has_right = t < tiles - 1

    pairs = (
        (x_hbm, x_ref), (wy_hbm, wy_ref), (wzx_hbm, wzx_ref),
        (wring_hbm.at[pl.ds(0, wring_ref.shape[0])], wring_ref),
        (whist_hbm.at[pl.ds(0, whist_ref.shape[0])], whist_ref),
    )
    loads = [pltpu.make_async_copy(src, dst, load_sem.at[i]) for i, (src, dst) in enumerate(pairs)]
    for load in loads:
        load.start()

    barrier = pltpu.get_barrier_semaphore()
    for k in range(1, slabs):
        pl.semaphore_signal(barrier, inc=1, device_id=(lax.rem(s + k, slabs), t), device_id_type=MESH)

    @pl.when(has_left)
    def _():
        pl.semaphore_signal(barrier, inc=1, device_id=(s, t - 1), device_id_type=MESH)

    @pl.when(has_right)
    def _():
        pl.semaphore_signal(barrier, inc=1, device_id=(s, t + 1), device_id_type=MESH)

    beside = jnp.where(has_left, 1, 0) + jnp.where(has_right, 1, 0)
    pl.semaphore_wait(barrier, slabs - 1 + beside)

    def ends_copy(src, dst, k):
        return pltpu.make_async_remote_copy(
            src_ref=ends_out.at[dst], dst_ref=ends_in.at[src],
            send_sem=end_send.at[k], recv_sem=end_recv.at[src],
            device_id=(dst, t), device_id_type=MESH,
        )

    def block_copy(src, dst, k, c):
        first = pl.multiple_of(dst * owned, LANES)
        return pltpu.make_async_remote_copy(
            src_ref=x_hbm.at[pl.ds(c * part, part), :, pl.ds(first, owned)],
            dst_ref=recv.at[src, pl.ds(c * part, part)],
            send_sem=send_sem.at[k * CHUNKS + c], recv_sem=recv_sem.at[src * CHUNKS + c],
            device_id=(dst, t), device_id_type=MESH,
        )

    def ends_left():
        return pltpu.make_async_remote_copy(
            src_ref=ends_in, dst_ref=ends_r, send_sem=side_sem.at[0], recv_sem=side_sem.at[1],
            device_id=(s, t - 1), device_id_type=MESH,
        )

    def ends_right():
        return pltpu.make_async_remote_copy(
            src_ref=ends_in, dst_ref=ends_l, send_sem=side_sem.at[2], recv_sem=side_sem.at[3],
            device_id=(s, t + 1), device_id_type=MESH,
        )

    def to_left(p, c):
        here = pl.ds(c * part, part)
        return pltpu.make_async_remote_copy(
            src_ref=recv.at[p, here, pl.ds(0, EDGE)], dst_ref=halo_r.at[p, here],
            send_sem=fl_send.at[p * CHUNKS + c], recv_sem=fl_recv.at[p * CHUNKS + c],
            device_id=(s, t - 1), device_id_type=MESH,
        )

    def to_right(p, c):
        here = pl.ds(c * part, part)
        return pltpu.make_async_remote_copy(
            src_ref=recv.at[p, here, pl.ds(rows - EDGE, EDGE)], dst_ref=halo_l.at[p, here],
            send_sem=fr_send.at[p * CHUNKS + c], recv_sem=fr_recv.at[p * CHUNKS + c],
            device_id=(s, t + 1), device_id_type=MESH,
        )

    def forward(p, c):
        @pl.when(has_left)
        def _():
            to_left(p, c).start()

        @pl.when(has_right)
        def _():
            to_right(p, c).start()

    sends = [block_copy(s, lax.rem(s + k, slabs), k, c) for c in range(CHUNKS) for k in range(1, slabs)]
    for send in sends[: slabs - 1]:
        send.start()

    loads[0].wait()
    lane = lax.broadcasted_iota(jnp.int32, (inner_rows, LANES), 1)
    edges = jnp.zeros((inner_rows, LANES), jnp.float32)

    def side(d, first):
        if d < 0 or d >= slabs:
            return jnp.zeros((inner_rows, LANES), jnp.float32)
        return x_ref[:, :, first : first + LANES].reshape(inner_rows, LANES)

    for d in range(slabs):
        before = side(d - 1, d * owned - LANES)
        after = side(d + 1, (d + 1) * owned)
        both = jnp.where(lane >= LANES // 2, before, after)
        turned = pltpu.roll(both, d * EDGE + RADIUS, 1)
        edges = jnp.where(lane // EDGE == d, turned, edges)
    edges = edges.T
    for d in range(slabs):
        ends_out[d] = edges[d * EDGE : (d + 1) * EDGE]

    others = [ends_copy(s, lax.rem(s + k, slabs), k) for k in range(1, slabs)]
    for send in others + sends[slabs - 1 :]:
        send.start()
    sends += others

    recv[s] = x_ref[:, :, pl.ds(pl.multiple_of(s * owned, LANES), owned)]
    ends_in[s] = ends_out[s]
    for c in range(CHUNKS):
        forward(s, c)

    @pl.when(jnp.logical_not(has_left))
    def _():
        halo_l[...] = jnp.zeros_like(halo_l)
        ends_l[...] = jnp.zeros_like(ends_l)

    @pl.when(jnp.logical_not(has_right))
    def _():
        halo_r[...] = jnp.zeros_like(halo_r)
        ends_r[...] = jnp.zeros_like(ends_r)

    for ref, count in ((y_high, inner_rows), (y_low, inner_rows), (ring_high, ring_rows), (ring_low, ring_rows)):
        blank = jnp.zeros((count, 2 * owned), jnp.bfloat16)
        ref[0:count, :] = blank
        ref[(slabs + 1) * count : (slabs + 2) * count, :] = blank

    for k in range(1, slabs):
        p = lax.rem(s + slabs - k, slabs)
        ends_copy(p, p, 0).wait_recv()

    @pl.when(has_left)
    def _():
        ends_left().start()

    @pl.when(has_right)
    def _():
        ends_right().start()

    @pl.when(has_left)
    def _():
        ends_right().wait_recv()

    @pl.when(has_right)
    def _():
        ends_left().wait_recv()

    def packed(ends):
        high, low = split(ends)
        high = high.astype(jnp.float32)
        low = low.astype(jnp.float32)
        all_parts = high + pltpu.roll(low, END_PART, 1) + pltpu.roll(high, 2 * END_PART, 1)
        return all_parts.astype(jnp.bfloat16)

    ring_lane = lax.broadcasted_iota(jnp.int32, (planes, EDGE, LANES), 2) // EDGE
    ring_step = lax.broadcasted_iota(jnp.int32, (planes, EDGE, LANES), 1)
    rest = jnp.zeros((LANES - 3 * EDGE, LANES), jnp.float32)
    for p in range(slabs):
        turned = jnp.concatenate([ends_in[p], ends_l[p], ends_r[p], rest], axis=0).T
        ends_main[p] = packed(jnp.where(lane < EDGE, turned, 0.0))
        turned = turned.reshape(planes, rows, LANES)
        right = jnp.where(ring_lane == 2, turned[:, 0:EDGE], 0.0)
        left = jnp.where(ring_lane == 1, turned[:, rows - EDGE : rows], 0.0)
        ring = jnp.where(ring_step < RADIUS, right, left).reshape(ring_rows, LANES)
        ends_ring[p * ring_rows : (p + 1) * ring_rows, :] = packed(ring)

    loads[1].wait()

    def along_y(block, ends):
        high, low = split(block)
        inner, finer = wy_ref[0:owned], wy_ref[owned : 2 * owned]
        result = dot(high, inner) + dot(low, inner) + dot(high, finer)
        return split(result + dot(ends, wy_ref[2 * owned : 2 * owned + LANES]))

    def inner_along_y(p):
        high, low = along_y(recv[p].reshape(inner_rows, owned), ends_main[p])
        at = pl.ds(pl.multiple_of((p + 1) * inner_rows, 16), inner_rows)
        y_high[at, :] = high
        y_low[at, :] = low

    inner_along_y(s)
    for c in range(CHUNKS):
        for k in range(1, slabs):
            p = lax.rem(s + slabs - k, slabs)
            block_copy(p, p, 0, c).wait_recv()
            forward(p, c)
    for k in range(1, slabs):
        inner_along_y(lax.rem(s + slabs - k, slabs))

    smooth_y = slice(0, owned)
    deriv_y = slice(owned, 2 * owned)
    pair = slice(0, 2 * inner_rows)
    last = slice(2 * inner_rows, 3 * inner_rows)
    loads[2].wait()

    def inner_group(g, carry):
        at = pl.ds(pl.multiple_of(g * inner_rows, 16), 3 * inner_rows)
        for out, field in ((pair, smooth_y), (last, deriv_y)):
            high = y_high[at, field]
            low = y_low[at, field]
            coarse = wzx_ref[0, out, :]
            partial[g, out, :] = dot(coarse, high) + dot(coarse, low) + dot(wzx_ref[1, out, :], high)
        return carry

    lax.fori_loop(0, slabs, inner_group, 0)

    for p in range(slabs):
        for c in range(CHUNKS):
            @pl.when(has_left)
            def _():
                to_right(p, c).wait_recv()

            @pl.when(has_right)
            def _():
                to_left(p, c).wait_recv()

    step = lax.broadcasted_iota(jnp.int32, (slabs, planes, EDGE, owned), 2)
    ring = jnp.where(step < RADIUS, halo_r[...], halo_l[...]).reshape(slabs * ring_rows, owned)
    high, low = along_y(ring, ends_ring[...])
    ring_high[ring_rows : (slabs + 1) * ring_rows, :] = high
    ring_low[ring_rows : (slabs + 1) * ring_rows, :] = low
    loads[3].wait()

    def group(g, sums):
        at = pl.ds(pl.multiple_of(g * ring_rows, 16), 3 * ring_rows)

        def gradient(out, field):
            high = ring_high[at, field]
            low = ring_low[at, field]
            return partial[g, out, :] + dot(wring_ref[out, :], jnp.concatenate([high, low, high], axis=0))

        both = gradient(pair, smooth_y)
        grad_z = both[:inner_rows]
        grad_x = both[inner_rows:]
        grad_y = gradient(last, deriv_y)
        products = (
            grad_z * grad_z, grad_z * grad_x, grad_z * grad_y,
            grad_x * grad_x, grad_x * grad_y, grad_y * grad_y,
        )
        return tuple(
            held + product.reshape(planes, rows, owned).sum(axis=0)
            for held, product in zip(sums, products)
        )

    blank = jnp.zeros((rows, owned), jnp.float32)
    sums = lax.fori_loop(0, slabs, group, (blank,) * 6)
    loads[4].wait()
    mixed = exact_dot(whist_ref[...], jnp.concatenate(sums, axis=0))
    cell = lax.broadcasted_iota(jnp.int32, (owned, owned // POOL), 0)
    voxel = lax.broadcasted_iota(jnp.int32, (owned, owned // POOL), 1)
    pooled = exact_dot(mixed, (cell // POOL == voxel).astype(jnp.float32))
    for b in range(rows // POOL):
        out_ref[0, b] = pooled[b * DIRS : (b + 1) * DIRS]

    for send in sends:
        send.wait_send()

    @pl.when(has_left)
    def _():
        ends_left().wait_send()
        for p in range(slabs):
            for c in range(CHUNKS):
                to_left(p, c).wait_send()

    @pl.when(has_right)
    def _():
        ends_right().wait_send()
        for p in range(slabs):
            for c in range(CHUNKS):
                to_right(p, c).wait_send()


def fused(slabs, tiles, volume):
    planes, rows, cells = volume.shape
    owned = cells // slabs
    inner_rows = planes * rows
    ring_rows = planes * EDGE
    wy = y_weights(owned)
    wzx, wring = zx_weights(planes, rows)
    whist = histogram_weights(rows)
    f32, bf16 = jnp.float32, jnp.bfloat16
    one = pltpu.SemaphoreType.DMA((slabs,))
    many = pltpu.SemaphoreType.DMA((slabs * CHUNKS,))
    halo = pltpu.VMEM((slabs, planes, EDGE, owned), f32)
    ends = pltpu.VMEM((slabs, EDGE, LANES), f32)
    held = pltpu.VMEM(((slabs + 2) * inner_rows, 2 * owned), bf16)
    ring = pltpu.VMEM(((slabs + 2) * ring_rows, 2 * owned), bf16)
    return pl.pallas_call(
        functools.partial(kernel, slabs, tiles),
        out_shape=jax.ShapeDtypeStruct((1, rows // POOL, DIRS, owned // POOL), f32),
        in_specs=[pl.BlockSpec(memory_space=pl.ANY)] * 5,
        out_specs=pl.BlockSpec(memory_space=pltpu.VMEM),
        scratch_shapes=[
            pltpu.VMEM(volume.shape, f32),
            pltpu.VMEM(wy.shape, bf16),
            pltpu.VMEM(wzx.shape, bf16),
            pltpu.VMEM(wring.shape, bf16),
            pltpu.VMEM(whist.shape, f32),
            pltpu.VMEM((slabs, planes, rows, owned), f32),
            halo, halo, ends, ends, ends, ends,
            pltpu.VMEM((slabs, inner_rows, LANES), bf16),
            pltpu.VMEM((slabs * ring_rows, LANES), bf16),
            held, held, ring, ring,
            pltpu.VMEM((slabs, 3 * inner_rows, owned), f32),
            pltpu.SemaphoreType.DMA((5,)),
            many, many, one, one, pltpu.SemaphoreType.DMA((4,)), many, many, many, many,
        ],
        compiler_params=pltpu.CompilerParams(collective_id=0, has_side_effects=True, vmem_limit_bytes=VMEM_LIMIT),
    )(volume, jnp.asarray(wy), jnp.asarray(wzx), jnp.asarray(tall(wring)), jnp.asarray(tall(whist)))


def fits(slabs, tiles, planes, rows, cells):
    owned = cells // slabs
    return (
        slabs * planes == POOL and planes >= RADIUS and planes * rows == LANES
        and rows % POOL == 0 and planes % CHUNKS == 0 and (planes * EDGE) % 16 == 0
        and owned % LANES == 0 and slabs * EDGE <= LANES
    )


def solution(mesh):
    slabs, tiles = mesh.shape["slab"], mesh.shape["tile"]

    def whole(volume):
        if slabs > 1 and tiles > 1 and fits(slabs, tiles, *volume.shape):
            return fused(slabs, tiles, volume)
        return body(volume)

    return jax.shard_map(
        whole,
        mesh=mesh,
        in_specs=(P("slab", "tile", None),),
        out_specs=P(None, "tile", None, "slab"),
        check_vma=False,
    )
```

```python
import functools

import jax
import jax.numpy as jnp
import ml_dtypes
import numpy as np
from jax import lax
from jax.experimental import pallas as pl
from jax.experimental.pallas import tpu as pltpu
from jax.sharding import PartitionSpec as P

RADIUS = 4
POOL = 16
DIRS = 32
MESH = pl.DeviceIdType.MESH
LANES = 128
CHUNKS = 2
EDGE = 2 * RADIUS
END_PART = 4 * EDGE


def extended(cells, sides, width):
    for axis, dim in sides:
        count = lax.axis_size(axis)
        ends = count - 1
        head = lax.slice_in_dim(cells, 0, width, axis=dim)
        tail = lax.slice_in_dim(cells, cells.shape[dim] - width, cells.shape[dim], axis=dim)
        cells = jnp.concatenate(
            [
                lax.ppermute(tail, axis, [(i, (i + 1) % count) for i in range(ends)]),
                cells,
                lax.ppermute(head, axis, [((i + 1) % count, i) for i in range(ends)]),
            ],
            axis=dim,
        )
    return cells


def kernel_taps():
    offsets = jnp.arange(-RADIUS, RADIUS + 1).astype(jnp.float32)
    base = jnp.exp(-offsets * offsets / 8.0)
    smooth = base / jnp.sqrt(jnp.sum(base * base))
    slope = -offsets * base
    deriv = slope / jnp.sqrt(jnp.sum(slope * slope))
    return (smooth, deriv)


def direction_table():
    index = jnp.arange(DIRS).astype(jnp.float32)
    height = 1.0 - (index + 0.5) / DIRS
    radial = jnp.sqrt(1.0 - height * height)
    phase = 2.399963229728653 * index
    d_x = radial * jnp.cos(phase)
    d_y = radial * jnp.sin(phase)
    return jnp.stack(
        [
            height * height,
            2.0 * height * d_x,
            2.0 * height * d_y,
            d_x * d_x,
            2.0 * d_x * d_y,
            d_y * d_y,
        ],
        axis=1,
    )


def filtered(padded, weights, axis, count):
    total = weights[0] * lax.slice_in_dim(padded, 0, count, axis=axis)
    for shift_index in range(1, 2 * RADIUS + 1):
        total = total + weights[shift_index] * lax.slice_in_dim(
            padded, shift_index, shift_index + count, axis=axis
        )
    return total


def pooled_full(field):
    planes, rows, cells = field.shape
    return field.reshape(planes // POOL, POOL, rows // POOL, POOL, cells // POOL, POOL).sum(
        axis=(1, 3, 5)
    )


def body(volume):
    smooth, deriv = kernel_taps()
    planes, rows, cells = volume.shape
    coeffs = direction_table()
    regrouped = lax.all_to_all(volume, "slab", split_axis=2, concat_axis=0, tiled=True)
    depth = regrouped.shape[0]
    owned = regrouped.shape[2]
    padded = extended(regrouped, (("slab", 2), ("tile", 1)), RADIUS)
    zpad = jnp.pad(padded, ((RADIUS, RADIUS), (0, 0), (0, 0)))
    z_smooth = filtered(zpad, smooth, 0, depth)
    z_deriv = filtered(zpad, deriv, 0, depth)
    both_smooth = filtered(z_smooth, smooth, 1, rows)
    smooth_deriv = filtered(z_smooth, deriv, 1, rows)
    deriv_smooth = filtered(z_deriv, smooth, 1, rows)
    grad_y = filtered(both_smooth, deriv, 2, owned)
    grad_x = filtered(smooth_deriv, smooth, 2, owned)
    grad_z = filtered(deriv_smooth, smooth, 2, owned)
    tensor = jnp.stack(
        [
            pooled_full(grad_z * grad_z),
            pooled_full(grad_z * grad_x),
            pooled_full(grad_z * grad_y),
            pooled_full(grad_x * grad_x),
            pooled_full(grad_x * grad_y),
            pooled_full(grad_y * grad_y),
        ]
    )
    hist = jnp.einsum("kc,cabv->abkv", coeffs, tensor, precision=lax.Precision.HIGHEST)
    return hist / float(POOL**3)


def host_taps():
    offsets = np.arange(-RADIUS, RADIUS + 1).astype(np.float64)
    base = np.exp(-offsets * offsets / 8.0)
    slope = -offsets * base
    return base / np.sqrt(np.sum(base * base)), slope / np.sqrt(np.sum(slope * slope))


def host_directions():
    index = np.arange(DIRS).astype(np.float32)
    height = np.float32(1.0) - (index + np.float32(0.5)) / np.float32(DIRS)
    radial = np.sqrt(np.float32(1.0) - height * height)
    phase = np.float32(2.399963229728653) * index
    d_x = radial * np.cos(phase)
    d_y = radial * np.sin(phase)
    two = np.float32(2.0)
    return np.stack(
        [height * height, two * height * d_x, two * height * d_y, d_x * d_x, two * d_x * d_y, d_y * d_y],
        axis=1,
    ).astype(np.float32)


def tap_at(weights, distance):
    index = distance + RADIUS
    inside = (index >= 0) & (index <= 2 * RADIUS)
    return np.where(inside, weights[np.clip(index, 0, 2 * RADIUS)], 0.0)


def halves(matrix):
    high = matrix.astype(np.float32).astype(ml_dtypes.bfloat16)
    low = (matrix - high.astype(np.float64)).astype(np.float32).astype(ml_dtypes.bfloat16)
    return np.stack([high, low])


def y_weights(owned):
    smooth, deriv = host_taps()
    edge = np.concatenate([np.arange(-RADIUS, 0), owned + np.arange(RADIUS)])
    out = np.arange(owned)
    inner = halves(np.concatenate([tap_at(w, out[:, None] - out[None, :]) for w in (smooth, deriv)], axis=1))
    outer = halves(np.concatenate([tap_at(w, edge[:, None] - out[None, :]) for w in (smooth, deriv)], axis=1))
    ends = np.zeros((LANES, 2 * owned), ml_dtypes.bfloat16)
    for part, which in enumerate((0, 0, 1)):
        for copy in range(3):
            start = part * END_PART + copy * EDGE
            ends[start : start + EDGE] = outer[which]
    return np.concatenate([inner[0], inner[1], ends], axis=0)


def zx_weights(planes, rows):
    smooth, deriv = host_taps()
    z_out, x_out = (g.ravel()[:, None] for g in np.meshgrid(np.arange(planes), np.arange(rows), indexing="ij"))
    step = np.arange(EDGE)
    around = np.where(step < RADIUS, rows + step, step - EDGE)
    tables = []
    for places in (np.arange(rows), around):
        z_in, x_in = (g.ravel()[None, :] for g in np.meshgrid(np.arange(planes), places, indexing="ij"))
        fields = []
        for z_taps, x_taps in ((deriv, smooth), (smooth, deriv), (smooth, smooth)):
            blocks = [
                tap_at(z_taps, group * planes + z_in - z_out) * tap_at(x_taps, x_in - x_out)
                for group in (-1, 0, 1)
            ]
            fields.append(np.concatenate(blocks, axis=1))
        tables.append(halves(np.concatenate(fields, axis=0)))
    inner, outer = tables
    return inner, np.concatenate([outer[0], outer[0], outer[1]], axis=1)


def histogram_weights(rows):
    voxels = rows // POOL
    inside = (np.arange(rows)[None, :] // POOL == np.arange(voxels)[:, None]).astype(np.float32)
    table = host_directions()[None, :, :, None] * inside[:, None, None, :]
    return (table.reshape(voxels * DIRS, -1) / np.float32(POOL**3)).astype(np.float32)


def split(values):
    high = values.astype(jnp.bfloat16)
    low = (values - high.astype(jnp.float32)).astype(jnp.bfloat16)
    return high, low


def dot(a, b):
    return jnp.dot(a, b, preferred_element_type=jnp.float32)


def exact_dot(a, b):
    return jnp.dot(a, b, preferred_element_type=jnp.float32, precision=lax.Precision.HIGHEST)


def kernel(
    slabs, tiles, x_hbm, wy_hbm, wzx_hbm, wring_hbm, whist_hbm, out_ref,
    x_ref, wy_ref, wzx_ref, wring_ref, whist_ref,
    recv, halo_l, halo_r, ends_out, ends_in, ends_l, ends_r, ends_main, ends_ring,
    y_high, y_low, ring_high, ring_low, partial,
    load_sem, send_sem, recv_sem, end_send, end_recv, side_sem, fl_send, fl_recv, fr_send, fr_recv,
):
    planes, rows, cells = x_ref.shape
    owned = cells // slabs
    inner_rows = planes * rows
    ring_rows = planes * EDGE
    part = planes // CHUNKS
    s = lax.axis_index("slab")
    t = lax.axis_index("tile")
    has_left = t > 0
    has_right = t < tiles - 1

    pairs = (
        (x_hbm, x_ref), (wy_hbm, wy_ref), (wzx_hbm, wzx_ref), (wring_hbm, wring_ref), (whist_hbm, whist_ref)
    )
    loads = [pltpu.make_async_copy(src, dst, load_sem.at[i]) for i, (src, dst) in enumerate(pairs)]
    for load in loads:
        load.start()

    barrier = pltpu.get_barrier_semaphore()
    for k in range(1, slabs):
        pl.semaphore_signal(barrier, inc=1, device_id=(lax.rem(s + k, slabs), t), device_id_type=MESH)

    @pl.when(has_left)
    def _():
        pl.semaphore_signal(barrier, inc=1, device_id=(s, t - 1), device_id_type=MESH)

    @pl.when(has_right)
    def _():
        pl.semaphore_signal(barrier, inc=1, device_id=(s, t + 1), device_id_type=MESH)

    loads[0].wait()
    lane = lax.broadcasted_iota(jnp.int32, (inner_rows, LANES), 1)
    edges = jnp.zeros((inner_rows, LANES), jnp.float32)

    def side(d, first):
        if d < 0 or d >= slabs:
            return jnp.zeros((inner_rows, LANES), jnp.float32)
        return x_ref[:, :, first : first + LANES].reshape(inner_rows, LANES)

    for d in range(slabs):
        before = side(d - 1, d * owned - LANES)
        after = side(d + 1, (d + 1) * owned)
        both = jnp.where(lane >= LANES // 2, before, after)
        turned = pltpu.roll(both, d * EDGE + RADIUS, 1)
        edges = jnp.where(lane // EDGE == d, turned, edges)
    edges = edges.T
    for d in range(slabs):
        ends_out[d] = edges[d * EDGE : (d + 1) * EDGE]

    beside = jnp.where(has_left, 1, 0) + jnp.where(has_right, 1, 0)
    pl.semaphore_wait(barrier, slabs - 1 + beside)

    def ends_copy(src, dst, k):
        return pltpu.make_async_remote_copy(
            src_ref=ends_out.at[dst], dst_ref=ends_in.at[src],
            send_sem=end_send.at[k], recv_sem=end_recv.at[src],
            device_id=(dst, t), device_id_type=MESH,
        )

    def block_copy(src, dst, k, c):
        first = pl.multiple_of(dst * owned, LANES)
        return pltpu.make_async_remote_copy(
            src_ref=x_ref.at[pl.ds(c * part, part), :, pl.ds(first, owned)],
            dst_ref=recv.at[src, pl.ds(c * part, part)],
            send_sem=send_sem.at[k * CHUNKS + c], recv_sem=recv_sem.at[src * CHUNKS + c],
            device_id=(dst, t), device_id_type=MESH,
        )

    def ends_left():
        return pltpu.make_async_remote_copy(
            src_ref=ends_in, dst_ref=ends_r, send_sem=side_sem.at[0], recv_sem=side_sem.at[1],
            device_id=(s, t - 1), device_id_type=MESH,
        )

    def ends_right():
        return pltpu.make_async_remote_copy(
            src_ref=ends_in, dst_ref=ends_l, send_sem=side_sem.at[2], recv_sem=side_sem.at[3],
            device_id=(s, t + 1), device_id_type=MESH,
        )

    def to_left(p, c):
        here = pl.ds(c * part, part)
        return pltpu.make_async_remote_copy(
            src_ref=recv.at[p, here, pl.ds(0, EDGE)], dst_ref=halo_r.at[p, here],
            send_sem=fl_send.at[p * CHUNKS + c], recv_sem=fl_recv.at[p * CHUNKS + c],
            device_id=(s, t - 1), device_id_type=MESH,
        )

    def to_right(p, c):
        here = pl.ds(c * part, part)
        return pltpu.make_async_remote_copy(
            src_ref=recv.at[p, here, pl.ds(rows - EDGE, EDGE)], dst_ref=halo_l.at[p, here],
            send_sem=fr_send.at[p * CHUNKS + c], recv_sem=fr_recv.at[p * CHUNKS + c],
            device_id=(s, t + 1), device_id_type=MESH,
        )

    def forward(p, c):
        @pl.when(has_left)
        def _():
            to_left(p, c).start()

        @pl.when(has_right)
        def _():
            to_right(p, c).start()

    paired = slabs & (slabs - 1) == 0

    def peer_to(k):
        return s ^ k if paired else lax.rem(s + k, slabs)

    def peer_from(k):
        return s ^ k if paired else lax.rem(s + slabs - k, slabs)

    sends = [ends_copy(s, peer_to(k), k) for k in range(1, slabs)]
    sends += [block_copy(s, peer_to(k), k, c) for c in range(CHUNKS) for k in range(1, slabs)]
    for send in sends:
        send.start()

    recv[s] = x_ref[:, :, pl.ds(pl.multiple_of(s * owned, LANES), owned)]
    ends_in[s] = ends_out[s]
    for c in range(CHUNKS):
        forward(s, c)

    @pl.when(jnp.logical_not(has_left))
    def _():
        halo_l[...] = jnp.zeros_like(halo_l)
        ends_l[...] = jnp.zeros_like(ends_l)

    @pl.when(jnp.logical_not(has_right))
    def _():
        halo_r[...] = jnp.zeros_like(halo_r)
        ends_r[...] = jnp.zeros_like(ends_r)

    for ref, count in ((y_high, inner_rows), (y_low, inner_rows), (ring_high, ring_rows), (ring_low, ring_rows)):
        blank = jnp.zeros((count, 2 * owned), jnp.bfloat16)
        ref[0:count, :] = blank
        ref[(slabs + 1) * count : (slabs + 2) * count, :] = blank

    for k in range(1, slabs):
        p = peer_from(k)
        ends_copy(p, p, 0).wait_recv()

    @pl.when(has_left)
    def _():
        ends_left().start()

    @pl.when(has_right)
    def _():
        ends_right().start()

    @pl.when(has_left)
    def _():
        ends_right().wait_recv()

    @pl.when(has_right)
    def _():
        ends_left().wait_recv()

    def packed(ends):
        high, low = split(ends)
        high = high.astype(jnp.float32)
        low = low.astype(jnp.float32)
        all_parts = high + pltpu.roll(low, END_PART, 1) + pltpu.roll(high, 2 * END_PART, 1)
        return all_parts.astype(jnp.bfloat16)

    ring_lane = lax.broadcasted_iota(jnp.int32, (planes, EDGE, LANES), 2) // EDGE
    ring_step = lax.broadcasted_iota(jnp.int32, (planes, EDGE, LANES), 1)
    rest = jnp.zeros((LANES - 3 * EDGE, LANES), jnp.float32)
    for p in range(slabs):
        turned = jnp.concatenate([ends_in[p], ends_l[p], ends_r[p], rest], axis=0).T
        ends_main[p] = packed(jnp.where(lane < EDGE, turned, 0.0))
        turned = turned.reshape(planes, rows, LANES)
        right = jnp.where(ring_lane == 2, turned[:, 0:EDGE], 0.0)
        left = jnp.where(ring_lane == 1, turned[:, rows - EDGE : rows], 0.0)
        ring = jnp.where(ring_step < RADIUS, right, left).reshape(ring_rows, LANES)
        ends_ring[p * ring_rows : (p + 1) * ring_rows, :] = packed(ring)

    loads[1].wait()

    def along_y(block, ends):
        high, low = split(block)
        inner, finer = wy_ref[0:owned], wy_ref[owned : 2 * owned]
        result = dot(high, inner) + dot(low, inner) + dot(high, finer)
        return split(result + dot(ends, wy_ref[2 * owned : 2 * owned + LANES]))

    def inner_along_y(p):
        high, low = along_y(recv[p].reshape(inner_rows, owned), ends_main[p])
        at = pl.ds(pl.multiple_of((p + 1) * inner_rows, 16), inner_rows)
        y_high[at, :] = high
        y_low[at, :] = low

    inner_along_y(s)
    for c in range(CHUNKS):
        for k in range(1, slabs):
            p = peer_from(k)
            block_copy(p, p, 0, c).wait_recv()
            forward(p, c)
    for k in range(1, slabs):
        inner_along_y(peer_from(k))

    smooth_y = slice(0, owned)
    deriv_y = slice(owned, 2 * owned)
    pair = slice(0, 2 * inner_rows)
    last = slice(2 * inner_rows, 3 * inner_rows)
    loads[2].wait()

    def inner_group(g, carry):
        at = pl.ds(pl.multiple_of(g * inner_rows, 16), 3 * inner_rows)
        for out, field in ((pair, smooth_y), (last, deriv_y)):
            high = y_high[at, field]
            low = y_low[at, field]
            coarse = wzx_ref[0, out, :]
            partial[g, out, :] = dot(coarse, high) + dot(coarse, low) + dot(wzx_ref[1, out, :], high)
        return carry

    lax.fori_loop(0, slabs, inner_group, 0)

    for p in range(slabs):
        for c in range(CHUNKS):
            @pl.when(has_left)
            def _():
                to_right(p, c).wait_recv()

            @pl.when(has_right)
            def _():
                to_left(p, c).wait_recv()

    step = lax.broadcasted_iota(jnp.int32, (slabs, planes, EDGE, owned), 2)
    ring = jnp.where(step < RADIUS, halo_r[...], halo_l[...]).reshape(slabs * ring_rows, owned)
    high, low = along_y(ring, ends_ring[...])
    ring_high[ring_rows : (slabs + 1) * ring_rows, :] = high
    ring_low[ring_rows : (slabs + 1) * ring_rows, :] = low
    loads[3].wait()

    def group(g, sums):
        at = pl.ds(pl.multiple_of(g * ring_rows, 16), 3 * ring_rows)

        def gradient(out, field):
            high = ring_high[at, field]
            low = ring_low[at, field]
            return partial[g, out, :] + dot(wring_ref[out, :], jnp.concatenate([high, low, high], axis=0))

        both = gradient(pair, smooth_y)
        grad_z = both[:inner_rows]
        grad_x = both[inner_rows:]
        grad_y = gradient(last, deriv_y)
        products = (
            grad_z * grad_z, grad_z * grad_x, grad_z * grad_y,
            grad_x * grad_x, grad_x * grad_y, grad_y * grad_y,
        )
        return tuple(
            held + product.reshape(planes, rows, owned).sum(axis=0)
            for held, product in zip(sums, products)
        )

    blank = jnp.zeros((rows, owned), jnp.float32)
    sums = lax.fori_loop(0, slabs, group, (blank,) * 6)
    loads[4].wait()
    mixed = exact_dot(whist_ref[...], jnp.concatenate(sums, axis=0))
    cell = lax.broadcasted_iota(jnp.int32, (owned, owned // POOL), 0)
    voxel = lax.broadcasted_iota(jnp.int32, (owned, owned // POOL), 1)
    pooled = exact_dot(mixed, (cell // POOL == voxel).astype(jnp.float32))
    for b in range(rows // POOL):
        out_ref[0, b] = pooled[b * DIRS : (b + 1) * DIRS]

    for send in sends:
        send.wait_send()

    @pl.when(has_left)
    def _():
        ends_left().wait_send()
        for p in range(slabs):
            for c in range(CHUNKS):
                to_left(p, c).wait_send()

    @pl.when(has_right)
    def _():
        ends_right().wait_send()
        for p in range(slabs):
            for c in range(CHUNKS):
                to_right(p, c).wait_send()


def fused(slabs, tiles, volume):
    planes, rows, cells = volume.shape
    owned = cells // slabs
    inner_rows = planes * rows
    ring_rows = planes * EDGE
    wy = y_weights(owned)
    wzx, wring = zx_weights(planes, rows)
    whist = histogram_weights(rows)
    f32, bf16 = jnp.float32, jnp.bfloat16
    one = pltpu.SemaphoreType.DMA((slabs,))
    many = pltpu.SemaphoreType.DMA((slabs * CHUNKS,))
    halo = pltpu.VMEM((slabs, planes, EDGE, owned), f32)
    ends = pltpu.VMEM((slabs, EDGE, LANES), f32)
    held = pltpu.VMEM(((slabs + 2) * inner_rows, 2 * owned), bf16)
    ring = pltpu.VMEM(((slabs + 2) * ring_rows, 2 * owned), bf16)
    return pl.pallas_call(
        functools.partial(kernel, slabs, tiles),
        out_shape=jax.ShapeDtypeStruct((1, rows // POOL, DIRS, owned // POOL), f32),
        in_specs=[pl.BlockSpec(memory_space=pl.ANY)] * 5,
        out_specs=pl.BlockSpec(memory_space=pltpu.VMEM),
        scratch_shapes=[
            pltpu.VMEM(volume.shape, f32),
            pltpu.VMEM(wy.shape, bf16),
            pltpu.VMEM(wzx.shape, bf16),
            pltpu.VMEM(wring.shape, bf16),
            pltpu.VMEM(whist.shape, f32),
            pltpu.VMEM((slabs, planes, rows, owned), f32),
            halo, halo, ends, ends, ends, ends,
            pltpu.VMEM((slabs, inner_rows, LANES), bf16),
            pltpu.VMEM((slabs * ring_rows, LANES), bf16),
            held, held, ring, ring,
            pltpu.VMEM((slabs, 3 * inner_rows, owned), f32),
            pltpu.SemaphoreType.DMA((5,)),
            many, many, one, one, pltpu.SemaphoreType.DMA((4,)), many, many, many, many,
        ],
        compiler_params=pltpu.CompilerParams(collective_id=0, has_side_effects=True),
    )(volume, jnp.asarray(wy), jnp.asarray(wzx), jnp.asarray(wring), jnp.asarray(whist))


def fits(slabs, tiles, planes, rows, cells):
    owned = cells // slabs
    return (
        slabs * planes == POOL and planes >= RADIUS and planes * rows == LANES
        and rows % POOL == 0 and planes % CHUNKS == 0 and (planes * EDGE) % 16 == 0
        and owned % LANES == 0 and slabs * EDGE <= LANES
    )


def solution(mesh):
    slabs, tiles = mesh.shape["slab"], mesh.shape["tile"]

    def whole(volume):
        if slabs > 1 and tiles > 1 and fits(slabs, tiles, *volume.shape):
            return fused(slabs, tiles, volume)
        return body(volume)

    return jax.shard_map(
        whole,
        mesh=mesh,
        in_specs=(P("slab", "tile", None),),
        out_specs=P(None, "tile", None, "slab"),
        check_vma=False,
    )
```

```python
import functools

import jax
import jax.numpy as jnp
import ml_dtypes
import numpy as np
from jax import lax
from jax.experimental import pallas as pl
from jax.experimental.pallas import tpu as pltpu
from jax.sharding import PartitionSpec as P

RADIUS = 4
POOL = 16
DIRS = 32
MESH = pl.DeviceIdType.MESH
LANES = 128
CHUNKS = 2
VMEM_LIMIT = 64 * 2**20 - 940 * 2**10
TALL = 1024
EDGE = 2 * RADIUS
END_PART = 4 * EDGE


def extended(cells, sides, width):
    for axis, dim in sides:
        count = lax.axis_size(axis)
        ends = count - 1
        head = lax.slice_in_dim(cells, 0, width, axis=dim)
        tail = lax.slice_in_dim(cells, cells.shape[dim] - width, cells.shape[dim], axis=dim)
        cells = jnp.concatenate(
            [
                lax.ppermute(tail, axis, [(i, (i + 1) % count) for i in range(ends)]),
                cells,
                lax.ppermute(head, axis, [((i + 1) % count, i) for i in range(ends)]),
            ],
            axis=dim,
        )
    return cells


def kernel_taps():
    offsets = jnp.arange(-RADIUS, RADIUS + 1).astype(jnp.float32)
    base = jnp.exp(-offsets * offsets / 8.0)
    smooth = base / jnp.sqrt(jnp.sum(base * base))
    slope = -offsets * base
    deriv = slope / jnp.sqrt(jnp.sum(slope * slope))
    return (smooth, deriv)


def direction_table():
    index = jnp.arange(DIRS).astype(jnp.float32)
    height = 1.0 - (index + 0.5) / DIRS
    radial = jnp.sqrt(1.0 - height * height)
    phase = 2.399963229728653 * index
    d_x = radial * jnp.cos(phase)
    d_y = radial * jnp.sin(phase)
    return jnp.stack(
        [
            height * height,
            2.0 * height * d_x,
            2.0 * height * d_y,
            d_x * d_x,
            2.0 * d_x * d_y,
            d_y * d_y,
        ],
        axis=1,
    )


def filtered(padded, weights, axis, count):
    total = weights[0] * lax.slice_in_dim(padded, 0, count, axis=axis)
    for shift_index in range(1, 2 * RADIUS + 1):
        total = total + weights[shift_index] * lax.slice_in_dim(
            padded, shift_index, shift_index + count, axis=axis
        )
    return total


def pooled_full(field):
    planes, rows, cells = field.shape
    return field.reshape(planes // POOL, POOL, rows // POOL, POOL, cells // POOL, POOL).sum(
        axis=(1, 3, 5)
    )


def body(volume):
    smooth, deriv = kernel_taps()
    planes, rows, cells = volume.shape
    coeffs = direction_table()
    regrouped = lax.all_to_all(volume, "slab", split_axis=2, concat_axis=0, tiled=True)
    depth = regrouped.shape[0]
    owned = regrouped.shape[2]
    padded = extended(regrouped, (("slab", 2), ("tile", 1)), RADIUS)
    zpad = jnp.pad(padded, ((RADIUS, RADIUS), (0, 0), (0, 0)))
    z_smooth = filtered(zpad, smooth, 0, depth)
    z_deriv = filtered(zpad, deriv, 0, depth)
    both_smooth = filtered(z_smooth, smooth, 1, rows)
    smooth_deriv = filtered(z_smooth, deriv, 1, rows)
    deriv_smooth = filtered(z_deriv, smooth, 1, rows)
    grad_y = filtered(both_smooth, deriv, 2, owned)
    grad_x = filtered(smooth_deriv, smooth, 2, owned)
    grad_z = filtered(deriv_smooth, smooth, 2, owned)
    tensor = jnp.stack(
        [
            pooled_full(grad_z * grad_z),
            pooled_full(grad_z * grad_x),
            pooled_full(grad_z * grad_y),
            pooled_full(grad_x * grad_x),
            pooled_full(grad_x * grad_y),
            pooled_full(grad_y * grad_y),
        ]
    )
    hist = jnp.einsum("kc,cabv->abkv", coeffs, tensor, precision=lax.Precision.HIGHEST)
    return hist / float(POOL**3)


def host_taps():
    offsets = np.arange(-RADIUS, RADIUS + 1).astype(np.float64)
    base = np.exp(-offsets * offsets / 8.0)
    slope = -offsets * base
    return base / np.sqrt(np.sum(base * base)), slope / np.sqrt(np.sum(slope * slope))


def host_directions():
    index = np.arange(DIRS).astype(np.float32)
    height = np.float32(1.0) - (index + np.float32(0.5)) / np.float32(DIRS)
    radial = np.sqrt(np.float32(1.0) - height * height)
    phase = np.float32(2.399963229728653) * index
    d_x = radial * np.cos(phase)
    d_y = radial * np.sin(phase)
    two = np.float32(2.0)
    return np.stack(
        [height * height, two * height * d_x, two * height * d_y, d_x * d_x, two * d_x * d_y, d_y * d_y],
        axis=1,
    ).astype(np.float32)


def tap_at(weights, distance):
    index = distance + RADIUS
    inside = (index >= 0) & (index <= 2 * RADIUS)
    return np.where(inside, weights[np.clip(index, 0, 2 * RADIUS)], 0.0)


def halves(matrix):
    high = matrix.astype(np.float32).astype(ml_dtypes.bfloat16)
    low = (matrix - high.astype(np.float64)).astype(np.float32).astype(ml_dtypes.bfloat16)
    return np.stack([high, low])


def y_weights(owned):
    smooth, deriv = host_taps()
    edge = np.concatenate([np.arange(-RADIUS, 0), owned + np.arange(RADIUS)])
    out = np.arange(owned)
    inner = halves(np.concatenate([tap_at(w, out[:, None] - out[None, :]) for w in (smooth, deriv)], axis=1))
    outer = halves(np.concatenate([tap_at(w, edge[:, None] - out[None, :]) for w in (smooth, deriv)], axis=1))
    ends = np.zeros((LANES, 2 * owned), ml_dtypes.bfloat16)
    for part, which in enumerate((0, 0, 1)):
        for copy in range(3):
            start = part * END_PART + copy * EDGE
            ends[start : start + EDGE] = outer[which]
    return np.concatenate([inner[0], inner[1], ends], axis=0)


def zx_weights(planes, rows):
    smooth, deriv = host_taps()
    z_out, x_out = (g.ravel()[:, None] for g in np.meshgrid(np.arange(planes), np.arange(rows), indexing="ij"))
    step = np.arange(EDGE)
    around = np.where(step < RADIUS, rows + step, step - EDGE)
    tables = []
    for places in (np.arange(rows), around):
        z_in, x_in = (g.ravel()[None, :] for g in np.meshgrid(np.arange(planes), places, indexing="ij"))
        fields = []
        for z_taps, x_taps in ((deriv, smooth), (smooth, deriv), (smooth, smooth)):
            blocks = [
                tap_at(z_taps, group * planes + z_in - z_out) * tap_at(x_taps, x_in - x_out)
                for group in (-1, 0, 1)
            ]
            fields.append(np.concatenate(blocks, axis=1))
        tables.append(halves(np.concatenate(fields, axis=0)))
    inner, outer = tables
    count = planes * rows
    shares = [
        inner[:, first:stop, i * count : (i + 1) * count]
        for first, stop in ((0, 2 * count), (2 * count, 3 * count))
        for i in range(3)
    ]
    shares = np.concatenate(shares, axis=1)
    inner = np.concatenate([shares[0], shares[0], shares[1]], axis=1)
    return inner, np.concatenate([outer[0], outer[0], outer[1]], axis=1)


def histogram_weights(rows):
    voxels = rows // POOL
    inside = (np.arange(rows)[None, :] // POOL == np.arange(voxels)[:, None]).astype(np.float32)
    table = host_directions()[None, :, :, None] * inside[:, None, None, :]
    return (table.reshape(voxels * DIRS, -1) / np.float32(POOL**3)).astype(np.float32)


def tall(table):
    rows = np.zeros((max(TALL, table.shape[0]), table.shape[1]), table.dtype)
    rows[: table.shape[0]] = table
    return rows


def split(values):
    high = values.astype(jnp.bfloat16)
    low = (values - high.astype(jnp.float32)).astype(jnp.bfloat16)
    return high, low


def dot(a, b):
    return jnp.dot(a, b, preferred_element_type=jnp.float32)


def exact_dot(a, b):
    return jnp.dot(a, b, preferred_element_type=jnp.float32, precision=lax.Precision.HIGHEST)


def kernel(
    slabs, tiles, x_hbm, wy_hbm, wzx_hbm, wring_hbm, whist_hbm, out_ref,
    x_ref, wy_ref, wzx_ref, wring_ref, whist_ref,
    recv, halo_l, halo_r, ends_out, ends_in, ends_l, ends_r, ends_main, ends_ring,
    ring_high, ring_low, partial,
    load_sem, send_sem, recv_sem, end_send, end_recv, side_sem, fl_send, fl_recv, fr_send, fr_recv,
):
    planes, rows, cells = x_ref.shape
    owned = cells // slabs
    inner_rows = planes * rows
    ring_rows = planes * EDGE
    part = planes // CHUNKS
    s = lax.axis_index("slab")
    t = lax.axis_index("tile")
    has_left = t > 0
    has_right = t < tiles - 1

    pairs = (
        (x_hbm, x_ref), (wy_hbm, wy_ref), (wzx_hbm, wzx_ref), (wring_hbm.at[pl.ds(0, wring_ref.shape[0])], wring_ref),
        (whist_hbm.at[pl.ds(0, whist_ref.shape[0])], whist_ref),
    )
    loads = [pltpu.make_async_copy(src, dst, load_sem.at[i]) for i, (src, dst) in enumerate(pairs)]
    for load in loads:
        load.start()

    barrier = pltpu.get_barrier_semaphore()
    for k in range(1, slabs):
        pl.semaphore_signal(barrier, inc=1, device_id=(lax.rem(s + k, slabs), t), device_id_type=MESH)

    @pl.when(has_left)
    def _():
        pl.semaphore_signal(barrier, inc=1, device_id=(s, t - 1), device_id_type=MESH)

    @pl.when(has_right)
    def _():
        pl.semaphore_signal(barrier, inc=1, device_id=(s, t + 1), device_id_type=MESH)

    loads[0].wait()
    lane = lax.broadcasted_iota(jnp.int32, (inner_rows, LANES), 1)
    edges = jnp.zeros((inner_rows, LANES), jnp.float32)

    def side(d, first):
        if d < 0 or d >= slabs:
            return jnp.zeros((inner_rows, LANES), jnp.float32)
        return x_ref[:, :, first : first + LANES].reshape(inner_rows, LANES)

    for d in range(slabs):
        before = side(d - 1, d * owned - LANES)
        after = side(d + 1, (d + 1) * owned)
        both = jnp.where(lane >= LANES // 2, before, after)
        turned = pltpu.roll(both, d * EDGE + RADIUS, 1)
        edges = jnp.where(lane // EDGE == d, turned, edges)
    edges = edges.T
    for d in range(slabs):
        ends_out[d] = edges[d * EDGE : (d + 1) * EDGE]

    beside = jnp.where(has_left, 1, 0) + jnp.where(has_right, 1, 0)
    pl.semaphore_wait(barrier, slabs - 1 + beside)

    def ends_copy(src, dst, k):
        return pltpu.make_async_remote_copy(
            src_ref=ends_out.at[dst], dst_ref=ends_in.at[src],
            send_sem=end_send.at[k], recv_sem=end_recv.at[src],
            device_id=(dst, t), device_id_type=MESH,
        )

    def block_copy(src, dst, k, c):
        first = pl.multiple_of(dst * owned, LANES)
        return pltpu.make_async_remote_copy(
            src_ref=x_ref.at[pl.ds(c * part, part), :, pl.ds(first, owned)],
            dst_ref=recv.at[src, pl.ds(c * part, part)],
            send_sem=send_sem.at[k * CHUNKS + c], recv_sem=recv_sem.at[src * CHUNKS + c],
            device_id=(dst, t), device_id_type=MESH,
        )

    def ends_left():
        return pltpu.make_async_remote_copy(
            src_ref=ends_in, dst_ref=ends_r, send_sem=side_sem.at[0], recv_sem=side_sem.at[1],
            device_id=(s, t - 1), device_id_type=MESH,
        )

    def ends_right():
        return pltpu.make_async_remote_copy(
            src_ref=ends_in, dst_ref=ends_l, send_sem=side_sem.at[2], recv_sem=side_sem.at[3],
            device_id=(s, t + 1), device_id_type=MESH,
        )

    def to_left(p, c):
        here = pl.ds(c * part, part)
        return pltpu.make_async_remote_copy(
            src_ref=recv.at[p, here, pl.ds(0, EDGE)], dst_ref=halo_r.at[p, here],
            send_sem=fl_send.at[p * CHUNKS + c], recv_sem=fl_recv.at[p * CHUNKS + c],
            device_id=(s, t - 1), device_id_type=MESH,
        )

    def to_right(p, c):
        here = pl.ds(c * part, part)
        return pltpu.make_async_remote_copy(
            src_ref=recv.at[p, here, pl.ds(rows - EDGE, EDGE)], dst_ref=halo_l.at[p, here],
            send_sem=fr_send.at[p * CHUNKS + c], recv_sem=fr_recv.at[p * CHUNKS + c],
            device_id=(s, t + 1), device_id_type=MESH,
        )

    def forward(p, c):
        @pl.when(has_left)
        def _():
            to_left(p, c).start()

        @pl.when(has_right)
        def _():
            to_right(p, c).start()

    paired = slabs & (slabs - 1) == 0

    def peer_to(k):
        return s ^ k if paired else lax.rem(s + k, slabs)

    def peer_from(k):
        return s ^ k if paired else lax.rem(s + slabs - k, slabs)

    sends = [ends_copy(s, peer_to(k), k) for k in range(1, slabs)]
    sends += [block_copy(s, peer_to(k), k, c) for c in range(CHUNKS) for k in range(1, slabs)]
    for send in sends:
        send.start()

    recv[s] = x_ref[:, :, pl.ds(pl.multiple_of(s * owned, LANES), owned)]
    ends_in[s] = ends_out[s]
    for c in range(CHUNKS):
        forward(s, c)

    @pl.when(jnp.logical_not(has_left))
    def _():
        halo_l[...] = jnp.zeros_like(halo_l)
        ends_l[...] = jnp.zeros_like(ends_l)

    @pl.when(jnp.logical_not(has_right))
    def _():
        halo_r[...] = jnp.zeros_like(halo_r)
        ends_r[...] = jnp.zeros_like(ends_r)

    partial[...] = jnp.zeros_like(partial)
    for ref, count in ((ring_high, ring_rows), (ring_low, ring_rows)):
        blank = jnp.zeros((count, 2 * owned), jnp.bfloat16)
        ref[0:count, :] = blank
        ref[(slabs + 1) * count : (slabs + 2) * count, :] = blank

    for k in range(1, slabs):
        p = peer_from(k)
        ends_copy(p, p, 0).wait_recv()

    @pl.when(has_left)
    def _():
        ends_left().start()

    @pl.when(has_right)
    def _():
        ends_right().start()

    @pl.when(has_left)
    def _():
        ends_right().wait_recv()

    @pl.when(has_right)
    def _():
        ends_left().wait_recv()

    def packed(ends):
        high, low = split(ends)
        high = high.astype(jnp.float32)
        low = low.astype(jnp.float32)
        all_parts = high + pltpu.roll(low, END_PART, 1) + pltpu.roll(high, 2 * END_PART, 1)
        return all_parts.astype(jnp.bfloat16)

    ring_lane = lax.broadcasted_iota(jnp.int32, (planes, EDGE, LANES), 2) // EDGE
    ring_step = lax.broadcasted_iota(jnp.int32, (planes, EDGE, LANES), 1)
    rest = jnp.zeros((LANES - 3 * EDGE, LANES), jnp.float32)
    for p in range(slabs):
        turned = jnp.concatenate([ends_in[p], ends_l[p], ends_r[p], rest], axis=0).T
        ends_main[p] = packed(jnp.where(lane < EDGE, turned, 0.0))
        turned = turned.reshape(planes, rows, LANES)
        right = jnp.where(ring_lane == 2, turned[:, 0:EDGE], 0.0)
        left = jnp.where(ring_lane == 1, turned[:, rows - EDGE : rows], 0.0)
        ring = jnp.where(ring_step < RADIUS, right, left).reshape(ring_rows, LANES)
        ends_ring[p * ring_rows : (p + 1) * ring_rows, :] = packed(ring)

    loads[1].wait()
    loads[2].wait()
    smooth_y = slice(0, owned)
    deriv_y = slice(owned, 2 * owned)
    pair = slice(0, 2 * inner_rows)
    last = slice(2 * inner_rows, 3 * inner_rows)

    def along_y(block, ends):
        high, low = split(block)
        inner, finer = wy_ref[0:owned], wy_ref[owned : 2 * owned]
        result = dot(high, inner) + dot(low, inner) + dot(high, finer)
        return split(result + dot(ends, wy_ref[2 * owned : 2 * owned + LANES]))

    def inner_along_y(p):
        high, low = along_y(recv[p].reshape(inner_rows, owned), ends_main[p])
        parts = jnp.concatenate([high, low, high], axis=0)
        for out, first, field in ((pair, 0, smooth_y), (last, 6 * inner_rows, deriv_y)):
            count = out.stop - out.start
            share = dot(wzx_ref[first : first + 3 * count, :], parts[:, field])
            for i in range(3):
                partial[p + 2 - i, out, :] += share[i * count : (i + 1) * count]

    inner_along_y(s)
    for c in range(CHUNKS):
        for k in range(1, slabs):
            p = peer_from(k)
            block_copy(p, p, 0, c).wait_recv()
            forward(p, c)
    for k in range(1, slabs):
        inner_along_y(peer_from(k))

    for p in range(slabs):
        for c in range(CHUNKS):
            @pl.when(has_left)
            def _():
                to_right(p, c).wait_recv()

            @pl.when(has_right)
            def _():
                to_left(p, c).wait_recv()

    step = lax.broadcasted_iota(jnp.int32, (slabs, planes, EDGE, owned), 2)
    ring = jnp.where(step < RADIUS, halo_r[...], halo_l[...]).reshape(slabs * ring_rows, owned)
    high, low = along_y(ring, ends_ring[...])
    ring_high[ring_rows : (slabs + 1) * ring_rows, :] = high
    ring_low[ring_rows : (slabs + 1) * ring_rows, :] = low
    loads[3].wait()

    def group(g, sums):
        at = pl.ds(pl.multiple_of(g * ring_rows, 16), 3 * ring_rows)

        def gradient(out, field):
            high = ring_high[at, field]
            low = ring_low[at, field]
            return partial[g + 1, out, :] + dot(wring_ref[out, :], jnp.concatenate([high, low, high], axis=0))

        both = gradient(pair, smooth_y)
        grad_z = both[:inner_rows]
        grad_x = both[inner_rows:]
        grad_y = gradient(last, deriv_y)
        products = (
            grad_z * grad_z, grad_z * grad_x, grad_z * grad_y,
            grad_x * grad_x, grad_x * grad_y, grad_y * grad_y,
        )
        return tuple(
            held + product.reshape(planes, rows, owned).sum(axis=0)
            for held, product in zip(sums, products)
        )

    blank = jnp.zeros((rows, owned), jnp.float32)
    sums = lax.fori_loop(0, slabs, group, (blank,) * 6)
    loads[4].wait()
    mixed = exact_dot(whist_ref[...], jnp.concatenate(sums, axis=0))
    cell = lax.broadcasted_iota(jnp.int32, (owned, owned // POOL), 0)
    voxel = lax.broadcasted_iota(jnp.int32, (owned, owned // POOL), 1)
    pooled = exact_dot(mixed, (cell // POOL == voxel).astype(jnp.float32))
    for b in range(rows // POOL):
        out_ref[0, b] = pooled[b * DIRS : (b + 1) * DIRS]

    for send in sends:
        send.wait_send()

    @pl.when(has_left)
    def _():
        ends_left().wait_send()
        for p in range(slabs):
            for c in range(CHUNKS):
                to_left(p, c).wait_send()

    @pl.when(has_right)
    def _():
        ends_right().wait_send()
        for p in range(slabs):
            for c in range(CHUNKS):
                to_right(p, c).wait_send()


def fused(slabs, tiles, volume):
    planes, rows, cells = volume.shape
    owned = cells // slabs
    inner_rows = planes * rows
    ring_rows = planes * EDGE
    wy = y_weights(owned)
    wzx, wring = zx_weights(planes, rows)
    whist = histogram_weights(rows)
    f32, bf16 = jnp.float32, jnp.bfloat16
    one = pltpu.SemaphoreType.DMA((slabs,))
    many = pltpu.SemaphoreType.DMA((slabs * CHUNKS,))
    halo = pltpu.VMEM((slabs, planes, EDGE, owned), f32)
    ends = pltpu.VMEM((slabs, EDGE, LANES), f32)
    ring = pltpu.VMEM(((slabs + 2) * ring_rows, 2 * owned), bf16)
    return pl.pallas_call(
        functools.partial(kernel, slabs, tiles),
        out_shape=jax.ShapeDtypeStruct((1, rows // POOL, DIRS, owned // POOL), f32),
        in_specs=[pl.BlockSpec(memory_space=pl.ANY)] * 5,
        out_specs=pl.BlockSpec(memory_space=pltpu.VMEM),
        scratch_shapes=[
            pltpu.VMEM(volume.shape, f32),
            pltpu.VMEM(wy.shape, bf16),
            pltpu.VMEM(wzx.shape, bf16),
            pltpu.VMEM(wring.shape, bf16),
            pltpu.VMEM(whist.shape, f32),
            pltpu.VMEM((slabs, planes, rows, owned), f32),
            halo, halo, ends, ends, ends, ends,
            pltpu.VMEM((slabs, inner_rows, LANES), bf16),
            pltpu.VMEM((slabs * ring_rows, LANES), bf16),
            ring, ring,
            pltpu.VMEM((slabs + 2, 3 * inner_rows, owned), f32),
            pltpu.SemaphoreType.DMA((5,)),
            many, many, one, one, pltpu.SemaphoreType.DMA((4,)), many, many, many, many,
        ],
        compiler_params=pltpu.CompilerParams(collective_id=0, has_side_effects=True, vmem_limit_bytes=VMEM_LIMIT),
    )(volume, jnp.asarray(wy), jnp.asarray(wzx), jnp.asarray(tall(wring)), jnp.asarray(tall(whist)))


def fits(slabs, tiles, planes, rows, cells):
    owned = cells // slabs
    return (
        slabs * planes == POOL and planes >= RADIUS and planes * rows == LANES
        and rows % POOL == 0 and planes % CHUNKS == 0 and (planes * EDGE) % 16 == 0
        and owned % LANES == 0 and slabs * EDGE <= LANES
    )


def solution(mesh):
    slabs, tiles = mesh.shape["slab"], mesh.shape["tile"]

    def whole(volume):
        if slabs > 1 and tiles > 1 and fits(slabs, tiles, *volume.shape):
            return fused(slabs, tiles, volume)
        return body(volume)

    return jax.shard_map(
        whole,
        mesh=mesh,
        in_specs=(P("slab", "tile", None),),
        out_specs=P(None, "tile", None, "slab"),
        check_vma=False,
    )
```

```python
import functools

import jax
import jax.numpy as jnp
import ml_dtypes
import numpy as np
from jax import lax
from jax.experimental import pallas as pl
from jax.experimental.pallas import tpu as pltpu
from jax.sharding import PartitionSpec as P

RADIUS = 4
POOL = 16
DIRS = 32
MESH = pl.DeviceIdType.MESH
LANES = 128
CHUNKS = 2
EDGE = 2 * RADIUS
END_PART = 4 * EDGE


def extended(cells, sides, width):
    for axis, dim in sides:
        count = lax.axis_size(axis)
        ends = count - 1
        head = lax.slice_in_dim(cells, 0, width, axis=dim)
        tail = lax.slice_in_dim(cells, cells.shape[dim] - width, cells.shape[dim], axis=dim)
        cells = jnp.concatenate(
            [
                lax.ppermute(tail, axis, [(i, (i + 1) % count) for i in range(ends)]),
                cells,
                lax.ppermute(head, axis, [((i + 1) % count, i) for i in range(ends)]),
            ],
            axis=dim,
        )
    return cells


def kernel_taps():
    offsets = jnp.arange(-RADIUS, RADIUS + 1).astype(jnp.float32)
    base = jnp.exp(-offsets * offsets / 8.0)
    smooth = base / jnp.sqrt(jnp.sum(base * base))
    slope = -offsets * base
    deriv = slope / jnp.sqrt(jnp.sum(slope * slope))
    return (smooth, deriv)


def direction_table():
    index = jnp.arange(DIRS).astype(jnp.float32)
    height = 1.0 - (index + 0.5) / DIRS
    radial = jnp.sqrt(1.0 - height * height)
    phase = 2.399963229728653 * index
    d_x = radial * jnp.cos(phase)
    d_y = radial * jnp.sin(phase)
    return jnp.stack(
        [
            height * height,
            2.0 * height * d_x,
            2.0 * height * d_y,
            d_x * d_x,
            2.0 * d_x * d_y,
            d_y * d_y,
        ],
        axis=1,
    )


def filtered(padded, weights, axis, count):
    total = weights[0] * lax.slice_in_dim(padded, 0, count, axis=axis)
    for shift_index in range(1, 2 * RADIUS + 1):
        total = total + weights[shift_index] * lax.slice_in_dim(
            padded, shift_index, shift_index + count, axis=axis
        )
    return total


def pooled_full(field):
    planes, rows, cells = field.shape
    return field.reshape(planes // POOL, POOL, rows // POOL, POOL, cells // POOL, POOL).sum(
        axis=(1, 3, 5)
    )


def body(volume):
    smooth, deriv = kernel_taps()
    planes, rows, cells = volume.shape
    coeffs = direction_table()
    regrouped = lax.all_to_all(volume, "slab", split_axis=2, concat_axis=0, tiled=True)
    depth = regrouped.shape[0]
    owned = regrouped.shape[2]
    padded = extended(regrouped, (("slab", 2), ("tile", 1)), RADIUS)
    zpad = jnp.pad(padded, ((RADIUS, RADIUS), (0, 0), (0, 0)))
    z_smooth = filtered(zpad, smooth, 0, depth)
    z_deriv = filtered(zpad, deriv, 0, depth)
    both_smooth = filtered(z_smooth, smooth, 1, rows)
    smooth_deriv = filtered(z_smooth, deriv, 1, rows)
    deriv_smooth = filtered(z_deriv, smooth, 1, rows)
    grad_y = filtered(both_smooth, deriv, 2, owned)
    grad_x = filtered(smooth_deriv, smooth, 2, owned)
    grad_z = filtered(deriv_smooth, smooth, 2, owned)
    tensor = jnp.stack(
        [
            pooled_full(grad_z * grad_z),
            pooled_full(grad_z * grad_x),
            pooled_full(grad_z * grad_y),
            pooled_full(grad_x * grad_x),
            pooled_full(grad_x * grad_y),
            pooled_full(grad_y * grad_y),
        ]
    )
    hist = jnp.einsum("kc,cabv->abkv", coeffs, tensor, precision=lax.Precision.HIGHEST)
    return hist / float(POOL**3)


def host_taps():
    offsets = np.arange(-RADIUS, RADIUS + 1).astype(np.float64)
    base = np.exp(-offsets * offsets / 8.0)
    slope = -offsets * base
    return base / np.sqrt(np.sum(base * base)), slope / np.sqrt(np.sum(slope * slope))


def host_directions():
    index = np.arange(DIRS).astype(np.float32)
    height = np.float32(1.0) - (index + np.float32(0.5)) / np.float32(DIRS)
    radial = np.sqrt(np.float32(1.0) - height * height)
    phase = np.float32(2.399963229728653) * index
    d_x = radial * np.cos(phase)
    d_y = radial * np.sin(phase)
    two = np.float32(2.0)
    return np.stack(
        [height * height, two * height * d_x, two * height * d_y, d_x * d_x, two * d_x * d_y, d_y * d_y],
        axis=1,
    ).astype(np.float32)


def tap_at(weights, distance):
    index = distance + RADIUS
    inside = (index >= 0) & (index <= 2 * RADIUS)
    return np.where(inside, weights[np.clip(index, 0, 2 * RADIUS)], 0.0)


def halves(matrix):
    high = matrix.astype(np.float32).astype(ml_dtypes.bfloat16)
    low = (matrix - high.astype(np.float64)).astype(np.float32).astype(ml_dtypes.bfloat16)
    return np.stack([high, low])


def y_weights(owned):
    smooth, deriv = host_taps()
    edge = np.concatenate([np.arange(-RADIUS, 0), owned + np.arange(RADIUS)])
    out = np.arange(owned)
    inner = halves(np.concatenate([tap_at(w, out[:, None] - out[None, :]) for w in (smooth, deriv)], axis=1))
    outer = halves(np.concatenate([tap_at(w, edge[:, None] - out[None, :]) for w in (smooth, deriv)], axis=1))
    ends = np.zeros((LANES, 2 * owned), ml_dtypes.bfloat16)
    for part, which in enumerate((0, 0, 1)):
        for copy in range(3):
            start = part * END_PART + copy * EDGE
            ends[start : start + EDGE] = outer[which]
    return np.concatenate([inner[0], inner[1], ends], axis=0)


def zx_weights(planes, rows):
    smooth, deriv = host_taps()
    z_out, x_out = (g.ravel()[:, None] for g in np.meshgrid(np.arange(planes), np.arange(rows), indexing="ij"))
    step = np.arange(EDGE)
    around = np.where(step < RADIUS, rows + step, step - EDGE)
    tables = []
    for places in (np.arange(rows), around):
        z_in, x_in = (g.ravel()[None, :] for g in np.meshgrid(np.arange(planes), places, indexing="ij"))
        fields = []
        for z_taps, x_taps in ((deriv, smooth), (smooth, deriv), (smooth, smooth)):
            blocks = [
                tap_at(z_taps, group * planes + z_in - z_out) * tap_at(x_taps, x_in - x_out)
                for group in (-1, 0, 1)
            ]
            fields.append(np.concatenate(blocks, axis=1))
        tables.append(halves(np.concatenate(fields, axis=0)))
    inner, outer = tables
    return inner, np.concatenate([outer[0], outer[0], outer[1]], axis=1)


def histogram_weights(rows):
    voxels = rows // POOL
    inside = (np.arange(rows)[None, :] // POOL == np.arange(voxels)[:, None]).astype(np.float32)
    table = host_directions()[None, :, :, None] * inside[:, None, None, :]
    return (table.reshape(voxels * DIRS, -1) / np.float32(POOL**3)).astype(np.float32)


def split(values):
    high = values.astype(jnp.bfloat16)
    low = (values - high.astype(jnp.float32)).astype(jnp.bfloat16)
    return high, low


def dot(a, b):
    return jnp.dot(a, b, preferred_element_type=jnp.float32)


def exact_dot(a, b):
    return jnp.dot(a, b, preferred_element_type=jnp.float32, precision=lax.Precision.HIGHEST)


def kernel(
    slabs, tiles, x_hbm, wy_hbm, wzx_hbm, wring_hbm, whist_hbm, out_ref,
    x_ref, wy_ref, wzx_ref, wring_ref, whist_ref,
    recv, halo_l, halo_r, ends_out, ends_in, ends_l, ends_r, ends_main, ends_ring,
    y_high, y_low, ring_high, ring_low, partial,
    load_sem, send_sem, recv_sem, end_send, end_recv, side_sem, fl_send, fl_recv, fr_send, fr_recv,
):
    planes, rows, cells = x_ref.shape
    owned = cells // slabs
    inner_rows = planes * rows
    ring_rows = planes * EDGE
    part = planes // CHUNKS
    s = lax.axis_index("slab")
    t = lax.axis_index("tile")
    has_left = t > 0
    has_right = t < tiles - 1

    pairs = (
        (x_hbm, x_ref), (wy_hbm, wy_ref), (wzx_hbm, wzx_ref), (wring_hbm, wring_ref), (whist_hbm, whist_ref)
    )
    loads = [pltpu.make_async_copy(src, dst, load_sem.at[i]) for i, (src, dst) in enumerate(pairs)]
    for load in loads:
        load.start()

    barrier = pltpu.get_barrier_semaphore()
    for k in range(1, slabs):
        pl.semaphore_signal(barrier, inc=1, device_id=(lax.rem(s + k, slabs), t), device_id_type=MESH)

    @pl.when(has_left)
    def _():
        pl.semaphore_signal(barrier, inc=1, device_id=(s, t - 1), device_id_type=MESH)

    @pl.when(has_right)
    def _():
        pl.semaphore_signal(barrier, inc=1, device_id=(s, t + 1), device_id_type=MESH)

    loads[0].wait()
    lane = lax.broadcasted_iota(jnp.int32, (inner_rows, LANES), 1)
    edges = jnp.zeros((inner_rows, LANES), jnp.float32)

    def side(d, first):
        if d < 0 or d >= slabs:
            return jnp.zeros((inner_rows, LANES), jnp.float32)
        return x_ref[:, :, first : first + LANES].reshape(inner_rows, LANES)

    for d in range(slabs):
        before = side(d - 1, d * owned - LANES)
        after = side(d + 1, (d + 1) * owned)
        both = jnp.where(lane >= LANES // 2, before, after)
        turned = pltpu.roll(both, d * EDGE + RADIUS, 1)
        edges = jnp.where(lane // EDGE == d, turned, edges)
    edges = edges.T
    for d in range(slabs):
        ends_out[d] = edges[d * EDGE : (d + 1) * EDGE]

    beside = jnp.where(has_left, 1, 0) + jnp.where(has_right, 1, 0)
    pl.semaphore_wait(barrier, slabs - 1 + beside)

    def ends_copy(src, dst, k):
        return pltpu.make_async_remote_copy(
            src_ref=ends_out.at[dst], dst_ref=ends_in.at[src],
            send_sem=end_send.at[k], recv_sem=end_recv.at[src],
            device_id=(dst, t), device_id_type=MESH,
        )

    def block_copy(src, dst, k, c):
        first = pl.multiple_of(dst * owned, LANES)
        return pltpu.make_async_remote_copy(
            src_ref=x_ref.at[pl.ds(c * part, part), :, pl.ds(first, owned)],
            dst_ref=recv.at[src, pl.ds(c * part, part)],
            send_sem=send_sem.at[k * CHUNKS + c], recv_sem=recv_sem.at[src * CHUNKS + c],
            device_id=(dst, t), device_id_type=MESH,
        )

    def ends_left():
        return pltpu.make_async_remote_copy(
            src_ref=ends_in, dst_ref=ends_r, send_sem=side_sem.at[0], recv_sem=side_sem.at[1],
            device_id=(s, t - 1), device_id_type=MESH,
        )

    def ends_right():
        return pltpu.make_async_remote_copy(
            src_ref=ends_in, dst_ref=ends_l, send_sem=side_sem.at[2], recv_sem=side_sem.at[3],
            device_id=(s, t + 1), device_id_type=MESH,
        )

    def to_left(p, c):
        here = pl.ds(c * part, part)
        return pltpu.make_async_remote_copy(
            src_ref=recv.at[p, here, pl.ds(0, EDGE)], dst_ref=halo_r.at[p, here],
            send_sem=fl_send.at[p * CHUNKS + c], recv_sem=fl_recv.at[p * CHUNKS + c],
            device_id=(s, t - 1), device_id_type=MESH,
        )

    def to_right(p, c):
        here = pl.ds(c * part, part)
        return pltpu.make_async_remote_copy(
            src_ref=recv.at[p, here, pl.ds(rows - EDGE, EDGE)], dst_ref=halo_l.at[p, here],
            send_sem=fr_send.at[p * CHUNKS + c], recv_sem=fr_recv.at[p * CHUNKS + c],
            device_id=(s, t + 1), device_id_type=MESH,
        )

    def forward(p, c):
        @pl.when(has_left)
        def _():
            to_left(p, c).start()

        @pl.when(has_right)
        def _():
            to_right(p, c).start()

    sends = [ends_copy(s, lax.rem(s + k, slabs), k) for k in range(1, slabs)]
    sends += [block_copy(s, lax.rem(s + k, slabs), k, c) for c in range(CHUNKS) for k in range(1, slabs)]
    for send in sends:
        send.start()

    recv[s] = x_ref[:, :, pl.ds(pl.multiple_of(s * owned, LANES), owned)]
    ends_in[s] = ends_out[s]
    for c in range(CHUNKS):
        forward(s, c)

    @pl.when(jnp.logical_not(has_left))
    def _():
        halo_l[...] = jnp.zeros_like(halo_l)
        ends_l[...] = jnp.zeros_like(ends_l)

    @pl.when(jnp.logical_not(has_right))
    def _():
        halo_r[...] = jnp.zeros_like(halo_r)
        ends_r[...] = jnp.zeros_like(ends_r)

    for ref, count in ((y_high, inner_rows), (y_low, inner_rows), (ring_high, ring_rows), (ring_low, ring_rows)):
        blank = jnp.zeros((count, 2 * owned), jnp.bfloat16)
        ref[0:count, :] = blank
        ref[(slabs + 1) * count : (slabs + 2) * count, :] = blank

    for k in range(1, slabs):
        p = lax.rem(s + slabs - k, slabs)
        ends_copy(p, p, 0).wait_recv()

    @pl.when(has_left)
    def _():
        ends_left().start()

    @pl.when(has_right)
    def _():
        ends_right().start()

    def turned_parts(*kinds):
        parts = [split(kind) for kind in kinds]
        rest = [jnp.zeros((END_PART - len(kinds) * EDGE, LANES), jnp.float32)]
        high = [part[0].astype(jnp.float32) for part in parts] + rest
        low = [part[1].astype(jnp.float32) for part in parts] + rest
        last = [jnp.zeros((LANES - 3 * END_PART, LANES), jnp.float32)]
        return jnp.concatenate(high + low + high + last, axis=0).T

    for p in range(slabs):
        ends_main[p] = turned_parts(ends_in[p]).astype(jnp.bfloat16)

    loads[1].wait()

    def along_y(block, ends):
        high, low = split(block)
        inner, finer = wy_ref[0:owned], wy_ref[owned : 2 * owned]
        result = dot(high, inner) + dot(low, inner) + dot(high, finer)
        return split(result + dot(ends, wy_ref[2 * owned : 2 * owned + LANES]))

    def inner_along_y(p):
        high, low = along_y(recv[p].reshape(inner_rows, owned), ends_main[p])
        at = pl.ds(pl.multiple_of((p + 1) * inner_rows, 16), inner_rows)
        y_high[at, :] = high
        y_low[at, :] = low

    inner_along_y(s)
    for c in range(CHUNKS):
        for k in range(1, slabs):
            p = lax.rem(s + slabs - k, slabs)
            block_copy(p, p, 0, c).wait_recv()
            forward(p, c)
    for k in range(1, slabs):
        inner_along_y(lax.rem(s + slabs - k, slabs))

    smooth_y = slice(0, owned)
    deriv_y = slice(owned, 2 * owned)
    pair = slice(0, 2 * inner_rows)
    last = slice(2 * inner_rows, 3 * inner_rows)
    loads[2].wait()

    def inner_group(g, carry):
        at = pl.ds(pl.multiple_of(g * inner_rows, 16), 3 * inner_rows)
        for out, field in ((pair, smooth_y), (last, deriv_y)):
            high = y_high[at, field]
            low = y_low[at, field]
            coarse = wzx_ref[0, out, :]
            partial[g, out, :] = dot(coarse, high) + dot(coarse, low) + dot(wzx_ref[1, out, :], high)
        return carry

    lax.fori_loop(0, slabs, inner_group, 0)

    @pl.when(has_left)
    def _():
        ends_right().wait_recv()

    @pl.when(has_right)
    def _():
        ends_left().wait_recv()

    ring_place = lax.broadcasted_iota(jnp.int32, (planes, EDGE, LANES), 2) // EDGE % (END_PART // EDGE)
    ring_step = lax.broadcasted_iota(jnp.int32, (planes, EDGE, LANES), 1)
    for p in range(slabs):
        turned = turned_parts(ends_l[p], ends_r[p]).reshape(planes, rows, LANES)
        right = jnp.where(ring_place == 1, turned[:, 0:EDGE], 0.0)
        left = jnp.where(ring_place == 0, turned[:, rows - EDGE : rows], 0.0)
        ring = jnp.where(ring_step < RADIUS, right, left).reshape(ring_rows, LANES)
        ends_ring[p * ring_rows : (p + 1) * ring_rows, :] = ring.astype(jnp.bfloat16)

    for p in range(slabs):
        for c in range(CHUNKS):
            @pl.when(has_left)
            def _():
                to_right(p, c).wait_recv()

            @pl.when(has_right)
            def _():
                to_left(p, c).wait_recv()

    step = lax.broadcasted_iota(jnp.int32, (slabs, planes, EDGE, owned), 2)
    ring = jnp.where(step < RADIUS, halo_r[...], halo_l[...]).reshape(slabs * ring_rows, owned)
    high, low = along_y(ring, ends_ring[...])
    ring_high[ring_rows : (slabs + 1) * ring_rows, :] = high
    ring_low[ring_rows : (slabs + 1) * ring_rows, :] = low
    loads[3].wait()

    def group(g, sums):
        at = pl.ds(pl.multiple_of(g * ring_rows, 16), 3 * ring_rows)

        def gradient(out, field):
            high = ring_high[at, field]
            low = ring_low[at, field]
            return partial[g, out, :] + dot(wring_ref[out, :], jnp.concatenate([high, low, high], axis=0))

        both = gradient(pair, smooth_y)
        grad_z = both[:inner_rows]
        grad_x = both[inner_rows:]
        grad_y = gradient(last, deriv_y)
        products = (
            grad_z * grad_z, grad_z * grad_x, grad_z * grad_y,
            grad_x * grad_x, grad_x * grad_y, grad_y * grad_y,
        )
        return tuple(
            held + product.reshape(planes, rows, owned).sum(axis=0)
            for held, product in zip(sums, products)
        )

    blank = jnp.zeros((rows, owned), jnp.float32)
    sums = lax.fori_loop(0, slabs, group, (blank,) * 6)
    loads[4].wait()
    mixed = exact_dot(whist_ref[...], jnp.concatenate(sums, axis=0))
    cell = lax.broadcasted_iota(jnp.int32, (owned, owned // POOL), 0)
    voxel = lax.broadcasted_iota(jnp.int32, (owned, owned // POOL), 1)
    pooled = exact_dot(mixed, (cell // POOL == voxel).astype(jnp.float32))
    for b in range(rows // POOL):
        out_ref[0, b] = pooled[b * DIRS : (b + 1) * DIRS]

    for send in sends:
        send.wait_send()

    @pl.when(has_left)
    def _():
        ends_left().wait_send()
        for p in range(slabs):
            for c in range(CHUNKS):
                to_left(p, c).wait_send()

    @pl.when(has_right)
    def _():
        ends_right().wait_send()
        for p in range(slabs):
            for c in range(CHUNKS):
                to_right(p, c).wait_send()


def fused(slabs, tiles, volume):
    planes, rows, cells = volume.shape
    owned = cells // slabs
    inner_rows = planes * rows
    ring_rows = planes * EDGE
    wy = y_weights(owned)
    wzx, wring = zx_weights(planes, rows)
    whist = histogram_weights(rows)
    f32, bf16 = jnp.float32, jnp.bfloat16
    one = pltpu.SemaphoreType.DMA((slabs,))
    many = pltpu.SemaphoreType.DMA((slabs * CHUNKS,))
    halo = pltpu.VMEM((slabs, planes, EDGE, owned), f32)
    ends = pltpu.VMEM((slabs, EDGE, LANES), f32)
    held = pltpu.VMEM(((slabs + 2) * inner_rows, 2 * owned), bf16)
    ring = pltpu.VMEM(((slabs + 2) * ring_rows, 2 * owned), bf16)
    return pl.pallas_call(
        functools.partial(kernel, slabs, tiles),
        out_shape=jax.ShapeDtypeStruct((1, rows // POOL, DIRS, owned // POOL), f32),
        in_specs=[pl.BlockSpec(memory_space=pl.ANY)] * 5,
        out_specs=pl.BlockSpec(memory_space=pltpu.VMEM),
        scratch_shapes=[
            pltpu.VMEM(volume.shape, f32),
            pltpu.VMEM(wy.shape, bf16),
            pltpu.VMEM(wzx.shape, bf16),
            pltpu.VMEM(wring.shape, bf16),
            pltpu.VMEM(whist.shape, f32),
            pltpu.VMEM((slabs, planes, rows, owned), f32),
            halo, halo, ends, ends, ends, ends,
            pltpu.VMEM((slabs, inner_rows, LANES), bf16),
            pltpu.VMEM((slabs * ring_rows, LANES), bf16),
            held, held, ring, ring,
            pltpu.VMEM((slabs, 3 * inner_rows, owned), f32),
            pltpu.SemaphoreType.DMA((5,)),
            many, many, one, one, pltpu.SemaphoreType.DMA((4,)), many, many, many, many,
        ],
        compiler_params=pltpu.CompilerParams(collective_id=0, has_side_effects=True),
    )(volume, jnp.asarray(wy), jnp.asarray(wzx), jnp.asarray(wring), jnp.asarray(whist))


def fits(slabs, tiles, planes, rows, cells):
    owned = cells // slabs
    return (
        slabs * planes == POOL and planes >= RADIUS and planes * rows == LANES
        and rows % POOL == 0 and planes % CHUNKS == 0 and (planes * EDGE) % 16 == 0
        and owned % LANES == 0 and slabs * EDGE <= LANES
    )


def solution(mesh):
    slabs, tiles = mesh.shape["slab"], mesh.shape["tile"]

    def whole(volume):
        if slabs > 1 and tiles > 1 and fits(slabs, tiles, *volume.shape):
            return fused(slabs, tiles, volume)
        return body(volume)

    return jax.shard_map(
        whole,
        mesh=mesh,
        in_specs=(P("slab", "tile", None),),
        out_specs=P(None, "tile", None, "slab"),
        check_vma=False,
    )
```

```python
import functools

import jax
import jax.numpy as jnp
import ml_dtypes
import numpy as np
from jax import lax
from jax.experimental import pallas as pl
from jax.experimental.pallas import tpu as pltpu
from jax.sharding import PartitionSpec as P

RADIUS = 4
POOL = 16
DIRS = 32
MESH = pl.DeviceIdType.MESH
LANES = 128
CHUNKS = 2
EDGE = 2 * RADIUS
END_PART = 4 * EDGE


def extended(cells, sides, width):
    for axis, dim in sides:
        count = lax.axis_size(axis)
        ends = count - 1
        head = lax.slice_in_dim(cells, 0, width, axis=dim)
        tail = lax.slice_in_dim(cells, cells.shape[dim] - width, cells.shape[dim], axis=dim)
        cells = jnp.concatenate(
            [
                lax.ppermute(tail, axis, [(i, (i + 1) % count) for i in range(ends)]),
                cells,
                lax.ppermute(head, axis, [((i + 1) % count, i) for i in range(ends)]),
            ],
            axis=dim,
        )
    return cells


def kernel_taps():
    offsets = jnp.arange(-RADIUS, RADIUS + 1).astype(jnp.float32)
    base = jnp.exp(-offsets * offsets / 8.0)
    smooth = base / jnp.sqrt(jnp.sum(base * base))
    slope = -offsets * base
    deriv = slope / jnp.sqrt(jnp.sum(slope * slope))
    return (smooth, deriv)


def direction_table():
    index = jnp.arange(DIRS).astype(jnp.float32)
    height = 1.0 - (index + 0.5) / DIRS
    radial = jnp.sqrt(1.0 - height * height)
    phase = 2.399963229728653 * index
    d_x = radial * jnp.cos(phase)
    d_y = radial * jnp.sin(phase)
    return jnp.stack(
        [
            height * height,
            2.0 * height * d_x,
            2.0 * height * d_y,
            d_x * d_x,
            2.0 * d_x * d_y,
            d_y * d_y,
        ],
        axis=1,
    )


def filtered(padded, weights, axis, count):
    total = weights[0] * lax.slice_in_dim(padded, 0, count, axis=axis)
    for shift_index in range(1, 2 * RADIUS + 1):
        total = total + weights[shift_index] * lax.slice_in_dim(
            padded, shift_index, shift_index + count, axis=axis
        )
    return total


def pooled_full(field):
    planes, rows, cells = field.shape
    return field.reshape(planes // POOL, POOL, rows // POOL, POOL, cells // POOL, POOL).sum(
        axis=(1, 3, 5)
    )


def body(volume):
    smooth, deriv = kernel_taps()
    planes, rows, cells = volume.shape
    coeffs = direction_table()
    regrouped = lax.all_to_all(volume, "slab", split_axis=2, concat_axis=0, tiled=True)
    depth = regrouped.shape[0]
    owned = regrouped.shape[2]
    padded = extended(regrouped, (("slab", 2), ("tile", 1)), RADIUS)
    zpad = jnp.pad(padded, ((RADIUS, RADIUS), (0, 0), (0, 0)))
    z_smooth = filtered(zpad, smooth, 0, depth)
    z_deriv = filtered(zpad, deriv, 0, depth)
    both_smooth = filtered(z_smooth, smooth, 1, rows)
    smooth_deriv = filtered(z_smooth, deriv, 1, rows)
    deriv_smooth = filtered(z_deriv, smooth, 1, rows)
    grad_y = filtered(both_smooth, deriv, 2, owned)
    grad_x = filtered(smooth_deriv, smooth, 2, owned)
    grad_z = filtered(deriv_smooth, smooth, 2, owned)
    tensor = jnp.stack(
        [
            pooled_full(grad_z * grad_z),
            pooled_full(grad_z * grad_x),
            pooled_full(grad_z * grad_y),
            pooled_full(grad_x * grad_x),
            pooled_full(grad_x * grad_y),
            pooled_full(grad_y * grad_y),
        ]
    )
    hist = jnp.einsum("kc,cabv->abkv", coeffs, tensor, precision=lax.Precision.HIGHEST)
    return hist / float(POOL**3)


def host_taps():
    offsets = np.arange(-RADIUS, RADIUS + 1).astype(np.float64)
    base = np.exp(-offsets * offsets / 8.0)
    slope = -offsets * base
    return base / np.sqrt(np.sum(base * base)), slope / np.sqrt(np.sum(slope * slope))


def host_directions():
    index = np.arange(DIRS).astype(np.float32)
    height = np.float32(1.0) - (index + np.float32(0.5)) / np.float32(DIRS)
    radial = np.sqrt(np.float32(1.0) - height * height)
    phase = np.float32(2.399963229728653) * index
    d_x = radial * np.cos(phase)
    d_y = radial * np.sin(phase)
    two = np.float32(2.0)
    return np.stack(
        [height * height, two * height * d_x, two * height * d_y, d_x * d_x, two * d_x * d_y, d_y * d_y],
        axis=1,
    ).astype(np.float32)


def tap_at(weights, distance):
    index = distance + RADIUS
    inside = (index >= 0) & (index <= 2 * RADIUS)
    return np.where(inside, weights[np.clip(index, 0, 2 * RADIUS)], 0.0)


def halves(matrix):
    high = matrix.astype(np.float32).astype(ml_dtypes.bfloat16)
    low = (matrix - high.astype(np.float64)).astype(np.float32).astype(ml_dtypes.bfloat16)
    return np.stack([high, low])


def y_weights(owned):
    smooth, deriv = host_taps()
    edge = np.concatenate([np.arange(-RADIUS, 0), owned + np.arange(RADIUS)])
    out = np.arange(owned)
    inner = halves(np.concatenate([tap_at(w, out[:, None] - out[None, :]) for w in (smooth, deriv)], axis=1))
    outer = halves(np.concatenate([tap_at(w, edge[:, None] - out[None, :]) for w in (smooth, deriv)], axis=1))
    ends = np.zeros((LANES, 2 * owned), ml_dtypes.bfloat16)
    for part, which in enumerate((0, 0, 1)):
        for copy in range(3):
            start = part * END_PART + copy * EDGE
            ends[start : start + EDGE] = outer[which]
    return np.concatenate([inner[0], inner[1], ends], axis=0)


def zx_weights(planes, rows):
    smooth, deriv = host_taps()
    z_out, x_out = (g.ravel()[:, None] for g in np.meshgrid(np.arange(planes), np.arange(rows), indexing="ij"))
    step = np.arange(EDGE)
    around = np.where(step < RADIUS, rows + step, step - EDGE)
    tables = []
    for places in (np.arange(rows), around):
        z_in, x_in = (g.ravel()[None, :] for g in np.meshgrid(np.arange(planes), places, indexing="ij"))
        fields = []
        for z_taps, x_taps in ((deriv, smooth), (smooth, deriv), (smooth, smooth)):
            blocks = [
                tap_at(z_taps, group * planes + z_in - z_out) * tap_at(x_taps, x_in - x_out)
                for group in (-1, 0, 1)
            ]
            fields.append(np.concatenate(blocks, axis=1))
        tables.append(halves(np.concatenate(fields, axis=0)))
    inner, outer = tables
    return inner, np.concatenate([outer[0], outer[0], outer[1]], axis=1)


def histogram_weights(rows):
    voxels = rows // POOL
    inside = (np.arange(rows)[None, :] // POOL == np.arange(voxels)[:, None]).astype(np.float32)
    table = host_directions()[None, :, :, None] * inside[:, None, None, :]
    return (table.reshape(voxels * DIRS, -1) / np.float32(POOL**3)).astype(np.float32)


def split(values):
    high = values.astype(jnp.bfloat16)
    low = (values - high.astype(jnp.float32)).astype(jnp.bfloat16)
    return high, low


def dot(a, b):
    return jnp.dot(a, b, preferred_element_type=jnp.float32)


def exact_dot(a, b):
    return jnp.dot(a, b, preferred_element_type=jnp.float32, precision=lax.Precision.HIGHEST)


def kernel(
    slabs, tiles, x_hbm, wy_hbm, wzx_hbm, wring_hbm, whist_hbm, out_ref,
    x_ref, wy_ref, wzx_ref, wring_ref, whist_ref,
    recv, halo_l, halo_r, ends_out, ends_in, ends_l, ends_r, ends_main, ends_ring,
    y_high, y_low, ring_high, ring_low, partial,
    load_sem, send_sem, recv_sem, end_send, end_recv, side_sem, fl_send, fl_recv, fr_send, fr_recv,
):
    planes, rows, cells = x_ref.shape
    owned = cells // slabs
    inner_rows = planes * rows
    ring_rows = planes * EDGE
    part = planes // CHUNKS
    s = lax.axis_index("slab")
    t = lax.axis_index("tile")
    has_left = t > 0
    has_right = t < tiles - 1

    pairs = (
        (x_hbm, x_ref), (wy_hbm, wy_ref), (wzx_hbm, wzx_ref), (wring_hbm, wring_ref), (whist_hbm, whist_ref)
    )
    loads = [pltpu.make_async_copy(src, dst, load_sem.at[i]) for i, (src, dst) in enumerate(pairs)]
    for load in loads:
        load.start()

    barrier = pltpu.get_barrier_semaphore()
    for k in range(1, slabs):
        pl.semaphore_signal(barrier, inc=1, device_id=(lax.rem(s + k, slabs), t), device_id_type=MESH)

    @pl.when(has_left)
    def _():
        pl.semaphore_signal(barrier, inc=1, device_id=(s, t - 1), device_id_type=MESH)

    @pl.when(has_right)
    def _():
        pl.semaphore_signal(barrier, inc=1, device_id=(s, t + 1), device_id_type=MESH)

    loads[0].wait()
    lane = lax.broadcasted_iota(jnp.int32, (inner_rows, LANES), 1)
    edges = jnp.zeros((inner_rows, LANES), jnp.float32)

    def side(d, first):
        if d < 0 or d >= slabs:
            return jnp.zeros((inner_rows, LANES), jnp.float32)
        return x_ref[:, :, first : first + LANES].reshape(inner_rows, LANES)

    for d in range(slabs):
        before = side(d - 1, d * owned - LANES)
        after = side(d + 1, (d + 1) * owned)
        both = jnp.where(lane >= LANES // 2, before, after)
        turned = pltpu.roll(both, d * EDGE + RADIUS, 1)
        edges = jnp.where(lane // EDGE == d, turned, edges)
    edges = edges.T
    for d in range(slabs):
        ends_out[d] = edges[d * EDGE : (d + 1) * EDGE]

    beside = jnp.where(has_left, 1, 0) + jnp.where(has_right, 1, 0)
    pl.semaphore_wait(barrier, slabs - 1 + beside)

    def ends_copy(src, dst, k):
        return pltpu.make_async_remote_copy(
            src_ref=ends_out.at[dst], dst_ref=ends_in.at[src],
            send_sem=end_send.at[k], recv_sem=end_recv.at[src],
            device_id=(dst, t), device_id_type=MESH,
        )

    def block_copy(src, dst, k, c):
        first = pl.multiple_of(dst * owned, LANES)
        return pltpu.make_async_remote_copy(
            src_ref=x_ref.at[pl.ds(c * part, part), :, pl.ds(first, owned)],
            dst_ref=recv.at[src, pl.ds(c * part, part)],
            send_sem=send_sem.at[k * CHUNKS + c], recv_sem=recv_sem.at[src * CHUNKS + c],
            device_id=(dst, t), device_id_type=MESH,
        )

    def ends_left():
        return pltpu.make_async_remote_copy(
            src_ref=ends_in, dst_ref=ends_r, send_sem=side_sem.at[0], recv_sem=side_sem.at[1],
            device_id=(s, t - 1), device_id_type=MESH,
        )

    def ends_right():
        return pltpu.make_async_remote_copy(
            src_ref=ends_in, dst_ref=ends_l, send_sem=side_sem.at[2], recv_sem=side_sem.at[3],
            device_id=(s, t + 1), device_id_type=MESH,
        )

    def to_left(p, c):
        here = pl.ds(c * part, part)
        return pltpu.make_async_remote_copy(
            src_ref=recv.at[p, here, pl.ds(0, EDGE)], dst_ref=halo_r.at[p, here],
            send_sem=fl_send.at[p * CHUNKS + c], recv_sem=fl_recv.at[p * CHUNKS + c],
            device_id=(s, t - 1), device_id_type=MESH,
        )

    def to_right(p, c):
        here = pl.ds(c * part, part)
        return pltpu.make_async_remote_copy(
            src_ref=recv.at[p, here, pl.ds(rows - EDGE, EDGE)], dst_ref=halo_l.at[p, here],
            send_sem=fr_send.at[p * CHUNKS + c], recv_sem=fr_recv.at[p * CHUNKS + c],
            device_id=(s, t + 1), device_id_type=MESH,
        )

    def forward(p, c):
        @pl.when(has_left)
        def _():
            to_left(p, c).start()

        @pl.when(has_right)
        def _():
            to_right(p, c).start()

    sends = [ends_copy(s, lax.rem(s + k, slabs), k) for k in range(1, slabs)]
    sends += [block_copy(s, lax.rem(s + k, slabs), k, c) for c in range(CHUNKS) for k in range(1, slabs)]
    for send in sends:
        send.start()

    recv[s] = x_ref[:, :, pl.ds(pl.multiple_of(s * owned, LANES), owned)]
    ends_in[s] = ends_out[s]
    for c in range(CHUNKS):
        forward(s, c)

    @pl.when(jnp.logical_not(has_left))
    def _():
        halo_l[...] = jnp.zeros_like(halo_l)
        ends_l[...] = jnp.zeros_like(ends_l)

    @pl.when(jnp.logical_not(has_right))
    def _():
        halo_r[...] = jnp.zeros_like(halo_r)
        ends_r[...] = jnp.zeros_like(ends_r)

    for ref, count in ((y_high, inner_rows), (y_low, inner_rows), (ring_high, ring_rows), (ring_low, ring_rows)):
        blank = jnp.zeros((count, 2 * owned), jnp.bfloat16)
        ref[0:count, :] = blank
        ref[(slabs + 1) * count : (slabs + 2) * count, :] = blank

    for k in range(1, slabs):
        p = lax.rem(s + slabs - k, slabs)
        ends_copy(p, p, 0).wait_recv()

    @pl.when(has_left)
    def _():
        ends_left().start()

    @pl.when(has_right)
    def _():
        ends_right().start()

    def turned_parts(*kinds):
        parts = [split(kind) for kind in kinds]
        rest = [jnp.zeros((END_PART - len(kinds) * EDGE, LANES), jnp.float32)]
        high = [part[0].astype(jnp.float32) for part in parts] + rest
        low = [part[1].astype(jnp.float32) for part in parts] + rest
        last = [jnp.zeros((LANES - 3 * END_PART, LANES), jnp.float32)]
        return jnp.concatenate(high + low + high + last, axis=0).T

    for p in range(slabs):
        ends_main[p] = turned_parts(ends_in[p]).astype(jnp.bfloat16)

    loads[1].wait()

    def along_y(block, ends):
        high, low = split(block)
        inner, finer = wy_ref[0:owned], wy_ref[owned : 2 * owned]
        result = dot(high, inner) + dot(low, inner) + dot(high, finer)
        return split(result + dot(ends, wy_ref[2 * owned : 2 * owned + LANES]))

    def inner_along_y(p):
        high, low = along_y(recv[p].reshape(inner_rows, owned), ends_main[p])
        at = pl.ds(pl.multiple_of((p + 1) * inner_rows, 16), inner_rows)
        y_high[at, :] = high
        y_low[at, :] = low

    inner_along_y(s)
    for c in range(CHUNKS):
        for k in range(1, slabs):
            p = lax.rem(s + slabs - k, slabs)
            block_copy(p, p, 0, c).wait_recv()
            forward(p, c)
    for k in range(1, slabs):
        inner_along_y(lax.rem(s + slabs - k, slabs))

    smooth_y = slice(0, owned)
    deriv_y = slice(owned, 2 * owned)
    pair = slice(0, 2 * inner_rows)
    last = slice(2 * inner_rows, 3 * inner_rows)
    loads[2].wait()

    def inner_group(g):
        at = pl.ds(g * inner_rows, 3 * inner_rows)
        for out, field in ((pair, smooth_y), (last, deriv_y)):
            high = y_high[at, field]
            low = y_low[at, field]
            coarse = wzx_ref[0, out, :]
            partial[g, out, :] = dot(coarse, high) + dot(coarse, low) + dot(wzx_ref[1, out, :], high)

    for g in range(slabs):
        inner_group(g)

    @pl.when(has_left)
    def _():
        ends_right().wait_recv()

    @pl.when(has_right)
    def _():
        ends_left().wait_recv()

    ring_place = lax.broadcasted_iota(jnp.int32, (planes, EDGE, LANES), 2) // EDGE % (END_PART // EDGE)
    ring_step = lax.broadcasted_iota(jnp.int32, (planes, EDGE, LANES), 1)
    for p in range(slabs):
        turned = turned_parts(ends_l[p], ends_r[p]).reshape(planes, rows, LANES)
        right = jnp.where(ring_place == 1, turned[:, 0:EDGE], 0.0)
        left = jnp.where(ring_place == 0, turned[:, rows - EDGE : rows], 0.0)
        ring = jnp.where(ring_step < RADIUS, right, left).reshape(ring_rows, LANES)
        ends_ring[p * ring_rows : (p + 1) * ring_rows, :] = ring.astype(jnp.bfloat16)

    for p in range(slabs):
        for c in range(CHUNKS):
            @pl.when(has_left)
            def _():
                to_right(p, c).wait_recv()

            @pl.when(has_right)
            def _():
                to_left(p, c).wait_recv()

    step = lax.broadcasted_iota(jnp.int32, (slabs, planes, EDGE, owned), 2)
    ring = jnp.where(step < RADIUS, halo_r[...], halo_l[...]).reshape(slabs * ring_rows, owned)
    high, low = along_y(ring, ends_ring[...])
    ring_high[ring_rows : (slabs + 1) * ring_rows, :] = high
    ring_low[ring_rows : (slabs + 1) * ring_rows, :] = low
    loads[3].wait()

    def group(g, sums):
        at = pl.ds(g * ring_rows, 3 * ring_rows)

        def gradient(out, field):
            high = ring_high[at, field]
            low = ring_low[at, field]
            return partial[g, out, :] + dot(wring_ref[out, :], jnp.concatenate([high, low, high], axis=0))

        both = gradient(pair, smooth_y)
        grad_z = both[:inner_rows]
        grad_x = both[inner_rows:]
        grad_y = gradient(last, deriv_y)
        products = (
            grad_z * grad_z, grad_z * grad_x, grad_z * grad_y,
            grad_x * grad_x, grad_x * grad_y, grad_y * grad_y,
        )
        return tuple(
            held + product.reshape(planes, rows, owned).sum(axis=0)
            for held, product in zip(sums, products)
        )

    blank = jnp.zeros((rows, owned), jnp.float32)
    sums = (blank,) * 6
    for g in range(slabs):
        sums = group(g, sums)
    loads[4].wait()
    mixed = exact_dot(whist_ref[...], jnp.concatenate(sums, axis=0))
    cell = lax.broadcasted_iota(jnp.int32, (owned, owned // POOL), 0)
    voxel = lax.broadcasted_iota(jnp.int32, (owned, owned // POOL), 1)
    pooled = exact_dot(mixed, (cell // POOL == voxel).astype(jnp.float32))
    for b in range(rows // POOL):
        out_ref[0, b] = pooled[b * DIRS : (b + 1) * DIRS]

    for send in sends:
        send.wait_send()

    @pl.when(has_left)
    def _():
        ends_left().wait_send()
        for p in range(slabs):
            for c in range(CHUNKS):
                to_left(p, c).wait_send()

    @pl.when(has_right)
    def _():
        ends_right().wait_send()
        for p in range(slabs):
            for c in range(CHUNKS):
                to_right(p, c).wait_send()


def fused(slabs, tiles, volume):
    planes, rows, cells = volume.shape
    owned = cells // slabs
    inner_rows = planes * rows
    ring_rows = planes * EDGE
    wy = y_weights(owned)
    wzx, wring = zx_weights(planes, rows)
    whist = histogram_weights(rows)
    f32, bf16 = jnp.float32, jnp.bfloat16
    one = pltpu.SemaphoreType.DMA((slabs,))
    many = pltpu.SemaphoreType.DMA((slabs * CHUNKS,))
    halo = pltpu.VMEM((slabs, planes, EDGE, owned), f32)
    ends = pltpu.VMEM((slabs, EDGE, LANES), f32)
    held = pltpu.VMEM(((slabs + 2) * inner_rows, 2 * owned), bf16)
    ring = pltpu.VMEM(((slabs + 2) * ring_rows, 2 * owned), bf16)
    return pl.pallas_call(
        functools.partial(kernel, slabs, tiles),
        out_shape=jax.ShapeDtypeStruct((1, rows // POOL, DIRS, owned // POOL), f32),
        in_specs=[pl.BlockSpec(memory_space=pl.ANY)] * 5,
        out_specs=pl.BlockSpec(memory_space=pltpu.VMEM),
        scratch_shapes=[
            pltpu.VMEM(volume.shape, f32),
            pltpu.VMEM(wy.shape, bf16),
            pltpu.VMEM(wzx.shape, bf16),
            pltpu.VMEM(wring.shape, bf16),
            pltpu.VMEM(whist.shape, f32),
            pltpu.VMEM((slabs, planes, rows, owned), f32),
            halo, halo, ends, ends, ends, ends,
            pltpu.VMEM((slabs, inner_rows, LANES), bf16),
            pltpu.VMEM((slabs * ring_rows, LANES), bf16),
            held, held, ring, ring,
            pltpu.VMEM((slabs, 3 * inner_rows, owned), f32),
            pltpu.SemaphoreType.DMA((5,)),
            many, many, one, one, pltpu.SemaphoreType.DMA((4,)), many, many, many, many,
        ],
        compiler_params=pltpu.CompilerParams(collective_id=0, has_side_effects=True),
    )(volume, jnp.asarray(wy), jnp.asarray(wzx), jnp.asarray(wring), jnp.asarray(whist))


def fits(slabs, tiles, planes, rows, cells):
    owned = cells // slabs
    return (
        slabs * planes == POOL and planes >= RADIUS and planes * rows == LANES
        and rows % POOL == 0 and planes % CHUNKS == 0 and (planes * EDGE) % 16 == 0
        and owned % LANES == 0 and slabs * EDGE <= LANES
    )


def solution(mesh):
    slabs, tiles = mesh.shape["slab"], mesh.shape["tile"]

    def whole(volume):
        if slabs > 1 and tiles > 1 and fits(slabs, tiles, *volume.shape):
            return fused(slabs, tiles, volume)
        return body(volume)

    return jax.shard_map(
        whole,
        mesh=mesh,
        in_specs=(P("slab", "tile", None),),
        out_specs=P(None, "tile", None, "slab"),
        check_vma=False,
    )
```

```python
import functools

import jax
import jax.numpy as jnp
import ml_dtypes
import numpy as np
from jax import lax
from jax.experimental import pallas as pl
from jax.experimental.pallas import tpu as pltpu
from jax.sharding import PartitionSpec as P

RADIUS = 4
POOL = 16
DIRS = 32
MESH = pl.DeviceIdType.MESH
LANES = 128
CHUNKS = 2
EDGE = 2 * RADIUS
END_PART = 4 * EDGE


def extended(cells, sides, width):
    for axis, dim in sides:
        count = lax.axis_size(axis)
        ends = count - 1
        head = lax.slice_in_dim(cells, 0, width, axis=dim)
        tail = lax.slice_in_dim(cells, cells.shape[dim] - width, cells.shape[dim], axis=dim)
        cells = jnp.concatenate(
            [
                lax.ppermute(tail, axis, [(i, (i + 1) % count) for i in range(ends)]),
                cells,
                lax.ppermute(head, axis, [((i + 1) % count, i) for i in range(ends)]),
            ],
            axis=dim,
        )
    return cells


def kernel_taps():
    offsets = jnp.arange(-RADIUS, RADIUS + 1).astype(jnp.float32)
    base = jnp.exp(-offsets * offsets / 8.0)
    smooth = base / jnp.sqrt(jnp.sum(base * base))
    slope = -offsets * base
    deriv = slope / jnp.sqrt(jnp.sum(slope * slope))
    return (smooth, deriv)


def direction_table():
    index = jnp.arange(DIRS).astype(jnp.float32)
    height = 1.0 - (index + 0.5) / DIRS
    radial = jnp.sqrt(1.0 - height * height)
    phase = 2.399963229728653 * index
    d_x = radial * jnp.cos(phase)
    d_y = radial * jnp.sin(phase)
    return jnp.stack(
        [
            height * height,
            2.0 * height * d_x,
            2.0 * height * d_y,
            d_x * d_x,
            2.0 * d_x * d_y,
            d_y * d_y,
        ],
        axis=1,
    )


def filtered(padded, weights, axis, count):
    total = weights[0] * lax.slice_in_dim(padded, 0, count, axis=axis)
    for shift_index in range(1, 2 * RADIUS + 1):
        total = total + weights[shift_index] * lax.slice_in_dim(
            padded, shift_index, shift_index + count, axis=axis
        )
    return total


def pooled_full(field):
    planes, rows, cells = field.shape
    return field.reshape(planes // POOL, POOL, rows // POOL, POOL, cells // POOL, POOL).sum(
        axis=(1, 3, 5)
    )


def body(volume):
    smooth, deriv = kernel_taps()
    planes, rows, cells = volume.shape
    coeffs = direction_table()
    regrouped = lax.all_to_all(volume, "slab", split_axis=2, concat_axis=0, tiled=True)
    depth = regrouped.shape[0]
    owned = regrouped.shape[2]
    padded = extended(regrouped, (("slab", 2), ("tile", 1)), RADIUS)
    zpad = jnp.pad(padded, ((RADIUS, RADIUS), (0, 0), (0, 0)))
    z_smooth = filtered(zpad, smooth, 0, depth)
    z_deriv = filtered(zpad, deriv, 0, depth)
    both_smooth = filtered(z_smooth, smooth, 1, rows)
    smooth_deriv = filtered(z_smooth, deriv, 1, rows)
    deriv_smooth = filtered(z_deriv, smooth, 1, rows)
    grad_y = filtered(both_smooth, deriv, 2, owned)
    grad_x = filtered(smooth_deriv, smooth, 2, owned)
    grad_z = filtered(deriv_smooth, smooth, 2, owned)
    tensor = jnp.stack(
        [
            pooled_full(grad_z * grad_z),
            pooled_full(grad_z * grad_x),
            pooled_full(grad_z * grad_y),
            pooled_full(grad_x * grad_x),
            pooled_full(grad_x * grad_y),
            pooled_full(grad_y * grad_y),
        ]
    )
    hist = jnp.einsum("kc,cabv->abkv", coeffs, tensor, precision=lax.Precision.HIGHEST)
    return hist / float(POOL**3)


def host_taps():
    offsets = np.arange(-RADIUS, RADIUS + 1).astype(np.float64)
    base = np.exp(-offsets * offsets / 8.0)
    slope = -offsets * base
    return base / np.sqrt(np.sum(base * base)), slope / np.sqrt(np.sum(slope * slope))


def host_directions():
    index = np.arange(DIRS).astype(np.float32)
    height = np.float32(1.0) - (index + np.float32(0.5)) / np.float32(DIRS)
    radial = np.sqrt(np.float32(1.0) - height * height)
    phase = np.float32(2.399963229728653) * index
    d_x = radial * np.cos(phase)
    d_y = radial * np.sin(phase)
    two = np.float32(2.0)
    return np.stack(
        [height * height, two * height * d_x, two * height * d_y, d_x * d_x, two * d_x * d_y, d_y * d_y],
        axis=1,
    ).astype(np.float32)


def tap_at(weights, distance):
    index = distance + RADIUS
    inside = (index >= 0) & (index <= 2 * RADIUS)
    return np.where(inside, weights[np.clip(index, 0, 2 * RADIUS)], 0.0)


def halves(matrix):
    high = matrix.astype(np.float32).astype(ml_dtypes.bfloat16)
    low = (matrix - high.astype(np.float64)).astype(np.float32).astype(ml_dtypes.bfloat16)
    return np.stack([high, low])


def y_weights(owned):
    smooth, deriv = host_taps()
    edge = np.concatenate([np.arange(-RADIUS, 0), owned + np.arange(RADIUS)])
    out = np.arange(owned)
    inner = halves(np.concatenate([tap_at(w, out[:, None] - out[None, :]) for w in (smooth, deriv)], axis=1))
    outer = halves(np.concatenate([tap_at(w, edge[:, None] - out[None, :]) for w in (smooth, deriv)], axis=1))
    ends = np.zeros((LANES, 2 * owned), ml_dtypes.bfloat16)
    for part, which in enumerate((0, 0, 1)):
        for copy in range(3):
            start = part * END_PART + copy * EDGE
            ends[start : start + EDGE] = outer[which]
    return np.concatenate([inner[0], inner[1], ends], axis=0)


def zx_weights(planes, rows):
    smooth, deriv = host_taps()
    z_out, x_out = (g.ravel()[:, None] for g in np.meshgrid(np.arange(planes), np.arange(rows), indexing="ij"))
    step = np.arange(EDGE)
    around = np.where(step < RADIUS, rows + step, step - EDGE)
    tables = []
    for places in (np.arange(rows), around):
        z_in, x_in = (g.ravel()[None, :] for g in np.meshgrid(np.arange(planes), places, indexing="ij"))
        fields = []
        for z_taps, x_taps in ((deriv, smooth), (smooth, deriv), (smooth, smooth)):
            blocks = [
                tap_at(z_taps, group * planes + z_in - z_out) * tap_at(x_taps, x_in - x_out)
                for group in (-1, 0, 1)
            ]
            fields.append(np.concatenate(blocks, axis=1))
        tables.append(halves(np.concatenate(fields, axis=0)))
    inner, outer = tables
    return inner, np.concatenate([outer[0], outer[0], outer[1]], axis=1)


def histogram_weights(rows):
    voxels = rows // POOL
    inside = (np.arange(rows)[None, :] // POOL == np.arange(voxels)[:, None]).astype(np.float32)
    table = host_directions()[None, :, :, None] * inside[:, None, None, :]
    return (table.reshape(voxels * DIRS, -1) / np.float32(POOL**3)).astype(np.float32)


def split(values):
    high = values.astype(jnp.bfloat16)
    low = (values - high.astype(jnp.float32)).astype(jnp.bfloat16)
    return high, low


def dot(a, b):
    return jnp.dot(a, b, preferred_element_type=jnp.float32)


def split_dot(a, b):
    a_high, a_low = split(a)
    b_high, b_low = split(b)
    return dot(jnp.concatenate([a_high, a_high, a_low], axis=1), jnp.concatenate([b_high, b_low, b_high], axis=0))


def kernel(
    slabs, tiles, x_hbm, wy_hbm, wzx_hbm, wring_hbm, whist_hbm, out_ref,
    x_ref, wy_ref, wzx_ref, wring_ref, whist_ref,
    recv, halo_l, halo_r, ends_out, ends_in, ends_l, ends_r, ends_main, ends_ring,
    y_high, y_low, ring_high, ring_low, partial,
    load_sem, send_sem, recv_sem, end_send, end_recv, side_sem, fl_send, fl_recv, fr_send, fr_recv,
):
    planes, rows, cells = x_ref.shape
    owned = cells // slabs
    inner_rows = planes * rows
    ring_rows = planes * EDGE
    part = planes // CHUNKS
    s = lax.axis_index("slab")
    t = lax.axis_index("tile")
    has_left = t > 0
    has_right = t < tiles - 1

    pairs = (
        (x_hbm, x_ref), (wy_hbm, wy_ref), (wzx_hbm, wzx_ref), (wring_hbm, wring_ref), (whist_hbm, whist_ref)
    )
    loads = [pltpu.make_async_copy(src, dst, load_sem.at[i]) for i, (src, dst) in enumerate(pairs)]
    for load in loads:
        load.start()

    barrier = pltpu.get_barrier_semaphore()
    for k in range(1, slabs):
        pl.semaphore_signal(barrier, inc=1, device_id=(lax.rem(s + k, slabs), t), device_id_type=MESH)

    @pl.when(has_left)
    def _():
        pl.semaphore_signal(barrier, inc=1, device_id=(s, t - 1), device_id_type=MESH)

    @pl.when(has_right)
    def _():
        pl.semaphore_signal(barrier, inc=1, device_id=(s, t + 1), device_id_type=MESH)

    loads[0].wait()
    lane = lax.broadcasted_iota(jnp.int32, (inner_rows, LANES), 1)
    edges = jnp.zeros((inner_rows, LANES), jnp.float32)

    def side(d, first):
        if d < 0 or d >= slabs:
            return jnp.zeros((inner_rows, LANES), jnp.float32)
        return x_ref[:, :, first : first + LANES].reshape(inner_rows, LANES)

    for d in range(slabs):
        before = side(d - 1, d * owned - LANES)
        after = side(d + 1, (d + 1) * owned)
        both = jnp.where(lane >= LANES // 2, before, after)
        turned = pltpu.roll(both, d * EDGE + RADIUS, 1)
        edges = jnp.where(lane // EDGE == d, turned, edges)
    edges = edges.T
    for d in range(slabs):
        ends_out[d] = edges[d * EDGE : (d + 1) * EDGE]

    beside = jnp.where(has_left, 1, 0) + jnp.where(has_right, 1, 0)
    pl.semaphore_wait(barrier, slabs - 1 + beside)

    def ends_copy(src, dst, k):
        return pltpu.make_async_remote_copy(
            src_ref=ends_out.at[dst], dst_ref=ends_in.at[src],
            send_sem=end_send.at[k], recv_sem=end_recv.at[src],
            device_id=(dst, t), device_id_type=MESH,
        )

    def block_copy(src, dst, k, c):
        first = pl.multiple_of(dst * owned, LANES)
        return pltpu.make_async_remote_copy(
            src_ref=x_ref.at[pl.ds(c * part, part), :, pl.ds(first, owned)],
            dst_ref=recv.at[src, pl.ds(c * part, part)],
            send_sem=send_sem.at[k * CHUNKS + c], recv_sem=recv_sem.at[src * CHUNKS + c],
            device_id=(dst, t), device_id_type=MESH,
        )

    def ends_left():
        return pltpu.make_async_remote_copy(
            src_ref=ends_in, dst_ref=ends_r, send_sem=side_sem.at[0], recv_sem=side_sem.at[1],
            device_id=(s, t - 1), device_id_type=MESH,
        )

    def ends_right():
        return pltpu.make_async_remote_copy(
            src_ref=ends_in, dst_ref=ends_l, send_sem=side_sem.at[2], recv_sem=side_sem.at[3],
            device_id=(s, t + 1), device_id_type=MESH,
        )

    def to_left(p, c):
        here = pl.ds(c * part, part)
        return pltpu.make_async_remote_copy(
            src_ref=recv.at[p, here, pl.ds(0, EDGE)], dst_ref=halo_r.at[p, here],
            send_sem=fl_send.at[p * CHUNKS + c], recv_sem=fl_recv.at[p * CHUNKS + c],
            device_id=(s, t - 1), device_id_type=MESH,
        )

    def to_right(p, c):
        here = pl.ds(c * part, part)
        return pltpu.make_async_remote_copy(
            src_ref=recv.at[p, here, pl.ds(rows - EDGE, EDGE)], dst_ref=halo_l.at[p, here],
            send_sem=fr_send.at[p * CHUNKS + c], recv_sem=fr_recv.at[p * CHUNKS + c],
            device_id=(s, t + 1), device_id_type=MESH,
        )

    def forward(p, c):
        @pl.when(has_left)
        def _():
            to_left(p, c).start()

        @pl.when(has_right)
        def _():
            to_right(p, c).start()

    sends = [ends_copy(s, lax.rem(s + k, slabs), k) for k in range(1, slabs)]
    sends += [block_copy(s, lax.rem(s + k, slabs), k, c) for c in range(CHUNKS) for k in range(1, slabs)]
    for send in sends:
        send.start()

    recv[s] = x_ref[:, :, pl.ds(pl.multiple_of(s * owned, LANES), owned)]
    ends_in[s] = ends_out[s]
    for c in range(CHUNKS):
        forward(s, c)

    @pl.when(jnp.logical_not(has_left))
    def _():
        halo_l[...] = jnp.zeros_like(halo_l)
        ends_l[...] = jnp.zeros_like(ends_l)

    @pl.when(jnp.logical_not(has_right))
    def _():
        halo_r[...] = jnp.zeros_like(halo_r)
        ends_r[...] = jnp.zeros_like(ends_r)

    for ref, count in ((y_high, inner_rows), (y_low, inner_rows), (ring_high, ring_rows), (ring_low, ring_rows)):
        blank = jnp.zeros((count, 2 * owned), jnp.bfloat16)
        ref[0:count, :] = blank
        ref[(slabs + 1) * count : (slabs + 2) * count, :] = blank

    for k in range(1, slabs):
        p = lax.rem(s + slabs - k, slabs)
        ends_copy(p, p, 0).wait_recv()

    @pl.when(has_left)
    def _():
        ends_left().start()

    @pl.when(has_right)
    def _():
        ends_right().start()

    def turned_parts(*kinds):
        parts = [split(kind) for kind in kinds]
        rest = [jnp.zeros((END_PART - len(kinds) * EDGE, LANES), jnp.float32)]
        high = [part[0].astype(jnp.float32) for part in parts] + rest
        low = [part[1].astype(jnp.float32) for part in parts] + rest
        last = [jnp.zeros((LANES - 3 * END_PART, LANES), jnp.float32)]
        return jnp.concatenate(high + low + high + last, axis=0).T

    for p in range(slabs):
        ends_main[p] = turned_parts(ends_in[p]).astype(jnp.bfloat16)

    loads[1].wait()

    def along_y(block, ends):
        high, low = split(block)
        inner, finer = wy_ref[0:owned], wy_ref[owned : 2 * owned]
        result = dot(high, inner) + dot(low, inner) + dot(high, finer)
        return split(result + dot(ends, wy_ref[2 * owned : 2 * owned + LANES]))

    def inner_along_y(p):
        high, low = along_y(recv[p].reshape(inner_rows, owned), ends_main[p])
        at = pl.ds(pl.multiple_of((p + 1) * inner_rows, 16), inner_rows)
        y_high[at, :] = high
        y_low[at, :] = low

    inner_along_y(s)
    for c in range(CHUNKS):
        for k in range(1, slabs):
            p = lax.rem(s + slabs - k, slabs)
            block_copy(p, p, 0, c).wait_recv()
            forward(p, c)
    for k in range(1, slabs):
        inner_along_y(lax.rem(s + slabs - k, slabs))

    smooth_y = slice(0, owned)
    deriv_y = slice(owned, 2 * owned)
    pair = slice(0, 2 * inner_rows)
    last = slice(2 * inner_rows, 3 * inner_rows)
    loads[2].wait()

    def inner_group(g):
        at = pl.ds(g * inner_rows, 3 * inner_rows)
        for out, field in ((pair, smooth_y), (last, deriv_y)):
            high = y_high[at, field]
            low = y_low[at, field]
            coarse = wzx_ref[0, out, :]
            partial[g, out, :] = dot(coarse, high) + dot(coarse, low) + dot(wzx_ref[1, out, :], high)

    for g in range(slabs):
        inner_group(g)

    @pl.when(has_left)
    def _():
        ends_right().wait_recv()

    @pl.when(has_right)
    def _():
        ends_left().wait_recv()

    ring_place = lax.broadcasted_iota(jnp.int32, (planes, EDGE, LANES), 2) // EDGE % (END_PART // EDGE)
    ring_step = lax.broadcasted_iota(jnp.int32, (planes, EDGE, LANES), 1)
    for p in range(slabs):
        turned = turned_parts(ends_l[p], ends_r[p]).reshape(planes, rows, LANES)
        right = jnp.where(ring_place == 1, turned[:, 0:EDGE], 0.0)
        left = jnp.where(ring_place == 0, turned[:, rows - EDGE : rows], 0.0)
        ring = jnp.where(ring_step < RADIUS, right, left).reshape(ring_rows, LANES)
        ends_ring[p * ring_rows : (p + 1) * ring_rows, :] = ring.astype(jnp.bfloat16)

    for p in range(slabs):
        for c in range(CHUNKS):
            @pl.when(has_left)
            def _():
                to_right(p, c).wait_recv()

            @pl.when(has_right)
            def _():
                to_left(p, c).wait_recv()

    step = lax.broadcasted_iota(jnp.int32, (slabs, planes, EDGE, owned), 2)
    ring = jnp.where(step < RADIUS, halo_r[...], halo_l[...]).reshape(slabs * ring_rows, owned)
    high, low = along_y(ring, ends_ring[...])
    ring_high[ring_rows : (slabs + 1) * ring_rows, :] = high
    ring_low[ring_rows : (slabs + 1) * ring_rows, :] = low
    loads[3].wait()

    def group(g, sums):
        at = pl.ds(g * ring_rows, 3 * ring_rows)

        def gradient(out, field):
            high = ring_high[at, field]
            low = ring_low[at, field]
            return partial[g, out, :] + dot(wring_ref[out, :], jnp.concatenate([high, low, high], axis=0))

        both = gradient(pair, smooth_y)
        grad_z = both[:inner_rows]
        grad_x = both[inner_rows:]
        grad_y = gradient(last, deriv_y)
        products = (
            grad_z * grad_z, grad_z * grad_x, grad_z * grad_y,
            grad_x * grad_x, grad_x * grad_y, grad_y * grad_y,
        )
        return tuple(
            held + product.reshape(planes, rows, owned).sum(axis=0)
            for held, product in zip(sums, products)
        )

    blank = jnp.zeros((rows, owned), jnp.float32)
    sums = (blank,) * 6
    for g in range(slabs):
        sums = group(g, sums)
    loads[4].wait()
    mixed = split_dot(whist_ref[...], jnp.concatenate(sums, axis=0))
    cell = lax.broadcasted_iota(jnp.int32, (owned, owned // POOL), 0)
    voxel = lax.broadcasted_iota(jnp.int32, (owned, owned // POOL), 1)
    pooled = split_dot(mixed, (cell // POOL == voxel).astype(jnp.float32))
    for b in range(rows // POOL):
        out_ref[0, b] = pooled[b * DIRS : (b + 1) * DIRS]

    for send in sends:
        send.wait_send()

    @pl.when(has_left)
    def _():
        ends_left().wait_send()
        for p in range(slabs):
            for c in range(CHUNKS):
                to_left(p, c).wait_send()

    @pl.when(has_right)
    def _():
        ends_right().wait_send()
        for p in range(slabs):
            for c in range(CHUNKS):
                to_right(p, c).wait_send()


def fused(slabs, tiles, volume):
    planes, rows, cells = volume.shape
    owned = cells // slabs
    inner_rows = planes * rows
    ring_rows = planes * EDGE
    wy = y_weights(owned)
    wzx, wring = zx_weights(planes, rows)
    whist = histogram_weights(rows)
    f32, bf16 = jnp.float32, jnp.bfloat16
    one = pltpu.SemaphoreType.DMA((slabs,))
    many = pltpu.SemaphoreType.DMA((slabs * CHUNKS,))
    halo = pltpu.VMEM((slabs, planes, EDGE, owned), f32)
    ends = pltpu.VMEM((slabs, EDGE, LANES), f32)
    held = pltpu.VMEM(((slabs + 2) * inner_rows, 2 * owned), bf16)
    ring = pltpu.VMEM(((slabs + 2) * ring_rows, 2 * owned), bf16)
    return pl.pallas_call(
        functools.partial(kernel, slabs, tiles),
        out_shape=jax.ShapeDtypeStruct((1, rows // POOL, DIRS, owned // POOL), f32),
        in_specs=[pl.BlockSpec(memory_space=pl.ANY)] * 5,
        out_specs=pl.BlockSpec(memory_space=pltpu.VMEM),
        scratch_shapes=[
            pltpu.VMEM(volume.shape, f32),
            pltpu.VMEM(wy.shape, bf16),
            pltpu.VMEM(wzx.shape, bf16),
            pltpu.VMEM(wring.shape, bf16),
            pltpu.VMEM(whist.shape, f32),
            pltpu.VMEM((slabs, planes, rows, owned), f32),
            halo, halo, ends, ends, ends, ends,
            pltpu.VMEM((slabs, inner_rows, LANES), bf16),
            pltpu.VMEM((slabs * ring_rows, LANES), bf16),
            held, held, ring, ring,
            pltpu.VMEM((slabs, 3 * inner_rows, owned), f32),
            pltpu.SemaphoreType.DMA((5,)),
            many, many, one, one, pltpu.SemaphoreType.DMA((4,)), many, many, many, many,
        ],
        compiler_params=pltpu.CompilerParams(collective_id=0, has_side_effects=True),
    )(volume, jnp.asarray(wy), jnp.asarray(wzx), jnp.asarray(wring), jnp.asarray(whist))


def fits(slabs, tiles, planes, rows, cells):
    owned = cells // slabs
    return (
        slabs * planes == POOL and planes >= RADIUS and planes * rows == LANES
        and rows % POOL == 0 and planes % CHUNKS == 0 and (planes * EDGE) % 16 == 0
        and owned % LANES == 0 and slabs * EDGE <= LANES
    )


def solution(mesh):
    slabs, tiles = mesh.shape["slab"], mesh.shape["tile"]

    def whole(volume):
        if slabs > 1 and tiles > 1 and fits(slabs, tiles, *volume.shape):
            return fused(slabs, tiles, volume)
        return body(volume)

    return jax.shard_map(
        whole,
        mesh=mesh,
        in_specs=(P("slab", "tile", None),),
        out_specs=P(None, "tile", None, "slab"),
        check_vma=False,
    )
```
